32 devices in a mesh: ctx: 16 (over z, y, x), head: 2 (over core).
Axes of the slice: x: 2, y: 2, z: 4, core: 2. Of those that a mesh axis runs over, the one named last changes fastest.
Arguments:
- queries: bfloat16 [4096, 2048], P('ctx', 'head'), may hold values from -8 to 8
- keys: bfloat16 [4096, 2048], P('ctx', 'head'), may hold values from -8 to 8
- values: bfloat16 [4096, 2048], P('ctx', 'head'), may hold values from -6 to 6
- out_weight: bfloat16 [2048, 2048], replicated, may hold values from -0.125 to 0.125
- cotangent: bfloat16 [4096, 2048], P('ctx', 'head'), may hold values from -6 to 6
- bounds: int32 [4], replicated, may hold values from 0 to 3968, as said below
Outputs:
- output: bfloat16 [4096, 2048], P('ctx', 'head')
- grad_queries: bfloat16 [4096, 2048], P('ctx', 'head')
- grad_keys: bfloat16 [4096, 2048], P('ctx', 'head')
- grad_values: bfloat16 [4096, 2048], P('ctx', 'head')
The draws below stay inside these ranges and needn't reach their ends.
Inputs may be any that keep to these rules, and one draw needn't show every extreme that they name: bounds starts at 0 and rises strictly; the last document begins 256 // 2 positions before the end of the sequence.
All inputs are finite; a program needn't handle non-finite values.
Results may differ from the reference program's by a relative error of at most 0.0079.
Values may be sent and summed in bfloat16 or wider, within the bound.
No kernel may reach another device: no remote copies, remote signals or barrier semaphores. Data moves between devices by JAX's collectives and lax.ppermute only.
A program may use at most 128 MiB of HBM per device.

```python
import math
import jax
import jax.numpy as jnp
from jax import lax

HEADS = 16
DH = 128
MODEL_WIDTH = 2048
BLOCK_TOKENS = 256
DILATION_STEP = 4
FAR_KEY_ROWS = 64
LEVELS = 4
KEYS = 512
TOKENS = 4096
N_CTX = 16


def shared_fields(key):
    base_q = jnp.clip(1.5 * jax.random.normal(jax.random.fold_in(key, 11), (TOKENS, MODEL_WIDTH), jnp.float32), -7.5, 7.5)
    base_k = jnp.clip(1.5 * jax.random.normal(jax.random.fold_in(key, 12), (TOKENS, MODEL_WIDTH), jnp.float32), -7.5, 7.5)
    return (base_q, base_k)


def draw_queries(key, part):
    base_q, base_k = shared_fields(key)
    result = base_q
    return result.astype(jnp.bfloat16)


def draw_keys(key, part):
    base_q, base_k = shared_fields(key)
    result = base_k
    return result.astype(jnp.bfloat16)


def draw_bounds(key, part):
    key = jax.random.fold_in(key, 5)
    first = jax.random.randint(jax.random.fold_in(key, 1), (), 5 * TOKENS // 8, 7 * TOKENS // 8)
    second = first + jax.random.randint(jax.random.fold_in(key, 2), (), 1, (TOKENS - first) // 2 + 1)
    third = jnp.full((), TOKENS - BLOCK_TOKENS // 2, jnp.int32)
    return jnp.stack([jnp.zeros((), jnp.int32), first, second, third]).astype(jnp.int32)


def levels(key, extent, split, smallest, largest):
    def one(axis_at, shards_of):
        draws = jax.random.uniform(jax.random.fold_in(jax.random.fold_in(key, 6), axis_at), (shards_of,), jnp.float32, smallest / len(split), largest / len(split))
        return jnp.repeat(jnp.exp(draws), extent[axis_at] // shards_of).reshape((-1,) + (1,) * (len(extent) - axis_at - 1))

    loudness = one(*split[0])
    for cut in split[1:]:
        loudness = loudness * one(*cut)
    return loudness


def scatter_about(own_key, extent, deviation, most, pieces=(), kind=jnp.bfloat16):
    level = levels(own_key, extent, pieces, -0.22, 0.18) if pieces else 1.0
    entries = jax.random.normal(own_key, extent, jnp.float32) * deviation * level
    return jnp.minimum(jnp.maximum(entries, -most), most).astype(kind)


def setup_inputs(seed: int = 0) -> dict:
    key_of = jax.random.split(jax.random.key(seed), 7)
    queries = draw_queries(jax.random.fold_in(key_of[6], 71), 0)
    keys = draw_keys(jax.random.fold_in(key_of[6], 71), 0)
    values = scatter_about(key_of[2], (TOKENS, MODEL_WIDTH), 1.0, 6.0, ((0, 16), (1, 2)))
    out_weight = scatter_about(key_of[3], (MODEL_WIDTH, MODEL_WIDTH), MODEL_WIDTH ** -0.5, 0.125)
    cotangent = scatter_about(key_of[4], (TOKENS, MODEL_WIDTH), 1.0, 6.0, ((0, 16), (1, 2)))
    bounds = draw_bounds(jax.random.fold_in(key_of[6], 71), 0)
    return dict(queries=queries, keys=keys, values=values, out_weight=out_weight, cotangent=cotangent, bounds=bounds)


def doc_index(positions, bounds):
    return lax.optimization_barrier(jnp.sum((bounds[None, :] <= positions[:, None]).astype(jnp.int32), axis=1))

def reference(queries, keys, values, out_weight, cotangent, bounds):
    scale = 1.0 / math.sqrt(DH)
    grad_attn_all = jnp.dot(cotangent, out_weight.T, preferred_element_type=jnp.float32).astype(jnp.bfloat16)

    def one_shard(device_piece):
        start = device_piece * BLOCK_TOKENS
        q_rows = lax.dynamic_slice_in_dim(queries, start, BLOCK_TOKENS, 0)
        k_rows = lax.dynamic_slice_in_dim(keys, start, BLOCK_TOKENS, 0)
        v_rows = lax.dynamic_slice_in_dim(values, start, BLOCK_TOKENS, 0)
        ga_rows = lax.dynamic_slice_in_dim(grad_attn_all, start, BLOCK_TOKENS, 0)
        own_pos = start + jnp.arange(BLOCK_TOKENS, dtype=jnp.int32)
        key_parts = [k_rows]
        value_parts = [v_rows]
        key_positions = [own_pos]
        for level_number in range(LEVELS):
            sender_index = device_piece - 2 ** level_number
            block_start = jnp.maximum(sender_index, 0) * BLOCK_TOKENS
            distant_keys = lax.dynamic_slice_in_dim(keys, block_start, BLOCK_TOKENS, 0).reshape(FAR_KEY_ROWS, DILATION_STEP, MODEL_WIDTH)[:, 0]
            distant_values = lax.dynamic_slice_in_dim(values, block_start, BLOCK_TOKENS, 0).reshape(FAR_KEY_ROWS, DILATION_STEP, MODEL_WIDTH)[:, 0]
            key_parts.append(distant_keys)
            value_parts.append(distant_values)
            key_positions.append(sender_index * BLOCK_TOKENS + jnp.arange(FAR_KEY_ROWS, dtype=jnp.int32) * DILATION_STEP)
        all_k = jnp.concatenate(key_parts, 0)
        all_v = jnp.concatenate(value_parts, 0)
        all_pos = jnp.concatenate(key_positions, 0)
        allowed = doc_index(own_pos, bounds)[:, None] == doc_index(all_pos, bounds)[None, :]
        allowed = allowed & (all_pos[None, :] <= own_pos[:, None]) & (all_pos[None, :] >= 0)
        q3 = q_rows.reshape(BLOCK_TOKENS, HEADS, DH).astype(jnp.float32)
        k3 = all_k.reshape(KEYS, HEADS, DH).astype(jnp.float32)
        v3 = all_v.reshape(KEYS, HEADS, DH).astype(jnp.float32)
        ga3 = ga_rows.reshape(BLOCK_TOKENS, HEADS, DH).astype(jnp.float32)
        scores = jnp.einsum('qhd,khd->hqk', q3, k3) * scale
        scores = jnp.where(allowed[None], scores, -jnp.inf)
        top = lax.optimization_barrier(jnp.max(scores, axis=2, keepdims=True))
        lse = top + jnp.log(lax.optimization_barrier(jnp.sum(jnp.exp(scores - top), axis=2, keepdims=True)))
        prob = jnp.exp(scores - lse)
        weights = prob.astype(jnp.bfloat16)
        attn = jnp.einsum('hqk,khd->qhd', weights.astype(jnp.float32), v3).astype(jnp.bfloat16).reshape(BLOCK_TOKENS, MODEL_WIDTH)
        grad_prob = jnp.einsum('qhd,khd->hqk', ga3, v3)
        delta = lax.optimization_barrier(jnp.sum(prob * grad_prob, axis=2, keepdims=True))
        grad_scores = (prob * (grad_prob - delta) * scale).astype(jnp.bfloat16).astype(jnp.float32)
        grad_q = jnp.einsum('hqk,khd->qhd', grad_scores, k3).astype(jnp.bfloat16).reshape(BLOCK_TOKENS, MODEL_WIDTH)
        grad_k = jnp.einsum('hqk,qhd->khd', grad_scores, q3).reshape(KEYS, MODEL_WIDTH)
        grad_v = jnp.einsum('hqk,qhd->khd', weights.astype(jnp.float32), ga3).reshape(KEYS, MODEL_WIDTH)
        return (attn, grad_q, grad_k[:BLOCK_TOKENS], grad_v[:BLOCK_TOKENS], grad_k[BLOCK_TOKENS:].reshape(LEVELS, FAR_KEY_ROWS, MODEL_WIDTH), grad_v[BLOCK_TOKENS:].reshape(LEVELS, FAR_KEY_ROWS, MODEL_WIDTH))
    attn, grad_q, near_k, near_v, distant_keys, distant_values = lax.map(one_shard, jnp.arange(N_CTX, dtype=jnp.int32))
    output = jnp.dot(attn.reshape(TOKENS, MODEL_WIDTH), out_weight, preferred_element_type=jnp.float32).astype(jnp.bfloat16)

    def collect(nearby_block, far):
        extra = jnp.zeros((N_CTX, FAR_KEY_ROWS, MODEL_WIDTH), jnp.float32)
        for level_number in range(LEVELS):
            step = 2 ** level_number
            moved = jnp.concatenate([far[step:, level_number], jnp.zeros((step, FAR_KEY_ROWS, MODEL_WIDTH), jnp.float32)], 0)
            extra = extra + moved
        block_list = nearby_block.reshape(N_CTX, FAR_KEY_ROWS, DILATION_STEP, MODEL_WIDTH)
        block_list = jnp.concatenate([block_list[:, :, :1] + extra[:, :, None], block_list[:, :, 1:]], 2)
        return block_list.reshape(TOKENS, MODEL_WIDTH).astype(jnp.bfloat16)
    return (output, grad_q.reshape(TOKENS, MODEL_WIDTH), collect(near_k, distant_keys), collect(near_v, distant_values))
```

```python
import functools
import math

import jax
import jax.numpy as jnp
from jax import lax
from jax.experimental import pallas as pl
from jax.experimental.pallas import tpu as pltpu
from jax.sharding import PartitionSpec as P

DH = 128
STEP = 4
VMEM_LIMIT = 40 * 1024 * 1024
BF16 = jnp.bfloat16
F32 = jnp.float32


def shift(block, axis, distance):
    devices = range(lax.axis_size(axis))
    route = [(i, i + distance) for i in devices if i + distance in devices]
    return lax.ppermute(block, axis, route)


def swap(block):
    return lax.ppermute(block, "head", [(0, 1), (1, 0)])


def nt(a, b):
    return lax.dot_general(a, b, (((1,), (1,)), ((), ())), preferred_element_type=F32)


def tn(a, b):
    return lax.dot_general(a, b, (((0,), (0,)), ((), ())), preferred_element_type=F32)


def nn(a, b):
    return jnp.dot(a, b, preferred_element_type=F32)


def params():
    return pltpu.CompilerParams(vmem_limit_bytes=VMEM_LIMIT)


def pick_kernel(k_ref, v_ref, out_ref):
    tokens = k_ref.shape[0]
    rows = tokens // STEP
    at = lax.broadcasted_iota(jnp.int32, (rows, tokens), 0) * STEP
    choose = (at == lax.broadcasted_iota(jnp.int32, (rows, tokens), 1)).astype(BF16)
    out_ref[:rows] = nn(choose, k_ref[...]).astype(BF16)
    out_ref[rows:] = nn(choose, v_ref[...]).astype(BF16)


def pick(keys, values):
    tokens, width = keys.shape
    return pl.pallas_call(
        pick_kernel,
        out_shape=jax.ShapeDtypeStruct((2 * tokens // STEP, width), BF16),
        compiler_params=params(),
        name="pick",
    )(keys, values)


def grad_attn_kernel(g_ref, own_ref, other_ref, w_own_ref, w_other_ref, out_ref):
    total = nt(own_ref[...], w_own_ref[...]) + nt(other_ref[...], w_other_ref[...])
    out_ref[...] = total.astype(BF16)


def grad_attn(group, own, other, weight):
    tokens, width = own.shape
    tile = 256
    tiles = width // tile
    whole = pl.BlockSpec((tokens, width), lambda i, g: (0, 0))
    return pl.pallas_call(
        grad_attn_kernel,
        grid_spec=pltpu.PrefetchScalarGridSpec(
            num_scalar_prefetch=1,
            grid=(tiles,),
            in_specs=[
                whole,
                whole,
                pl.BlockSpec((tile, width), lambda i, g: (g[0] * tiles + i, g[0])),
                pl.BlockSpec((tile, width), lambda i, g: (g[0] * tiles + i, 1 - g[0])),
            ],
            out_specs=pl.BlockSpec((tokens, tile), lambda i, g: (0, i)),
        ),
        out_shape=jax.ShapeDtypeStruct((tokens, width), BF16),
        compiler_params=params(),
        cost_estimate=pl.CostEstimate(
            flops=4 * tokens * width * width, bytes_accessed=6 * width * width, transcendentals=0
        ),
        name="grad_attn",
    )(group, own, other, weight, weight)


def project_kernel(g_ref, own_ref, other_ref, w_own_ref, w_other_ref, out_ref):
    total = nn(own_ref[...], w_own_ref[...]) + nn(other_ref[...], w_other_ref[...])
    out_ref[...] = total.astype(BF16)


def project(group, own, other, weight):
    tokens, width = own.shape
    tile = 256
    tiles = width // tile
    whole = pl.BlockSpec((tokens, width), lambda i, g: (0, 0))
    return pl.pallas_call(
        project_kernel,
        grid_spec=pltpu.PrefetchScalarGridSpec(
            num_scalar_prefetch=1,
            grid=(tiles,),
            in_specs=[
                whole,
                whole,
                pl.BlockSpec((width, tile), lambda i, g: (g[0], g[0] * tiles + i)),
                pl.BlockSpec((width, tile), lambda i, g: (1 - g[0], g[0] * tiles + i)),
            ],
            out_specs=pl.BlockSpec((tokens, tile), lambda i, g: (0, i)),
        ),
        out_shape=jax.ShapeDtypeStruct((tokens, width), BF16),
        compiler_params=params(),
        cost_estimate=pl.CostEstimate(
            flops=4 * tokens * width * width, bytes_accessed=6 * width * width, transcendentals=0
        ),
        name="project",
    )(group, own, other, weight, weight)


def documents(positions, bounds_ref):
    count = jnp.zeros(positions.shape, jnp.int32)
    for i in range(bounds_ref.shape[0]):
        count = count + (bounds_ref[i] <= positions).astype(jnp.int32)
    return count


def mask_bias(me, bounds_ref, tokens, levels):
    rows = tokens // STEP
    own = lax.broadcasted_iota(jnp.int32, (tokens, 1), 0) + me * tokens
    parts = [lax.broadcasted_iota(jnp.int32, (1, tokens), 1) + me * tokens]
    far = lax.broadcasted_iota(jnp.int32, (1, levels * rows), 1)
    level = far // rows
    source = me - (jnp.ones_like(level) << level)
    parts.append(source * tokens + (far - level * rows) * STEP)
    own_doc = documents(own, bounds_ref)
    out = []
    for part in parts:
        part_doc = jnp.where(part >= 0, documents(part, bounds_ref), -1)
        ok = (own_doc == part_doc) & (part <= own)
        out.append(jnp.where(ok, 0.0, -jnp.inf).astype(F32))
    return jnp.concatenate(out, 1)


def attention_kernel(levels, *refs):
    me_ref, bounds_ref, q_ref, k_ref, v_ref, ga_ref = refs[:6]
    far_refs = refs[6 : 6 + levels]
    attn_ref, gq_ref, gk_ref, gv_ref = refs[6 + levels : 10 + levels]
    gfar_refs = refs[10 + levels : 10 + 2 * levels]
    bias_ref = refs[10 + 2 * levels]
    tokens = q_ref.shape[0]
    rows = tokens // STEP
    scale = 1.0 / math.sqrt(DH)

    @pl.when(pl.program_id(0) == 0)
    def _():
        bias_ref[...] = mask_bias(me_ref[0], bounds_ref, tokens, levels)

    for h in range(q_ref.shape[1] // DH):
        cols = slice(h * DH, (h + 1) * DH)
        q, ga = q_ref[:, cols], ga_ref[:, cols]
        k = jnp.concatenate([k_ref[:, cols]] + [r[:rows, cols] for r in far_refs], 0)
        v = jnp.concatenate([v_ref[:, cols]] + [r[rows:, cols] for r in far_refs], 0)
        scores = nt(q, k) * scale + bias_ref[...]
        top = jnp.max(scores, axis=1, keepdims=True)
        grown = jnp.exp(scores - top)
        prob = grown * (1.0 / jnp.sum(grown, axis=1, keepdims=True))
        weights = prob.astype(BF16)
        grad_prob = nt(ga, v)
        delta = jnp.sum(prob * grad_prob, axis=1, keepdims=True)
        grad_scores = (prob * (grad_prob - delta) * scale).astype(BF16)
        gk = tn(grad_scores, q)
        gv = tn(weights, ga)
        for i in range(levels):
            at = tokens + i * rows
            gfar_refs[i][:rows, cols] = gk[at : at + rows].astype(BF16)
            gfar_refs[i][rows:, cols] = gv[at : at + rows].astype(BF16)
        gk_ref[:, cols] = gk[:tokens]
        gv_ref[:, cols] = gv[:tokens]
        attn_ref[:, cols] = nn(weights, v).astype(BF16)
        gq_ref[:, cols] = nn(grad_scores, k).astype(BF16)


def attention(me, bounds, q, k, v, ga, far):
    tokens, width = q.shape
    levels = len(far)
    rows = tokens // STEP
    cols = 2 * DH
    block = pl.BlockSpec((tokens, cols), lambda i: (0, i))
    far_block = pl.BlockSpec((2 * rows, cols), lambda i: (0, i))
    smem = pl.BlockSpec(memory_space=pltpu.SMEM)
    bf = jax.ShapeDtypeStruct((tokens, width), BF16)
    f32 = jax.ShapeDtypeStruct((tokens, width), F32)
    return pl.pallas_call(
        functools.partial(attention_kernel, levels),
        grid=(width // cols,),
        in_specs=[smem, smem] + [block] * 4 + [far_block] * levels,
        out_specs=[block] * 4 + [far_block] * levels,
        out_shape=[bf, bf, f32, f32] + [jax.ShapeDtypeStruct((2 * rows, width), BF16)] * levels,
        scratch_shapes=[pltpu.VMEM((tokens, tokens + levels * rows), F32)],
        compiler_params=params(),
        cost_estimate=pl.CostEstimate(
            flops=12 * tokens * (tokens + levels * rows) * width,
            bytes_accessed=16 * tokens * width,
            transcendentals=0,
        ),
        name="attention",
    )(me, bounds, q, k, v, ga, *far)


def settle_kernel(count, *refs):
    gk_ref, gv_ref = refs[:2]
    back_refs = refs[2 : 2 + count]
    out_k_ref, out_v_ref = refs[2 + count :]
    tokens = gk_ref.shape[0]
    rows = tokens // STEP
    at = lax.broadcasted_iota(jnp.int32, (tokens, rows), 0)
    place = (at == lax.broadcasted_iota(jnp.int32, (tokens, rows), 1) * STEP).astype(BF16)
    place = jnp.concatenate([place] * count, 1)
    extra_k = nn(place, jnp.concatenate([r[:rows] for r in back_refs], 0))
    extra_v = nn(place, jnp.concatenate([r[rows:] for r in back_refs], 0))
    out_k_ref[...] = (gk_ref[...] + extra_k).astype(BF16)
    out_v_ref[...] = (gv_ref[...] + extra_v).astype(BF16)


def settle(gk, gv, back):
    tokens, width = gk.shape
    out = jax.ShapeDtypeStruct((tokens, width), BF16)
    cols = 512
    block = pl.BlockSpec((tokens, cols), lambda i: (0, i))
    back_block = pl.BlockSpec((back[0].shape[0], cols), lambda i: (0, i))
    return pl.pallas_call(
        functools.partial(settle_kernel, len(back)),
        grid=(width // cols,),
        in_specs=[block] * 2 + [back_block] * len(back),
        out_specs=[block] * 2,
        out_shape=[out, out],
        compiler_params=params(),
        name="settle",
    )(gk, gv, *back)


def per_device(queries, keys, values, out_weight, cotangent, bounds):
    levels = lax.axis_size("ctx").bit_length() - 1
    me = lax.axis_index("ctx").astype(jnp.int32).reshape(1)
    group = lax.axis_index("head").astype(jnp.int32).reshape(1)
    other_cot = swap(cotangent)
    picked = pick(keys, values)
    far = [shift(picked, "ctx", 2**i) for i in range(levels)]
    ga = grad_attn(group, cotangent, other_cot, out_weight)
    attn, gq, gk, gv, *gfar = attention(me, bounds, queries, keys, values, ga, far)
    back = [shift(gfar[i], "ctx", -(2**i)) for i in range(levels)]
    other_attn = swap(attn)
    output = project(group, attn, other_attn, out_weight)
    gk, gv = settle(gk, gv, back)
    return output, gq, gk, gv


def solution(mesh):
    shared = P("ctx", "head")
    return jax.shard_map(
        per_device,
        mesh=mesh,
        in_specs=(shared, shared, shared, P(), shared, P()),
        out_specs=(shared,) * 4,
        check_vma=False,
    )
```

```python
import functools
import math

import jax
import jax.numpy as jnp
from jax import lax
from jax.experimental import pallas as pl
from jax.experimental.pallas import tpu as pltpu
from jax.sharding import PartitionSpec as P

DH = 128
STEP = 4
VMEM_LIMIT = 40 * 1024 * 1024
VMEM_MOST = 58 * 1024 * 1024
BF16 = jnp.bfloat16
F32 = jnp.float32


def hop(distance, n):
    return [(i, i + distance) for i in range(n) if 0 <= i + distance < n]


def pairs(n):
    return [(i, i ^ 2) for i in range(n)]


def mixed(block, route_of_core):
    cores = len(route_of_core)
    route = [(a * cores + c, b * cores + c) for c, r in enumerate(route_of_core) for a, b in r]
    return lax.ppermute(block, ("ctx", "head"), route)


def swap(block):
    return lax.ppermute(block, "head", [(0, 1), (1, 0)])


def nt(a, b):
    return lax.dot_general(a, b, (((1,), (1,)), ((), ())), preferred_element_type=F32)


def tn(a, b):
    return lax.dot_general(a, b, (((0,), (0,)), ((), ())), preferred_element_type=F32)


def nn(a, b):
    return jnp.dot(a, b, preferred_element_type=F32)


def params(limit=VMEM_LIMIT):
    return pltpu.CompilerParams(vmem_limit_bytes=limit)


def pick_kernel(k_ref, v_ref, out_ref):
    tokens = k_ref.shape[0]
    rows = tokens // STEP
    at = lax.broadcasted_iota(jnp.int32, (rows, tokens), 0) * STEP
    choose = (at == lax.broadcasted_iota(jnp.int32, (rows, tokens), 1)).astype(BF16)
    out_ref[:rows] = nn(choose, k_ref[...]).astype(BF16)
    out_ref[rows:] = nn(choose, v_ref[...]).astype(BF16)


def pick(keys, values):
    tokens, width = keys.shape
    return pl.pallas_call(
        pick_kernel,
        out_shape=jax.ShapeDtypeStruct((2 * tokens // STEP, width), BF16),
        compiler_params=params(VMEM_MOST),
        name="pick",
    )(keys, values)


def grad_attn_kernel(g_ref, own_ref, other_ref, w_own_ref, w_other_ref, out_ref):
    total = nt(own_ref[...], w_own_ref[...]) + nt(other_ref[...], w_other_ref[...])
    out_ref[...] = total.astype(BF16)


def grad_attn(group, own, other, weight):
    tokens, width = own.shape
    tile = 256
    tiles = width // tile
    whole = pl.BlockSpec((tokens, width), lambda i, g: (0, 0))
    return pl.pallas_call(
        grad_attn_kernel,
        grid_spec=pltpu.PrefetchScalarGridSpec(
            num_scalar_prefetch=1,
            grid=(tiles,),
            in_specs=[
                whole,
                whole,
                pl.BlockSpec((tile, width), lambda i, g: (g[0] * tiles + i, g[0])),
                pl.BlockSpec((tile, width), lambda i, g: (g[0] * tiles + i, 1 - g[0])),
            ],
            out_specs=pl.BlockSpec((tokens, tile), lambda i, g: (0, i)),
        ),
        out_shape=jax.ShapeDtypeStruct((tokens, width), BF16),
        compiler_params=params(VMEM_MOST),
        cost_estimate=pl.CostEstimate(
            flops=4 * tokens * width * width, bytes_accessed=6 * width * width, transcendentals=0
        ),
        name="grad_attn",
    )(group, own, other, weight, weight)


def project_kernel(g_ref, own_ref, other_ref, w_own_ref, w_other_ref, out_ref):
    total = nn(own_ref[...], w_own_ref[...]) + nn(other_ref[...], w_other_ref[...])
    out_ref[...] = total.astype(BF16)


def project(group, own, other, weight):
    tokens, width = own.shape
    tile = 256
    tiles = width // tile
    whole = pl.BlockSpec((tokens, width), lambda i, g: (0, 0))
    return pl.pallas_call(
        project_kernel,
        grid_spec=pltpu.PrefetchScalarGridSpec(
            num_scalar_prefetch=1,
            grid=(tiles,),
            in_specs=[
                whole,
                whole,
                pl.BlockSpec((width, tile), lambda i, g: (g[0], g[0] * tiles + i)),
                pl.BlockSpec((width, tile), lambda i, g: (1 - g[0], g[0] * tiles + i)),
            ],
            out_specs=pl.BlockSpec((tokens, tile), lambda i, g: (0, i)),
        ),
        out_shape=jax.ShapeDtypeStruct((tokens, width), BF16),
        compiler_params=params(VMEM_MOST),
        cost_estimate=pl.CostEstimate(
            flops=4 * tokens * width * width, bytes_accessed=6 * width * width, transcendentals=0
        ),
        name="project",
    )(group, own, other, weight, weight)


def documents(positions, bounds_ref):
    count = jnp.zeros(positions.shape, jnp.int32)
    for i in range(bounds_ref.shape[0]):
        count = count + (bounds_ref[i] <= positions).astype(jnp.int32)
    return count


def mask_bias(me, bounds_ref, tokens, levels):
    rows = tokens // STEP
    own = lax.broadcasted_iota(jnp.int32, (tokens, 1), 0) + me * tokens
    parts = [lax.broadcasted_iota(jnp.int32, (1, tokens), 1) + me * tokens]
    far = lax.broadcasted_iota(jnp.int32, (1, levels * rows), 1)
    level = far // rows
    source = me - (jnp.ones_like(level) << level)
    parts.append(source * tokens + (far - level * rows) * STEP)
    own_doc = documents(own, bounds_ref)
    out = []
    for part in parts:
        part_doc = jnp.where(part >= 0, documents(part, bounds_ref), -1)
        ok = (own_doc == part_doc) & (part <= own)
        out.append(jnp.where(ok, 0.0, -jnp.inf).astype(F32))
    return jnp.concatenate(out, 1)


def attention_kernel(levels, *refs):
    place_ref, bounds_ref, q_ref, k_ref, v_ref, ga_ref = refs[:6]
    arrived_refs = refs[6 : 6 + levels]
    attn_ref, gq_ref, gk_ref, gv_ref = refs[6 + levels : 10 + levels]
    gfar_refs = refs[10 + levels : 10 + 2 * levels]
    bias_ref = refs[10 + 2 * levels]
    tokens = q_ref.shape[0]
    rows = tokens // STEP
    scale = 1.0 / math.sqrt(DH)
    first = place_ref[1] == 0

    @pl.when(pl.program_id(0) == 0)
    def _():
        bias_ref[...] = mask_bias(place_ref[0], bounds_ref, tokens, levels)

    for h in range(q_ref.shape[1] // DH):
        cols = slice(h * DH, (h + 1) * DH)
        q, ga = q_ref[:, cols], ga_ref[:, cols]
        one, two, three, four, *more = [r[:, cols] for r in arrived_refs]
        far = [jnp.where(first, a, b) for a, b in ((two, one), (four, three), (one, two), (three, four))]
        far += more
        k = jnp.concatenate([k_ref[:, cols]] + [f[:rows] for f in far], 0)
        v = jnp.concatenate([v_ref[:, cols]] + [f[rows:] for f in far], 0)
        scores = nt(q, k) * scale + bias_ref[...]
        top = jnp.max(scores, axis=1, keepdims=True)
        grown = jnp.exp(scores - top)
        prob = grown * (1.0 / jnp.sum(grown, axis=1, keepdims=True))
        weights = prob.astype(BF16)
        grad_prob = nt(ga, v)
        delta = jnp.sum(prob * grad_prob, axis=1, keepdims=True)
        grad_scores = (prob * (grad_prob - delta) * scale).astype(BF16)
        gk = tn(grad_scores, q)
        gv = tn(weights, ga)
        for i in range(levels):
            at = tokens + i * rows
            gfar_refs[i][:rows, cols] = gk[at : at + rows].astype(BF16)
            gfar_refs[i][rows:, cols] = gv[at : at + rows].astype(BF16)
        gk_ref[:, cols] = gk[:tokens]
        gv_ref[:, cols] = gv[:tokens]
        attn_ref[:, cols] = nn(weights, v).astype(BF16)
        gq_ref[:, cols] = nn(grad_scores, k).astype(BF16)


def attention(place, bounds, q, k, v, ga, arrived):
    tokens, width = q.shape
    levels = len(arrived)
    rows = tokens // STEP
    cols = 2 * DH
    block = pl.BlockSpec((tokens, cols), lambda i: (0, i))
    far_block = pl.BlockSpec((2 * rows, cols), lambda i: (0, i))
    smem = pl.BlockSpec(memory_space=pltpu.SMEM)
    bf = jax.ShapeDtypeStruct((tokens, width), BF16)
    f32 = jax.ShapeDtypeStruct((tokens, width), F32)
    return pl.pallas_call(
        functools.partial(attention_kernel, levels),
        grid=(width // cols,),
        in_specs=[smem, smem] + [block] * 4 + [far_block] * levels,
        out_specs=[block] * 4 + [far_block] * levels,
        out_shape=[bf, bf, f32, f32] + [jax.ShapeDtypeStruct((2 * rows, width), BF16)] * levels,
        scratch_shapes=[pltpu.VMEM((tokens, tokens + levels * rows), F32)],
        compiler_params=params(),
        cost_estimate=pl.CostEstimate(
            flops=12 * tokens * (tokens + levels * rows) * width,
            bytes_accessed=16 * tokens * width,
            transcendentals=0,
        ),
        name="attention",
    )(place, bounds, q, k, v, ga, *arrived)


def settle_kernel(count, *refs):
    gk_ref, gv_ref = refs[:2]
    back_refs = refs[2 : 2 + count]
    out_k_ref, out_v_ref = refs[3 + count :]
    tokens = gk_ref.shape[0]
    rows = tokens // STEP
    at = lax.broadcasted_iota(jnp.int32, (tokens, rows), 0)
    place = (at == lax.broadcasted_iota(jnp.int32, (tokens, rows), 1) * STEP).astype(BF16)
    place = jnp.concatenate([place] * count, 1)
    extra_k = nn(place, jnp.concatenate([r[:rows] for r in back_refs], 0))
    extra_v = nn(place, jnp.concatenate([r[rows:] for r in back_refs], 0))
    out_k_ref[...] = (gk_ref[...] + extra_k).astype(BF16)
    out_v_ref[...] = (gv_ref[...] + extra_v).astype(BF16)


def settle(gk, gv, back, after):
    tokens, width = gk.shape
    out = jax.ShapeDtypeStruct((tokens, width), BF16)
    cols = 512
    block = pl.BlockSpec((tokens, cols), lambda i: (0, i))
    back_block = pl.BlockSpec((back[0].shape[0], cols), lambda i: (0, i))
    return pl.pallas_call(
        functools.partial(settle_kernel, len(back)),
        grid=(width // cols,),
        in_specs=[block] * 2 + [back_block] * len(back) + [pl.BlockSpec(memory_space=pl.ANY)],
        out_specs=[block] * 2,
        out_shape=[out, out],
        compiler_params=params(),
        name="settle",
    )(gk, gv, *back, after)


def add(*blocks):
    total = blocks[0].astype(F32)
    for block in blocks[1:]:
        total = total + block.astype(F32)
    return total.astype(BF16)


def per_device(queries, keys, values, out_weight, cotangent, bounds):
    n = lax.axis_size("ctx")
    levels = n.bit_length() - 1
    index, core = lax.axis_index("ctx"), lax.axis_index("head")
    place = jnp.stack([index, core]).astype(jnp.int32)
    group = core.astype(jnp.int32).reshape(1)
    first = core == 0
    low = (index & 2) == 0

    other_cot = swap(cotangent)
    picked = pick(keys, values)
    one = mixed(picked, (hop(4, n), hop(1, n)))
    two = mixed(picked, (hop(1, n), hop(4, n)))
    far4 = jnp.where(first, one, two)
    lent = jnp.where(low, picked, far4)
    three = mixed(jnp.where(first, far4, lent), (hop(4, n), pairs(n)))
    four = mixed(jnp.where(first, lent, far4), (pairs(n), hop(4, n)))
    arrived = [one, two, three, four]
    farther = jnp.where(first, three, four) if levels > 4 else None
    for i in range(4, levels):
        farther = lax.ppermute(farther, "ctx", hop(2 ** (i - 1), n))
        arrived.append(farther)

    ga = grad_attn(group, cotangent, other_cot, out_weight)
    attn, gq, gk, gv, *gfar = attention(place, bounds, queries, keys, values, ga, arrived)

    for i in reversed(range(4, levels)):
        gfar[i - 1] = add(gfar[i - 1], lax.ppermute(gfar[i], "ctx", hop(-(2 ** (i - 1)), n)))
    g1, g2, g4, g8 = gfar[:4]
    one = mixed(jnp.where(first, g8, g2), (hop(-4, n), pairs(n)))
    two = mixed(jnp.where(first, g2, g8), (pairs(n), hop(-4, n)))
    back8, back2 = jnp.where(first, one, two), jnp.where(first, two, one)
    zero = jnp.zeros_like(back2)
    g4 = add(g4, back8, jnp.where(low, zero, back2))
    three = mixed(jnp.where(first, g4, g1), (hop(-4, n), hop(-1, n)))
    four = mixed(jnp.where(first, g1, g4), (hop(-1, n), hop(-4, n)))
    other_attn = swap(attn)
    output = project(group, attn, other_attn, out_weight)
    gk, gv = settle(gk, gv, [jnp.where(low, back2, zero), three, four], output)
    return output, gq, gk, gv


def solution(mesh):
    shared = P("ctx", "head")
    return jax.shard_map(
        per_device,
        mesh=mesh,
        in_specs=(shared, shared, shared, P(), shared, P()),
        out_specs=(shared,) * 4,
        check_vma=False,
    )
```

```python
import functools
import math

import jax
import jax.numpy as jnp
from jax import lax
from jax.experimental import pallas as pl
from jax.experimental.pallas import tpu as pltpu
from jax.sharding import PartitionSpec as P

DH = 128
STEP = 4
BF16 = jnp.bfloat16
F32 = jnp.float32
HBM_BLOCK = pl.BlockSpec(memory_space=pltpu.HBM)
VMEM_BLOCK = pl.BlockSpec(memory_space=pltpu.VMEM)
SMEM_BLOCK = pl.BlockSpec(memory_space=pltpu.SMEM)


def hop(distance, n):
    return [(i, i + distance) for i in range(n) if 0 <= i + distance < n]


def pairs(n):
    return [(i, i ^ 2) for i in range(n)]


def steps(n):
    return [(i, i - 3 if i % 4 == 3 else i + 1) for i in range(n)]


def turned(route):
    return [(b, a) for a, b in route]


def mixed(block, route_of_core):
    cores = len(route_of_core)
    route = [(a * cores + c, b * cores + c) for c, r in enumerate(route_of_core) for a, b in r]
    return lax.ppermute(block, ("ctx", "head"), route)


def swap(block):
    return lax.ppermute(block, "head", [(0, 1), (1, 0)])


def nt(a, b):
    return lax.dot_general(a, b, (((1,), (1,)), ((), ())), preferred_element_type=F32)


def tn(a, b):
    return lax.dot_general(a, b, (((0,), (0,)), ((), ())), preferred_element_type=F32)


def nn(a, b):
    return jnp.dot(a, b, preferred_element_type=F32)


def params(mib=24):
    return pltpu.CompilerParams(vmem_limit_bytes=int(mib * 1024 * 1024))


def pick_kernel(k_hbm, v_hbm, out_ref, held, sems):
    tokens = k_hbm.shape[0]
    rows = tokens // STEP
    copies = [pltpu.make_async_copy(x, held.at[i], sems.at[i]) for i, x in enumerate((k_hbm, v_hbm))]
    for copy in copies:
        copy.start()
    at = lax.broadcasted_iota(jnp.int32, (rows, tokens), 0) * STEP
    choose = (at == lax.broadcasted_iota(jnp.int32, (rows, tokens), 1)).astype(BF16)
    for i, copy in enumerate(copies):
        copy.wait()
        out_ref[i * rows : (i + 1) * rows] = nn(choose, held[i]).astype(BF16)


def pick(keys, values):
    tokens, width = keys.shape
    return pl.pallas_call(
        pick_kernel,
        in_specs=[HBM_BLOCK, HBM_BLOCK],
        out_shape=jax.ShapeDtypeStruct((2 * tokens // STEP, width), BF16),
        scratch_shapes=[pltpu.VMEM((2, tokens, width), BF16), pltpu.SemaphoreType.DMA((2,))],
        compiler_params=params(63.5),
        name="pick",
    )(keys, values)


def grad_attn_kernel(place_ref, own_ref, other_ref, w_hbm, out_ref, flag_ref, held, sems):
    pieces, tile, _ = held.shape
    core = place_ref[1]
    copies = []
    for i in range(pieces):
        rows = w_hbm.at[pl.ds((core * pieces + i) * tile, tile), :]
        copies.append(pltpu.make_async_copy(rows, held.at[i], sems.at[i]))
        copies[i].start()
    flag_ref[0] = place_ref[0]
    flag_ref[1] = core
    own, other = own_ref[...], other_ref[...]
    whole = jnp.concatenate([jnp.where(core == 0, own, other), jnp.where(core == 0, other, own)], 1)
    for i in range(pieces):
        copies[i].wait()
        out_ref[:, i * tile : (i + 1) * tile] = nt(whole, held[i]).astype(BF16)


def grad_attn(place, own, other, weight):
    tokens, width = own.shape
    pieces = 4
    return pl.pallas_call(
        grad_attn_kernel,
        in_specs=[SMEM_BLOCK, VMEM_BLOCK, VMEM_BLOCK, HBM_BLOCK],
        out_specs=[VMEM_BLOCK, SMEM_BLOCK],
        out_shape=[
            jax.ShapeDtypeStruct((tokens, width), BF16),
            jax.ShapeDtypeStruct(place.shape, jnp.int32),
        ],
        scratch_shapes=[
            pltpu.VMEM((pieces, width // pieces, weight.shape[1]), BF16),
            pltpu.SemaphoreType.DMA((pieces,)),
        ],
        compiler_params=params(57),
        cost_estimate=pl.CostEstimate(
            flops=4 * tokens * width * width, bytes_accessed=6 * width * width, transcendentals=0
        ),
        name="grad_attn",
    )(place, own, other, weight)


def project_kernel(place_ref, own_ref, other_ref, w_hbm, out_ref, flag_ref, held, sems):
    flag_ref[0] = place_ref[0]
    flag_ref[1] = place_ref[1]
    pieces, tile, width = held.shape
    core = place_ref[1]
    columns = pl.ds(pl.multiple_of(core * width, width), width)
    copies = []
    for i in range(pieces):
        part = w_hbm.at[pl.ds(i * tile, tile), columns]
        copies.append(pltpu.make_async_copy(part, held.at[i], sems.at[i]))
        copies[i].start()
    own, other = own_ref[...], other_ref[...]
    whole = jnp.concatenate([jnp.where(core == 0, own, other), jnp.where(core == 0, other, own)], 1)
    total = None
    for i in range(pieces):
        copies[i].wait()
        term = nn(whole[:, i * tile : (i + 1) * tile], held[i])
        total = term if total is None else total + term
    out_ref[...] = total.astype(BF16)


def project(place, own, other, weight):
    tokens, width = own.shape
    pieces = 4
    return pl.pallas_call(
        project_kernel,
        in_specs=[SMEM_BLOCK, VMEM_BLOCK, VMEM_BLOCK, HBM_BLOCK],
        out_specs=[VMEM_BLOCK, SMEM_BLOCK],
        out_shape=[
            jax.ShapeDtypeStruct((tokens, width), BF16),
            jax.ShapeDtypeStruct(place.shape, jnp.int32),
        ],
        scratch_shapes=[
            pltpu.VMEM((pieces, weight.shape[0] // pieces, width), BF16),
            pltpu.SemaphoreType.DMA((pieces,)),
        ],
        compiler_params=params(57),
        cost_estimate=pl.CostEstimate(
            flops=4 * tokens * width * width, bytes_accessed=6 * width * width, transcendentals=0
        ),
        name="project",
    )(place, own, other, weight)


def documents(positions, bounds_ref):
    count = jnp.zeros(positions.shape, jnp.int32)
    for i in range(bounds_ref.shape[0]):
        count = count + (bounds_ref[i] <= positions).astype(jnp.int32)
    return count


def mask_bias(me, bounds_ref, tokens, levels):
    rows = tokens // STEP
    own = lax.broadcasted_iota(jnp.int32, (1, tokens), 1) + me * tokens
    parts = [lax.broadcasted_iota(jnp.int32, (tokens, 1), 0) + me * tokens]
    for i in range(levels):
        at = lax.broadcasted_iota(jnp.int32, (rows, 1), 0) * STEP
        parts.append(at + (me - 2**i) * tokens)
    keys = jnp.concatenate(parts, 0)
    key_doc = jnp.where(keys >= 0, documents(keys, bounds_ref), -1)
    ok = (documents(own, bounds_ref) == key_doc) & (keys <= own)
    return jnp.where(ok, 0.0, -jnp.inf).astype(F32)


def sort_arrived(first, arrived):
    far4, two, three, four, *more = arrived
    far1 = jnp.where(first, three, two)
    far2 = jnp.where(first, four, three)
    far8 = jnp.where(first, two, four)
    return [far1, far2, far4, far8, *more]


def scores_kernel(levels, *refs):
    place_ref, bounds_ref, q_ref, k_ref, v_ref, ga_ref = refs[:6]
    arrived_refs = refs[6 : 6 + levels]
    w_ref, u_ref = refs[6 + levels : 8 + levels]
    gfar_refs = refs[8 + levels : 8 + 2 * levels]
    bias_ref = refs[8 + 2 * levels]
    tokens = q_ref.shape[0]
    rows = tokens // STEP
    scale = 1.0 / math.sqrt(DH)
    first = place_ref[1] == 0

    @pl.when(pl.program_id(0) == 0)
    def _():
        bias_ref[...] = mask_bias(place_ref[0], bounds_ref, tokens, levels)

    for h in range(q_ref.shape[1] // DH):
        cols = slice(h * DH, (h + 1) * DH)
        q, ga = q_ref[:, cols], ga_ref[:, cols]
        far = sort_arrived(first, [r[:, cols] for r in arrived_refs])
        k = jnp.concatenate([k_ref[:, cols]] + [f[:rows] for f in far], 0)
        v = jnp.concatenate([v_ref[:, cols]] + [f[rows:] for f in far], 0)
        scores = nt(k, q) + bias_ref[...]
        top = jnp.max(scores, axis=0, keepdims=True)
        grown = jnp.exp2((scores - top) * (scale * math.log2(math.e)))
        prob = grown * (1.0 / jnp.sum(grown, axis=0, keepdims=True))
        weights = prob.astype(BF16)
        grad_prob = nt(v, ga)
        delta = jnp.sum(prob * grad_prob, axis=0, keepdims=True)
        grad_scores = (prob * (grad_prob - delta)).astype(BF16)
        w_ref[h] = weights
        u_ref[h] = grad_scores
        gk = (nn(grad_scores[tokens:], q) * scale).astype(BF16)
        gv = nn(weights[tokens:], ga).astype(BF16)
        g1, g2, g4, g8, *more = [
            jnp.concatenate([g[i * rows : (i + 1) * rows] for g in (gk, gv)], 0) for i in range(levels)
        ]
        out = [g4, jnp.where(first, g8, g1), jnp.where(first, g1, g2), jnp.where(first, g2, g8)]
        for ref, block in zip(gfar_refs, out + more):
            ref[:, cols] = block


def attention_scores(place, bounds, q, k, v, ga, arrived):
    tokens, width = q.shape
    levels = len(arrived)
    rows = tokens // STEP
    count = tokens + levels * rows
    step = 2
    block = pl.BlockSpec((tokens, step * DH), lambda i: (0, i))
    far_block = pl.BlockSpec((2 * rows, step * DH), lambda i: (0, i))
    prob_block = pl.BlockSpec((step, count, tokens), lambda i: (i, 0, 0))
    prob = jax.ShapeDtypeStruct((width // DH, count, tokens), BF16)
    return pl.pallas_call(
        functools.partial(scores_kernel, levels),
        grid=(width // (step * DH),),
        in_specs=[SMEM_BLOCK, SMEM_BLOCK] + [block] * 4 + [far_block] * levels,
        out_specs=[prob_block] * 2 + [far_block] * levels,
        out_shape=[prob, prob] + [jax.ShapeDtypeStruct((2 * rows, width), BF16)] * levels,
        scratch_shapes=[pltpu.VMEM((count, tokens), F32)],
        compiler_params=params(),
        cost_estimate=pl.CostEstimate(
            flops=6 * tokens * count * width, bytes_accessed=16 * tokens * width, transcendentals=0
        ),
        name="attention_scores",
    )(place, bounds, q, k, v, ga, *arrived)


def local_kernel(levels, *refs):
    place_ref, q_ref, k_ref, v_ref, ga_ref, w_ref, u_ref = refs[:7]
    arrived_refs = refs[7 : 7 + levels]
    attn_ref, gq_ref, gk_ref, gv_ref, flag_ref = refs[7 + levels :]
    tokens = q_ref.shape[0]
    rows = tokens // STEP
    scale = 1.0 / math.sqrt(DH)
    first = place_ref[1] == 0
    flag_ref[0] = place_ref[0]
    flag_ref[1] = place_ref[1]
    for h in range(q_ref.shape[1] // DH):
        cols = slice(h * DH, (h + 1) * DH)
        far = sort_arrived(first, [r[:, cols] for r in arrived_refs])
        k = jnp.concatenate([k_ref[:, cols]] + [f[:rows] for f in far], 0)
        v = jnp.concatenate([v_ref[:, cols]] + [f[rows:] for f in far], 0)
        weights, grad_scores = w_ref[h], u_ref[h]
        attn_ref[:, cols] = tn(weights, v).astype(BF16)
        gq_ref[:, cols] = (tn(grad_scores, k) * scale).astype(BF16)
        gk_ref[:, cols] = nn(grad_scores[:tokens], q_ref[:, cols]) * scale
        gv_ref[:, cols] = nn(weights[:tokens], ga_ref[:, cols])


def attention_local(place, q, k, v, ga, weights, grad_scores, arrived):
    tokens, width = q.shape
    levels = len(arrived)
    rows = tokens // STEP
    count = tokens + levels * rows
    step = 2
    block = pl.BlockSpec((tokens, step * DH), lambda i: (0, i))
    far_block = pl.BlockSpec((2 * rows, step * DH), lambda i: (0, i))
    prob_block = pl.BlockSpec((step, count, tokens), lambda i: (i, 0, 0))
    bf = jax.ShapeDtypeStruct((tokens, width), BF16)
    f32 = jax.ShapeDtypeStruct((tokens, width), F32)
    return pl.pallas_call(
        functools.partial(local_kernel, levels),
        grid=(width // (step * DH),),
        in_specs=[SMEM_BLOCK] + [block] * 4 + [prob_block] * 2 + [far_block] * levels,
        out_specs=[block] * 4 + [SMEM_BLOCK],
        out_shape=[bf, bf, f32, f32, jax.ShapeDtypeStruct(place.shape, jnp.int32)],
        compiler_params=params(),
        cost_estimate=pl.CostEstimate(
            flops=6 * tokens * count * width, bytes_accessed=16 * tokens * width, transcendentals=0
        ),
        name="attention_local",
    )(place, q, k, v, ga, weights, grad_scores, *arrived)


def settle_kernel(count, *refs):
    gk_ref, gv_ref = refs[:2]
    back_refs = refs[2 : 2 + count]
    out_k_ref, out_v_ref = refs[3 + count :]
    tokens = gk_ref.shape[0]
    rows = tokens // STEP
    at = lax.broadcasted_iota(jnp.int32, (tokens, rows), 0)
    place = (at == lax.broadcasted_iota(jnp.int32, (tokens, rows), 1) * STEP).astype(BF16)
    place = jnp.concatenate([place] * count, 1)
    extra_k = nn(place, jnp.concatenate([r[:rows] for r in back_refs], 0))
    extra_v = nn(place, jnp.concatenate([r[rows:] for r in back_refs], 0))
    out_k_ref[...] = (gk_ref[...] + extra_k).astype(BF16)
    out_v_ref[...] = (gv_ref[...] + extra_v).astype(BF16)


def settle(gk, gv, back, after):
    tokens, width = gk.shape
    out = jax.ShapeDtypeStruct((tokens, width), BF16)
    cols = 512
    block = pl.BlockSpec((tokens, cols), lambda i: (0, i))
    back_block = pl.BlockSpec((back[0].shape[0], cols), lambda i: (0, i))
    return pl.pallas_call(
        functools.partial(settle_kernel, len(back)),
        grid=(width // cols,),
        in_specs=[block] * 2 + [back_block] * len(back) + [SMEM_BLOCK],
        out_specs=[block] * 2,
        out_shape=[out, out],
        compiler_params=params(),
        name="settle",
    )(gk, gv, *back, after)


def add(*blocks):
    total = blocks[0].astype(F32)
    for block in blocks[1:]:
        total = total + block.astype(F32)
    return total.astype(BF16)


def per_device(queries, keys, values, out_weight, cotangent, bounds):
    n = lax.axis_size("ctx")
    levels = n.bit_length() - 1
    place = jnp.stack([lax.axis_index("ctx"), lax.axis_index("head")]).astype(jnp.int32)

    other_cot = swap(cotangent)
    picked = pick(keys, values)
    far4 = lax.ppermute(picked, "ctx", hop(4, n))
    ga, flags = grad_attn(place, cotangent, other_cot, out_weight)

    first = flags[1] == 0
    lent1 = jnp.where(flags[0] % 4 == 3, far4, picked)
    lent2 = jnp.where(flags[0] % 4 < 2, picked, far4)
    hops, ones, twos = hop(4, n), steps(n), pairs(n)
    two = mixed(jnp.where(first, far4, lent1), (hops, ones))
    three = mixed(jnp.where(first, lent1, lent2), (ones, twos))
    four = mixed(jnp.where(first, lent2, far4), (twos, hops))
    arrived = [far4, two, three, four]
    farther = jnp.where(first, two, four) if levels > 4 else None
    for i in range(4, levels):
        farther = lax.ppermute(farther, "ctx", hop(2 ** (i - 1), n))
        arrived.append(farther)

    weights, grad_scores, g4, two, three, four, *more = attention_scores(
        place, bounds, queries, keys, values, ga, arrived
    )
    for i in reversed(range(len(more))):
        back = lax.ppermute(more[i], "ctx", hop(-(2 ** (i + 3)), n))
        if i > 0:
            more[i - 1] = add(more[i - 1], back)
        else:
            two = jnp.where(place[1] == 0, add(two, back), two)
            four = jnp.where(place[1] == 0, four, add(four, back))
    hops, ones, twos = hop(-4, n), turned(ones), turned(twos)
    two = mixed(two, (hops, ones))
    three = mixed(three, (ones, twos))
    four = mixed(four, (twos, hops))
    attn, gq, gk, gv, flags = attention_local(
        place, queries, keys, values, ga, weights, grad_scores, arrived
    )
    first = flags[1] == 0
    own1, own2 = flags[0] % 4 != 3, flags[0] % 4 < 2
    back1, back2 = jnp.where(first, three, two), jnp.where(first, four, three)
    back8 = jnp.where(first, two, four)
    zero = jnp.zeros_like(back1)
    g4 = add(g4, back8, jnp.where(own1, zero, back1), jnp.where(own2, zero, back2))
    back4 = lax.ppermute(g4, "ctx", hop(-4, n))
    other_attn = swap(attn)
    output, flags = project(place, attn, other_attn, out_weight)
    back = [back4, jnp.where(own1, back1, zero), jnp.where(own2, back2, zero)]
    gk, gv = settle(gk, gv, back, flags)
    return output, gq, gk, gv


def solution(mesh):
    shared = P("ctx", "head")
    return jax.shard_map(
        per_device,
        mesh=mesh,
        in_specs=(shared, shared, shared, P(), shared, P()),
        out_specs=(shared,) * 4,
        check_vma=False,
    )
```

```python
import functools
import math

import jax
import jax.numpy as jnp
from jax import lax
from jax.experimental import pallas as pl
from jax.experimental.pallas import tpu as pltpu
from jax.sharding import PartitionSpec as P

DH = 128
STEP = 4
BF16 = jnp.bfloat16
F32 = jnp.float32
HBM_BLOCK = pl.BlockSpec(memory_space=pltpu.HBM)
VMEM_BLOCK = pl.BlockSpec(memory_space=pltpu.VMEM)
SMEM_BLOCK = pl.BlockSpec(memory_space=pltpu.SMEM)


def hop(distance, n):
    return [(i, i + distance) for i in range(n) if 0 <= i + distance < n]


def pairs(n):
    return [(i, i ^ 2) for i in range(n)]


def steps(n):
    return [(i, i - 3 if i % 4 == 3 else i + 1) for i in range(n)]


def turned(route):
    return [(b, a) for a, b in route]


def mixed(block, route_of_core):
    cores = len(route_of_core)
    route = [(a * cores + c, b * cores + c) for c, r in enumerate(route_of_core) for a, b in r]
    return lax.ppermute(block, ("ctx", "head"), route)


def swap(block):
    return lax.ppermute(block, "head", [(0, 1), (1, 0)])


def nt(a, b):
    return lax.dot_general(a, b, (((1,), (1,)), ((), ())), preferred_element_type=F32)


def tn(a, b):
    return lax.dot_general(a, b, (((0,), (0,)), ((), ())), preferred_element_type=F32)


def nn(a, b):
    return jnp.dot(a, b, preferred_element_type=F32)


def params(mib=24):
    return pltpu.CompilerParams(vmem_limit_bytes=int(mib * 1024 * 1024))


def pick_kernel(k_hbm, v_hbm, out_ref, held, sems):
    tokens = k_hbm.shape[0]
    rows = tokens // STEP
    copies = [pltpu.make_async_copy(x, held.at[i], sems.at[i]) for i, x in enumerate((k_hbm, v_hbm))]
    for copy in copies:
        copy.start()
    at = lax.broadcasted_iota(jnp.int32, (rows, tokens), 0) * STEP
    choose = (at == lax.broadcasted_iota(jnp.int32, (rows, tokens), 1)).astype(BF16)
    for i, copy in enumerate(copies):
        copy.wait()
        out_ref[i * rows : (i + 1) * rows] = nn(choose, held[i]).astype(BF16)


def pick(keys, values):
    tokens, width = keys.shape
    return pl.pallas_call(
        pick_kernel,
        in_specs=[HBM_BLOCK, HBM_BLOCK],
        out_shape=jax.ShapeDtypeStruct((2 * tokens // STEP, width), BF16),
        scratch_shapes=[pltpu.VMEM((2, tokens, width), BF16), pltpu.SemaphoreType.DMA((2,))],
        compiler_params=params(63.5),
        name="pick",
    )(keys, values)


def grad_attn_kernel(place_ref, own_ref, other_ref, w_hbm, out_ref, held, sems):
    pieces, tile, _ = held.shape
    core = place_ref[1]
    copies = []
    for i in range(pieces):
        rows = w_hbm.at[pl.ds((core * pieces + i) * tile, tile), :]
        copies.append(pltpu.make_async_copy(rows, held.at[i], sems.at[i]))
        copies[i].start()
    own, other = own_ref[...], other_ref[...]
    whole = jnp.concatenate([jnp.where(core == 0, own, other), jnp.where(core == 0, other, own)], 1)
    for i in range(pieces):
        copies[i].wait()
        out_ref[:, i * tile : (i + 1) * tile] = nt(whole, held[i]).astype(BF16)


def grad_attn(place, own, other, weight):
    tokens, width = own.shape
    pieces = 4
    return pl.pallas_call(
        grad_attn_kernel,
        in_specs=[SMEM_BLOCK, VMEM_BLOCK, VMEM_BLOCK, HBM_BLOCK],
        out_specs=VMEM_BLOCK,
        out_shape=jax.ShapeDtypeStruct((tokens, width), BF16),
        scratch_shapes=[
            pltpu.VMEM((pieces, width // pieces, weight.shape[1]), BF16),
            pltpu.SemaphoreType.DMA((pieces,)),
        ],
        compiler_params=params(57),
        cost_estimate=pl.CostEstimate(
            flops=4 * tokens * width * width, bytes_accessed=6 * width * width, transcendentals=0
        ),
        name="grad_attn",
    )(place, own, other, weight)


def project_kernel(place_ref, own_ref, other_ref, w_hbm, out_ref, held, sems):
    pieces, tile, width = held.shape
    core = place_ref[1]
    columns = pl.ds(pl.multiple_of(core * width, width), width)
    copies = []
    for i in range(pieces):
        part = w_hbm.at[pl.ds(i * tile, tile), columns]
        copies.append(pltpu.make_async_copy(part, held.at[i], sems.at[i]))
        copies[i].start()
    own, other = own_ref[...], other_ref[...]
    whole = jnp.concatenate([jnp.where(core == 0, own, other), jnp.where(core == 0, other, own)], 1)
    total = None
    for i in range(pieces):
        copies[i].wait()
        term = nn(whole[:, i * tile : (i + 1) * tile], held[i])
        total = term if total is None else total + term
    out_ref[...] = total.astype(BF16)


def project(place, own, other, weight):
    tokens, width = own.shape
    pieces = 4
    return pl.pallas_call(
        project_kernel,
        in_specs=[SMEM_BLOCK, VMEM_BLOCK, VMEM_BLOCK, HBM_BLOCK],
        out_specs=VMEM_BLOCK,
        out_shape=jax.ShapeDtypeStruct((tokens, width), BF16),
        scratch_shapes=[
            pltpu.VMEM((pieces, weight.shape[0] // pieces, width), BF16),
            pltpu.SemaphoreType.DMA((pieces,)),
        ],
        compiler_params=params(57),
        cost_estimate=pl.CostEstimate(
            flops=4 * tokens * width * width, bytes_accessed=6 * width * width, transcendentals=0
        ),
        name="project",
    )(place, own, other, weight)


def documents(positions, bounds_ref):
    count = jnp.zeros(positions.shape, jnp.int32)
    for i in range(bounds_ref.shape[0]):
        count = count + (bounds_ref[i] <= positions).astype(jnp.int32)
    return count


def mask_bias(me, bounds_ref, tokens, levels):
    rows = tokens // STEP
    own = lax.broadcasted_iota(jnp.int32, (1, tokens), 1) + me * tokens
    parts = [lax.broadcasted_iota(jnp.int32, (tokens, 1), 0) + me * tokens]
    for i in range(levels):
        at = lax.broadcasted_iota(jnp.int32, (rows, 1), 0) * STEP
        parts.append(at + (me - 2**i) * tokens)
    keys = jnp.concatenate(parts, 0)
    key_doc = jnp.where(keys >= 0, documents(keys, bounds_ref), -1)
    ok = (documents(own, bounds_ref) == key_doc) & (keys <= own)
    return jnp.where(ok, 0.0, -jnp.inf).astype(F32)


def sort_arrived(first, arrived):
    far4, two, three, four, *more = arrived
    far1 = jnp.where(first, three, two)
    far2 = jnp.where(first, four, three)
    far8 = jnp.where(first, two, four)
    return [far1, far2, far4, far8, *more]


def scores_kernel(levels, *refs):
    place_ref, bounds_ref, q_ref, k_ref, v_ref, ga_ref = refs[:6]
    arrived_refs = refs[6 : 6 + levels]
    w_ref, u_ref = refs[6 + levels : 8 + levels]
    gfar_refs = refs[8 + levels : 8 + 2 * levels]
    bias_ref = refs[8 + 2 * levels]
    tokens = q_ref.shape[0]
    rows = tokens // STEP
    scale = 1.0 / math.sqrt(DH)
    first = place_ref[1] == 0
    bias_ref[...] = mask_bias(place_ref[0], bounds_ref, tokens, levels)
    for h in range(q_ref.shape[1] // DH):
        cols = slice(h * DH, (h + 1) * DH)
        q, ga = q_ref[:, cols], ga_ref[:, cols]
        far = sort_arrived(first, [r[:, cols] for r in arrived_refs])
        k = jnp.concatenate([k_ref[:, cols]] + [f[:rows] for f in far], 0)
        v = jnp.concatenate([v_ref[:, cols]] + [f[rows:] for f in far], 0)
        scores = nt(k, q) + bias_ref[...]
        top = jnp.max(scores, axis=0, keepdims=True)
        grown = jnp.exp2((scores - top) * (scale * math.log2(math.e)))
        prob = grown * (1.0 / jnp.sum(grown, axis=0, keepdims=True))
        weights = prob.astype(BF16)
        grad_prob = nt(v, ga)
        delta = jnp.sum(prob * grad_prob, axis=0, keepdims=True)
        grad_scores = (prob * (grad_prob - delta)).astype(BF16)
        w_ref[h] = weights
        u_ref[h] = grad_scores
        gk = (nn(grad_scores[tokens:], q) * scale).astype(BF16)
        gv = nn(weights[tokens:], ga).astype(BF16)
        g1, g2, g4, g8, *more = [
            jnp.concatenate([g[i * rows : (i + 1) * rows] for g in (gk, gv)], 0) for i in range(levels)
        ]
        out = [g4, jnp.where(first, g8, g1), jnp.where(first, g1, g2), jnp.where(first, g2, g8)]
        for ref, block in zip(gfar_refs, out + more):
            ref[:, cols] = block


def attention_scores(place, bounds, q, k, v, ga, arrived):
    tokens, width = q.shape
    levels = len(arrived)
    rows = tokens // STEP
    count = tokens + levels * rows
    prob = jax.ShapeDtypeStruct((width // DH, count, tokens), BF16)
    return pl.pallas_call(
        functools.partial(scores_kernel, levels),
        in_specs=[SMEM_BLOCK, SMEM_BLOCK] + [VMEM_BLOCK] * (4 + levels),
        out_specs=[VMEM_BLOCK] * (2 + levels),
        out_shape=[prob, prob] + [jax.ShapeDtypeStruct((2 * rows, width), BF16)] * levels,
        scratch_shapes=[pltpu.VMEM((count, tokens), F32)],
        compiler_params=params(),
        cost_estimate=pl.CostEstimate(
            flops=6 * tokens * count * width, bytes_accessed=16 * tokens * width, transcendentals=0
        ),
        name="attention_scores",
    )(place, bounds, q, k, v, ga, *arrived)


def local_kernel(levels, *refs):
    place_ref, q_ref, k_ref, v_ref, ga_ref, w_ref, u_ref = refs[:7]
    arrived_refs = refs[7 : 7 + levels]
    attn_ref, gq_ref, gk_ref, gv_ref = refs[7 + levels :]
    tokens = q_ref.shape[0]
    rows = tokens // STEP
    scale = 1.0 / math.sqrt(DH)
    first = place_ref[1] == 0
    for h in range(q_ref.shape[1] // DH):
        cols = slice(h * DH, (h + 1) * DH)
        far = sort_arrived(first, [r[:, cols] for r in arrived_refs])
        k = jnp.concatenate([k_ref[:, cols]] + [f[:rows] for f in far], 0)
        v = jnp.concatenate([v_ref[:, cols]] + [f[rows:] for f in far], 0)
        weights, grad_scores = w_ref[h], u_ref[h]
        attn_ref[:, cols] = tn(weights, v).astype(BF16)
        gq_ref[:, cols] = (tn(grad_scores, k) * scale).astype(BF16)
        gk_ref[:, cols] = nn(grad_scores[:tokens], q_ref[:, cols]) * scale
        gv_ref[:, cols] = nn(weights[:tokens], ga_ref[:, cols])


def attention_local(place, q, k, v, ga, weights, grad_scores, arrived):
    tokens, width = q.shape
    levels = len(arrived)
    count = weights.shape[1]
    bf = jax.ShapeDtypeStruct((tokens, width), BF16)
    f32 = jax.ShapeDtypeStruct((tokens, width), F32)
    return pl.pallas_call(
        functools.partial(local_kernel, levels),
        in_specs=[SMEM_BLOCK] + [VMEM_BLOCK] * (6 + levels),
        out_specs=[VMEM_BLOCK] * 4,
        out_shape=[bf, bf, f32, f32],
        compiler_params=params(),
        cost_estimate=pl.CostEstimate(
            flops=6 * tokens * count * width, bytes_accessed=16 * tokens * width, transcendentals=0
        ),
        name="attention_local",
    )(place, q, k, v, ga, weights, grad_scores, *arrived)


def lends_own(index):
    return index % 4 != 3, index % 4 < 2


def settle_kernel(place_ref, gk_ref, gv_ref, four_ref, one_ref, two_ref, three_ref, *out_refs):
    tokens = gk_ref.shape[0]
    rows = tokens // STEP
    first = place_ref[1] == 0
    own1, own2 = lends_own(place_ref[0])
    back1 = jnp.where(first, two_ref[...], one_ref[...])
    back2 = jnp.where(first, three_ref[...], two_ref[...])
    back1 = jnp.where(own1, back1, jnp.zeros_like(back1))
    back2 = jnp.where(own2, back2, jnp.zeros_like(back2))
    back = (four_ref[...], back1, back2)
    at = lax.broadcasted_iota(jnp.int32, (tokens, rows), 0)
    spot = (at == lax.broadcasted_iota(jnp.int32, (tokens, rows), 1) * STEP).astype(BF16)
    spot = jnp.concatenate([spot] * len(back), 1)
    for i, (near_ref, out_ref) in enumerate(zip((gk_ref, gv_ref), out_refs)):
        extra = nn(spot, jnp.concatenate([b[i * rows : (i + 1) * rows] for b in back], 0))
        out_ref[...] = (near_ref[...] + extra).astype(BF16)


def settle(place, gk, gv, back4, one, two, three):
    out = jax.ShapeDtypeStruct(gk.shape, BF16)
    return pl.pallas_call(
        settle_kernel,
        in_specs=[SMEM_BLOCK] + [VMEM_BLOCK] * 6,
        out_specs=[VMEM_BLOCK] * 2,
        out_shape=[out, out],
        compiler_params=params(),
        name="settle",
    )(place, gk, gv, back4, one, two, three)


def add(*blocks):
    total = blocks[0].astype(F32)
    for block in blocks[1:]:
        total = total + block.astype(F32)
    return total.astype(BF16)


def per_device(queries, keys, values, out_weight, cotangent, bounds):
    n = lax.axis_size("ctx")
    levels = n.bit_length() - 1
    place = jnp.stack([lax.axis_index("ctx"), lax.axis_index("head")]).astype(jnp.int32)

    other_cot = swap(cotangent)
    picked = pick(keys, values)
    far4 = lax.ppermute(picked, "ctx", hop(4, n))
    ga = grad_attn(place, cotangent, other_cot, out_weight)

    first = lax.axis_index("head") == 0
    own1, own2 = lends_own(lax.axis_index("ctx"))
    lent1, lent2 = jnp.where(own1, picked, far4), jnp.where(own2, picked, far4)
    hops, ones, twos = hop(4, n), steps(n), pairs(n)
    two = mixed(jnp.where(first, far4, lent1), (hops, ones))
    three = mixed(jnp.where(first, lent1, lent2), (ones, twos))
    four = mixed(jnp.where(first, lent2, far4), (twos, hops))
    arrived = [far4, two, three, four]
    farther = jnp.where(first, two, four) if levels > 4 else None
    for i in range(4, levels):
        farther = lax.ppermute(farther, "ctx", hop(2 ** (i - 1), n))
        arrived.append(farther)

    weights, grad_scores, g4, two, three, four, *more = attention_scores(
        place, bounds, queries, keys, values, ga, arrived
    )
    for i in reversed(range(len(more))):
        back = lax.ppermute(more[i], "ctx", hop(-(2 ** (i + 3)), n))
        if i > 0:
            more[i - 1] = add(more[i - 1], back)
        else:
            two = jnp.where(first, add(two, back), two)
            four = jnp.where(first, four, add(four, back))
    hops, ones, twos = hop(-4, n), turned(ones), turned(twos)
    two = mixed(two, (hops, ones))
    three = mixed(three, (ones, twos))
    four = mixed(four, (twos, hops))
    attn, gq, gk, gv = attention_local(
        place, queries, keys, values, ga, weights, grad_scores, arrived
    )
    back1, back2 = jnp.where(first, three, two), jnp.where(first, four, three)
    back8 = jnp.where(first, two, four)
    zero = jnp.zeros_like(back1)
    g4 = add(g4, back8, jnp.where(own1, zero, back1), jnp.where(own2, zero, back2))
    back4 = lax.ppermute(g4, "ctx", hop(-4, n))
    other_attn = swap(attn)
    output = project(place, attn, other_attn, out_weight)
    gk, gv = settle(place, gk, gv, back4, two, three, four)
    return output, gq, gk, gv


def solution(mesh):
    shared = P("ctx", "head")
    return jax.shard_map(
        per_device,
        mesh=mesh,
        in_specs=(shared, shared, shared, P(), shared, P()),
        out_specs=(shared,) * 4,
        check_vma=False,
    )
```

```python
import functools
import math

import jax
import jax.numpy as jnp
from jax import lax
from jax.experimental import pallas as pl
from jax.experimental.pallas import tpu as pltpu
from jax.sharding import PartitionSpec as P

DH = 128
STEP = 4
BF16 = jnp.bfloat16
F32 = jnp.float32
HBM_BLOCK = pl.BlockSpec(memory_space=pltpu.HBM)
VMEM_BLOCK = pl.BlockSpec(memory_space=pltpu.VMEM)
SMEM_BLOCK = pl.BlockSpec(memory_space=pltpu.SMEM)


def hop(distance, n):
    return [(i, i + distance) for i in range(n) if 0 <= i + distance < n]


def pairs(n):
    return [(i, i ^ 2) for i in range(n)]


def steps(n):
    return [(i, i - 3 if i % 4 == 3 else i + 1) for i in range(n)]


def turned(route):
    return [(b, a) for a, b in route]


def mixed(block, route_of_core):
    cores = len(route_of_core)
    route = [(a * cores + c, b * cores + c) for c, r in enumerate(route_of_core) for a, b in r]
    return lax.ppermute(block, ("ctx", "head"), route)


def swap(block):
    return lax.ppermute(block, "head", [(0, 1), (1, 0)])


def nt(a, b):
    return lax.dot_general(a, b, (((1,), (1,)), ((), ())), preferred_element_type=F32)


def tn(a, b):
    return lax.dot_general(a, b, (((0,), (0,)), ((), ())), preferred_element_type=F32)


def nn(a, b):
    return jnp.dot(a, b, preferred_element_type=F32)


def params(mib=24):
    return pltpu.CompilerParams(vmem_limit_bytes=int(mib * 1024 * 1024))


def pick_kernel(k_hbm, v_hbm, out_ref, held, sems):
    tokens = k_hbm.shape[0]
    rows = tokens // STEP
    copies = [pltpu.make_async_copy(x, held.at[i], sems.at[i]) for i, x in enumerate((k_hbm, v_hbm))]
    for copy in copies:
        copy.start()
    at = lax.broadcasted_iota(jnp.int32, (rows, tokens), 0) * STEP
    choose = (at == lax.broadcasted_iota(jnp.int32, (rows, tokens), 1)).astype(BF16)
    for i, copy in enumerate(copies):
        copy.wait()
        out_ref[i * rows : (i + 1) * rows] = nn(choose, held[i]).astype(BF16)


def pick(keys, values):
    tokens, width = keys.shape
    return pl.pallas_call(
        pick_kernel,
        in_specs=[HBM_BLOCK, HBM_BLOCK],
        out_shape=jax.ShapeDtypeStruct((2 * tokens // STEP, width), BF16),
        scratch_shapes=[pltpu.VMEM((2, tokens, width), BF16), pltpu.SemaphoreType.DMA((2,))],
        compiler_params=params(63.5),
        name="pick",
    )(keys, values)


def grad_attn_kernel(
    core_ref, own_hbm, other_hbm, picked_ref, w_hbm, out_ref, handed_ref, cot, held, cot_sems, sems
):
    pieces, tile, _ = held.shape
    width = own_hbm.shape[1]
    core = core_ref[0]
    copies = []
    for source, at, i in ((own_hbm, core, 0), (other_hbm, 1 - core, 1)):
        columns = pl.ds(pl.multiple_of(at * width, width), width)
        copies.append(pltpu.make_async_copy(source, cot.at[:, columns], cot_sems.at[i]))
    for i in range(pieces):
        rows = w_hbm.at[pl.ds((core * pieces + i) * tile, tile), :]
        copies.append(pltpu.make_async_copy(rows, held.at[i], sems.at[i]))
    for copy in copies:
        copy.start()
    handed_ref[...] = picked_ref[...]
    copies[0].wait()
    copies[1].wait()
    for i in range(pieces):
        copies[2 + i].wait()
        out_ref[:, i * tile : (i + 1) * tile] = nt(cot[...], held[i]).astype(BF16)


def grad_attn(core, own, other, picked, weight):
    tokens, width = own.shape
    pieces = 4
    return pl.pallas_call(
        grad_attn_kernel,
        in_specs=[SMEM_BLOCK, HBM_BLOCK, HBM_BLOCK, VMEM_BLOCK, HBM_BLOCK],
        out_specs=[VMEM_BLOCK] * 2,
        out_shape=[
            jax.ShapeDtypeStruct((tokens, width), BF16),
            jax.ShapeDtypeStruct(picked.shape, BF16),
        ],
        scratch_shapes=[
            pltpu.VMEM((tokens, weight.shape[1]), BF16),
            pltpu.VMEM((pieces, width // pieces, weight.shape[1]), BF16),
            pltpu.SemaphoreType.DMA((2,)),
            pltpu.SemaphoreType.DMA((pieces,)),
        ],
        compiler_params=params(57),
        cost_estimate=pl.CostEstimate(
            flops=4 * tokens * width * width, bytes_accessed=6 * width * width, transcendentals=0
        ),
        name="grad_attn",
    )(core, own, other, picked, weight)


def project_kernel(core_ref, own_ref, other_ref, w_hbm, out_ref, held, sems):
    pieces, tile, width = held.shape
    core = core_ref[0]
    columns = pl.ds(pl.multiple_of(core * width, width), width)
    copies = []
    for i in range(pieces):
        part = w_hbm.at[pl.ds(i * tile, tile), columns]
        copies.append(pltpu.make_async_copy(part, held.at[i], sems.at[i]))
        copies[i].start()
    own, other = own_ref[...], other_ref[...]
    whole = jnp.concatenate([jnp.where(core == 0, own, other), jnp.where(core == 0, other, own)], 1)
    total = None
    for i in range(pieces):
        copies[i].wait()
        term = nn(whole[:, i * tile : (i + 1) * tile], held[i])
        total = term if total is None else total + term
    out_ref[...] = total.astype(BF16)


def project(core, own, other, weight):
    tokens, width = own.shape
    pieces = 4
    return pl.pallas_call(
        project_kernel,
        in_specs=[SMEM_BLOCK, VMEM_BLOCK, VMEM_BLOCK, HBM_BLOCK],
        out_specs=VMEM_BLOCK,
        out_shape=jax.ShapeDtypeStruct((tokens, width), BF16),
        scratch_shapes=[
            pltpu.VMEM((pieces, weight.shape[0] // pieces, width), BF16),
            pltpu.SemaphoreType.DMA((pieces,)),
        ],
        compiler_params=params(57),
        cost_estimate=pl.CostEstimate(
            flops=4 * tokens * width * width, bytes_accessed=6 * width * width, transcendentals=0
        ),
        name="project",
    )(core, own, other, weight)


def documents(positions, bounds_ref):
    count = jnp.zeros(positions.shape, jnp.int32)
    for i in range(bounds_ref.shape[0]):
        count = count + (bounds_ref[i] <= positions).astype(jnp.int32)
    return count


def mask_bias(me, bounds_ref, tokens, order):
    rows = tokens // STEP
    own = lax.broadcasted_iota(jnp.int32, (1, tokens), 1) + me * tokens
    parts = [lax.broadcasted_iota(jnp.int32, (tokens, 1), 0) + me * tokens]
    for distance in order:
        at = lax.broadcasted_iota(jnp.int32, (rows, 1), 0) * STEP
        parts.append(at + (me - distance) * tokens)
    keys = jnp.concatenate(parts, 0)
    key_doc = jnp.where(keys >= 0, documents(keys, bounds_ref), -1)
    ok = (documents(own, bounds_ref) == key_doc) & (keys <= own)
    return jnp.where(ok, 0.0, -jnp.inf).astype(F32)


def sort_arrived(first, two, three, four, *more):
    return [jnp.where(first, three, two), jnp.where(first, four, three), jnp.where(first, two, four), *more]


def distances(levels):
    return [4, 1, 2] + [2**i for i in range(3, levels)]


SCALE = 1.0 / math.sqrt(DH)
POWER = SCALE * math.log2(math.e)


def near_kernel(
    levels, me_ref, bounds_ref, q_ref, k_ref, v_ref, ga_ref, far4_ref, grown_ref, gp_ref, stat_ref, bias_ref
):
    tokens = q_ref.shape[0]
    rows = tokens // STEP
    near = tokens + rows
    bias_ref[...] = mask_bias(me_ref[0], bounds_ref, tokens, distances(levels))
    for h in range(q_ref.shape[1] // DH):
        cols = slice(h * DH, (h + 1) * DH)
        k = jnp.concatenate([k_ref[:, cols], far4_ref[:rows, cols]], 0)
        v = jnp.concatenate([v_ref[:, cols], far4_ref[rows:, cols]], 0)
        scores = nt(k, q_ref[:, cols]) + bias_ref[:near]
        top = jnp.max(scores, axis=0, keepdims=True)
        grown = jnp.exp2((scores - top) * POWER)
        grad_prob = nt(v, ga_ref[:, cols])
        grown_ref[h] = grown
        gp_ref[h] = grad_prob
        stat_ref[h, 0:1] = top
        stat_ref[h, 1:2] = jnp.sum(grown, axis=0, keepdims=True)
        stat_ref[h, 2:3] = jnp.sum(grown * grad_prob, axis=0, keepdims=True)


def attention_near(me, bounds, q, k, v, ga, far4, levels):
    tokens, width = q.shape
    heads, rows = width // DH, tokens // STEP
    near, count = tokens + rows, tokens + levels * rows
    early = jax.ShapeDtypeStruct((heads, near, tokens), F32)
    return pl.pallas_call(
        functools.partial(near_kernel, levels),
        in_specs=[SMEM_BLOCK, SMEM_BLOCK] + [VMEM_BLOCK] * 5,
        out_specs=[VMEM_BLOCK] * 4,
        out_shape=[
            early,
            early,
            jax.ShapeDtypeStruct((heads, 8, tokens), F32),
            jax.ShapeDtypeStruct((count, tokens), F32),
        ],
        compiler_params=params(),
        cost_estimate=pl.CostEstimate(
            flops=4 * tokens * near * width, bytes_accessed=16 * tokens * width, transcendentals=0
        ),
        name="attention_near",
    )(me, bounds, q, k, v, ga, far4)


def far_kernel(levels, *refs):
    core_ref, q_ref, ga_ref, grown_ref, gp_ref, stat_ref, bias_ref = refs[:7]
    arrived_refs = refs[7 : 6 + levels]
    w_ref, u_ref, use_ref, far_ref = refs[6 + levels : 10 + levels]
    gfar_refs = refs[10 + levels :]
    tokens = q_ref.shape[0]
    rows = tokens // STEP
    near = tokens + rows
    first = core_ref[0] == 0
    for h in range(q_ref.shape[1] // DH):
        cols = slice(h * DH, (h + 1) * DH)
        q, ga = q_ref[:, cols], ga_ref[:, cols]
        far = sort_arrived(first, *[r[:, cols] for r in arrived_refs])
        k = jnp.concatenate([f[:rows] for f in far], 0)
        v = jnp.concatenate([f[rows:] for f in far], 0)
        far_ref[0, :, cols] = k
        far_ref[1, :, cols] = v
        scores = nt(k, q) + bias_ref[near:]
        early_top = stat_ref[h, 0:1]
        top = jnp.maximum(early_top, jnp.max(scores, axis=0, keepdims=True))
        shrink = jnp.exp2((early_top - top) * POWER)
        grown = jnp.exp2((scores - top) * POWER)
        grad_prob = nt(v, ga)
        total = stat_ref[h, 1:2] * shrink + jnp.sum(grown, axis=0, keepdims=True)
        weighted = stat_ref[h, 2:3] * shrink + jnp.sum(grown * grad_prob, axis=0, keepdims=True)
        part = 1.0 / total
        delta = weighted * part
        early_part = shrink * part
        use_ref[h, 0:1] = early_part
        use_ref[h, 1:2] = delta
        prob = jnp.concatenate([grown_ref[h, tokens:] * early_part, grown * part], 0)
        grad_prob = jnp.concatenate([gp_ref[h, tokens:], grad_prob], 0)
        weights = prob.astype(BF16)
        grad_scores = (prob * (grad_prob - delta)).astype(BF16)
        w_ref[h] = weights
        u_ref[h] = grad_scores
        gk = (nn(grad_scores, q) * SCALE).astype(BF16)
        gv = nn(weights, ga).astype(BF16)
        g4, g1, g2, g8, *more = [
            jnp.concatenate([g[i * rows : (i + 1) * rows] for g in (gk, gv)], 0) for i in range(levels)
        ]
        out = [g4, jnp.where(first, g8, g1), jnp.where(first, g1, g2), jnp.where(first, g2, g8)]
        for ref, block in zip(gfar_refs, out + more):
            ref[:, cols] = block


def attention_far(core, q, ga, grown, grad_prob, stats, bias, arrived):
    tokens, width = q.shape
    levels = 1 + len(arrived)
    heads, rows = width // DH, tokens // STEP
    prob = jax.ShapeDtypeStruct((heads, levels * rows, tokens), BF16)
    return pl.pallas_call(
        functools.partial(far_kernel, levels),
        in_specs=[SMEM_BLOCK] + [VMEM_BLOCK] * (6 + len(arrived)),
        out_specs=[VMEM_BLOCK] * (4 + levels),
        out_shape=[
            prob,
            prob,
            jax.ShapeDtypeStruct(stats.shape, F32),
            jax.ShapeDtypeStruct((2, (levels - 1) * rows, width), BF16),
        ]
        + [jax.ShapeDtypeStruct((2 * rows, width), BF16)] * levels,
        compiler_params=params(),
        cost_estimate=pl.CostEstimate(
            flops=8 * tokens * levels * rows * width, bytes_accessed=16 * tokens * width, transcendentals=0
        ),
        name="attention_far",
    )(core, q, ga, grown, grad_prob, stats, bias, *arrived)


def local_kernel(
    q_ref, k_ref, v_ref, ga_ref, far4_ref, far_ref, grown_ref, gp_ref, use_ref, w_ref, u_ref,
    attn_ref, gq_ref, gk_ref, gv_ref,
):
    tokens = q_ref.shape[0]
    rows = tokens // STEP
    for h in range(q_ref.shape[1] // DH):
        cols = slice(h * DH, (h + 1) * DH)
        k = jnp.concatenate([k_ref[:, cols], far4_ref[:rows, cols], far_ref[0, :, cols]], 0)
        v = jnp.concatenate([v_ref[:, cols], far4_ref[rows:, cols], far_ref[1, :, cols]], 0)
        prob = grown_ref[h, :tokens] * use_ref[h, 0:1]
        near_weights = prob.astype(BF16)
        near_scores = (prob * (gp_ref[h, :tokens] - use_ref[h, 1:2])).astype(BF16)
        weights = jnp.concatenate([near_weights, w_ref[h]], 0)
        grad_scores = jnp.concatenate([near_scores, u_ref[h]], 0)
        attn_ref[:, cols] = tn(weights, v).astype(BF16)
        gq_ref[:, cols] = (tn(grad_scores, k) * SCALE).astype(BF16)
        gk_ref[:, cols] = nn(near_scores, q_ref[:, cols]) * SCALE
        gv_ref[:, cols] = nn(near_weights, ga_ref[:, cols])


def attention_local(q, *operands):
    tokens, width = q.shape
    bf = jax.ShapeDtypeStruct((tokens, width), BF16)
    f32 = jax.ShapeDtypeStruct((tokens, width), F32)
    return pl.pallas_call(
        local_kernel,
        in_specs=[VMEM_BLOCK] * (1 + len(operands)),
        out_specs=[VMEM_BLOCK] * 4,
        out_shape=[bf, bf, f32, f32],
        compiler_params=params(),
        cost_estimate=pl.CostEstimate(
            flops=12 * tokens * tokens * width, bytes_accessed=16 * tokens * width, transcendentals=0
        ),
        name="attention_local",
    )(q, *operands)


def lends_own(index):
    return index % 4 != 3, index % 4 < 2


def settle_kernel(me_ref, core_ref, gk_ref, gv_ref, four_ref, one_ref, two_ref, three_ref, *out_refs):
    tokens = gk_ref.shape[0]
    rows = tokens // STEP
    first = core_ref[0] == 0
    own1, own2 = lends_own(me_ref[0])
    back1 = jnp.where(first, two_ref[...], one_ref[...])
    back2 = jnp.where(first, three_ref[...], two_ref[...])
    back1 = jnp.where(own1, back1, jnp.zeros_like(back1))
    back2 = jnp.where(own2, back2, jnp.zeros_like(back2))
    back = (four_ref[...], back1, back2)
    at = lax.broadcasted_iota(jnp.int32, (tokens, rows), 0)
    spot = (at == lax.broadcasted_iota(jnp.int32, (tokens, rows), 1) * STEP).astype(BF16)
    spot = jnp.concatenate([spot] * len(back), 1)
    for i, (near_ref, out_ref) in enumerate(zip((gk_ref, gv_ref), out_refs)):
        extra = nn(spot, jnp.concatenate([b[i * rows : (i + 1) * rows] for b in back], 0))
        out_ref[...] = (near_ref[...] + extra).astype(BF16)


def settle(me, core, gk, gv, back4, one, two, three):
    out = jax.ShapeDtypeStruct(gk.shape, BF16)
    return pl.pallas_call(
        settle_kernel,
        in_specs=[SMEM_BLOCK] * 2 + [VMEM_BLOCK] * 6,
        out_specs=[VMEM_BLOCK] * 2,
        out_shape=[out, out],
        compiler_params=params(),
        name="settle",
    )(me, core, gk, gv, back4, one, two, three)


def add(*blocks):
    total = blocks[0].astype(F32)
    for block in blocks[1:]:
        total = total + block.astype(F32)
    return total.astype(BF16)


def per_device(queries, keys, values, out_weight, cotangent, bounds):
    n = lax.axis_size("ctx")
    levels = n.bit_length() - 1
    me = lax.axis_index("ctx").astype(jnp.int32).reshape(1)
    core = lax.axis_index("head").astype(jnp.int32).reshape(1)

    other_cot = swap(cotangent)
    picked = pick(keys, values)
    far4 = lax.ppermute(picked, "ctx", hop(4, n))
    ga, picked = grad_attn(core, cotangent, other_cot, picked, out_weight)

    first = lax.axis_index("head") == 0
    own1, own2 = lends_own(lax.axis_index("ctx"))
    lent1, lent2 = jnp.where(own1, picked, far4), jnp.where(own2, picked, far4)
    hops, ones, twos = hop(4, n), steps(n), pairs(n)
    two = mixed(jnp.where(first, far4, lent1), (hops, ones))
    three = mixed(jnp.where(first, lent1, lent2), (ones, twos))
    four = mixed(jnp.where(first, lent2, far4), (twos, hops))
    arrived = [two, three, four]
    farther = jnp.where(first, two, four) if levels > 4 else None
    for i in range(4, levels):
        farther = lax.ppermute(farther, "ctx", hop(2 ** (i - 1), n))
        arrived.append(farther)

    grown, grad_prob, stats, bias = attention_near(me, bounds, queries, keys, values, ga, far4, levels)
    weights, grad_scores, use, far, g4, two, three, four, *more = attention_far(
        core, queries, ga, grown, grad_prob, stats, bias, arrived
    )
    for i in reversed(range(len(more))):
        back = lax.ppermute(more[i], "ctx", hop(-(2 ** (i + 3)), n))
        if i > 0:
            more[i - 1] = add(more[i - 1], back)
        else:
            two = jnp.where(first, add(two, back), two)
            four = jnp.where(first, four, add(four, back))
    hops, ones, twos = hop(-4, n), turned(ones), turned(twos)
    two = mixed(two, (hops, ones))
    three = mixed(three, (ones, twos))
    four = mixed(four, (twos, hops))
    attn, gq, gk, gv = attention_local(
        queries, keys, values, ga, far4, far, grown, grad_prob, use, weights, grad_scores
    )
    back1, back2 = jnp.where(first, three, two), jnp.where(first, four, three)
    back8 = jnp.where(first, two, four)
    zero = jnp.zeros_like(back1)
    g4 = add(g4, back8, jnp.where(own1, zero, back1), jnp.where(own2, zero, back2))
    back4 = lax.ppermute(g4, "ctx", hop(-4, n))
    other_attn = swap(attn)
    output = project(core, attn, other_attn, out_weight)
    gk, gv = settle(me, core, gk, gv, back4, two, three, four)
    return output, gq, gk, gv


def solution(mesh):
    shared = P("ctx", "head")
    return jax.shard_map(
        per_device,
        mesh=mesh,
        in_specs=(shared, shared, shared, P(), shared, P()),
        out_specs=(shared,) * 4,
        check_vma=False,
    )
```

```python
import functools
import math

import jax
import jax.numpy as jnp
from jax import lax
from jax.experimental import pallas as pl
from jax.experimental.pallas import tpu as pltpu
from jax.sharding import PartitionSpec as P

DH = 128
STEP = 4
BF16 = jnp.bfloat16
F32 = jnp.float32
HBM_BLOCK = pl.BlockSpec(memory_space=pltpu.HBM)
VMEM_BLOCK = pl.BlockSpec(memory_space=pltpu.VMEM)
SMEM_BLOCK = pl.BlockSpec(memory_space=pltpu.SMEM)


def hop(distance, n):
    return [(i, i + distance) for i in range(n) if 0 <= i + distance < n]


def pairs(n):
    return [(i, i ^ 2) for i in range(n)]


def steps(n):
    return [(i, i - 3 if i % 4 == 3 else i + 1) for i in range(n)]


def neighbours(n):
    return [(i, i ^ 1) for i in range(n)]


def turned(route):
    return [(b, a) for a, b in route]


def mixed(block, route_of_core):
    cores = len(route_of_core)
    route = [(a * cores + c, b * cores + c) for c, r in enumerate(route_of_core) for a, b in r]
    return lax.ppermute(block, ("ctx", "head"), route)


def swap(block):
    return lax.ppermute(block, "head", [(0, 1), (1, 0)])


def nt(a, b):
    return lax.dot_general(a, b, (((1,), (1,)), ((), ())), preferred_element_type=F32)


def tn(a, b):
    return lax.dot_general(a, b, (((0,), (0,)), ((), ())), preferred_element_type=F32)


def nn(a, b):
    return jnp.dot(a, b, preferred_element_type=F32)


def params(mib=24):
    return pltpu.CompilerParams(vmem_limit_bytes=int(mib * 1024 * 1024))


def pick_kernel(k_hbm, v_hbm, out_ref, held, sems):
    tokens = k_hbm.shape[0]
    rows = tokens // STEP
    copies = [pltpu.make_async_copy(x, held.at[i], sems.at[i]) for i, x in enumerate((k_hbm, v_hbm))]
    for copy in copies:
        copy.start()
    at = lax.broadcasted_iota(jnp.int32, (rows, tokens), 0) * STEP
    choose = (at == lax.broadcasted_iota(jnp.int32, (rows, tokens), 1)).astype(BF16)
    for i, copy in enumerate(copies):
        copy.wait()
        out_ref[i * rows : (i + 1) * rows] = nn(choose, held[i]).astype(BF16)


def pick(keys, values):
    tokens, width = keys.shape
    return pl.pallas_call(
        pick_kernel,
        in_specs=[HBM_BLOCK, HBM_BLOCK],
        out_shape=jax.ShapeDtypeStruct((2 * tokens // STEP, width), BF16),
        scratch_shapes=[pltpu.VMEM((2, tokens, width), BF16), pltpu.SemaphoreType.DMA((2,))],
        compiler_params=params(63.5),
        name="pick",
    )(keys, values)


def grad_attn_kernel(core_ref, own_ref, other_ref, picked_ref, w_ref, out_ref, handed_ref):
    width = own_ref.shape[1]
    tile = 256
    core = core_ref[0]
    handed_ref[...] = picked_ref[...]
    own, other = own_ref[...], other_ref[...]
    cot = jnp.concatenate([jnp.where(core == 0, own, other), jnp.where(core == 0, other, own)], 1)
    for i in range(width // tile):
        rows = pl.ds(pl.multiple_of(core * width + i * tile, tile), tile)
        out_ref[:, i * tile : (i + 1) * tile] = nt(cot, w_ref[rows, :]).astype(BF16)


def grad_attn(core, own, other, picked, weight):
    tokens, width = own.shape
    return pl.pallas_call(
        grad_attn_kernel,
        in_specs=[SMEM_BLOCK] + [VMEM_BLOCK] * 4,
        out_specs=[VMEM_BLOCK] * 2,
        out_shape=[
            jax.ShapeDtypeStruct((tokens, width), BF16),
            jax.ShapeDtypeStruct(picked.shape, BF16),
        ],
        compiler_params=params(),
        cost_estimate=pl.CostEstimate(
            flops=4 * tokens * width * width, bytes_accessed=6 * width * width, transcendentals=0
        ),
        name="grad_attn",
    )(core, own, other, picked, weight)


def project_kernel(core_ref, own_ref, other_ref, w_ref, out_ref):
    width = own_ref.shape[1]
    tile = 256
    core = core_ref[0]
    own, other = own_ref[...], other_ref[...]
    heads = jnp.concatenate([jnp.where(core == 0, own, other), jnp.where(core == 0, other, own)], 1)
    for i in range(width // tile):
        columns = pl.ds(pl.multiple_of(core * width + i * tile, tile), tile)
        out_ref[:, i * tile : (i + 1) * tile] = nn(heads, w_ref[:, columns]).astype(BF16)


def project(core, own, other, weight):
    tokens, width = own.shape
    return pl.pallas_call(
        project_kernel,
        in_specs=[SMEM_BLOCK] + [VMEM_BLOCK] * 3,
        out_specs=VMEM_BLOCK,
        out_shape=jax.ShapeDtypeStruct((tokens, width), BF16),
        compiler_params=params(),
        cost_estimate=pl.CostEstimate(
            flops=4 * tokens * width * width, bytes_accessed=6 * width * width, transcendentals=0
        ),
        name="project",
    )(core, own, other, weight)


def documents(positions, bounds_ref):
    count = jnp.zeros(positions.shape, jnp.int32)
    for i in range(bounds_ref.shape[0]):
        count = count + (bounds_ref[i] <= positions).astype(jnp.int32)
    return count


def mask_bias(me, bounds_ref, tokens, order):
    rows = tokens // STEP
    own = lax.broadcasted_iota(jnp.int32, (1, tokens), 1) + me * tokens
    parts = [lax.broadcasted_iota(jnp.int32, (tokens, 1), 0) + me * tokens]
    for distance in order:
        at = lax.broadcasted_iota(jnp.int32, (rows, 1), 0) * STEP
        parts.append(at + (me - distance) * tokens)
    keys = jnp.concatenate(parts, 0)
    key_doc = jnp.where(keys >= 0, documents(keys, bounds_ref), -1)
    ok = (documents(own, bounds_ref) == key_doc) & (keys <= own)
    return jnp.where(ok, 0.0, -jnp.inf).astype(F32)


def sort_arrived(first, two, three, four, *more):
    return [jnp.where(first, three, four), jnp.where(first, four, two), jnp.where(first, two, three), *more]


def distances(levels):
    return [4, 1, 2] + [2**i for i in range(3, levels)]


SCALE = 1.0 / math.sqrt(DH)
POWER = SCALE * math.log2(math.e)


def near_kernel(
    levels, me_ref, bounds_ref, q_ref, k_ref, v_ref, ga_ref, far4_ref, grown_ref, gp_ref, stat_ref, bias_ref
):
    tokens = q_ref.shape[0]
    rows = tokens // STEP
    near = tokens + rows
    bias_ref[...] = mask_bias(me_ref[0], bounds_ref, tokens, distances(levels))
    for h in range(q_ref.shape[1] // DH):
        cols = slice(h * DH, (h + 1) * DH)
        k = jnp.concatenate([k_ref[:, cols], far4_ref[:rows, cols]], 0)
        v = jnp.concatenate([v_ref[:, cols], far4_ref[rows:, cols]], 0)
        scores = nt(k, q_ref[:, cols]) + bias_ref[:near]
        top = jnp.max(scores, axis=0, keepdims=True)
        grown = jnp.exp2((scores - top) * POWER)
        grad_prob = nt(v, ga_ref[:, cols])
        grown_ref[h] = grown
        gp_ref[h] = grad_prob
        stat_ref[h, 0:1] = top
        stat_ref[h, 1:2] = jnp.sum(grown, axis=0, keepdims=True)
        stat_ref[h, 2:3] = jnp.sum(grown * grad_prob, axis=0, keepdims=True)


def attention_near(me, bounds, q, k, v, ga, far4, levels):
    tokens, width = q.shape
    heads, rows = width // DH, tokens // STEP
    near, count = tokens + rows, tokens + levels * rows
    early = jax.ShapeDtypeStruct((heads, near, tokens), F32)
    return pl.pallas_call(
        functools.partial(near_kernel, levels),
        in_specs=[SMEM_BLOCK, SMEM_BLOCK] + [VMEM_BLOCK] * 5,
        out_specs=[VMEM_BLOCK] * 4,
        out_shape=[
            early,
            early,
            jax.ShapeDtypeStruct((heads, 8, tokens), F32),
            jax.ShapeDtypeStruct((count, tokens), F32),
        ],
        compiler_params=params(),
        cost_estimate=pl.CostEstimate(
            flops=4 * tokens * near * width, bytes_accessed=16 * tokens * width, transcendentals=0
        ),
        name="attention_near",
    )(me, bounds, q, k, v, ga, far4)


def far_kernel(levels, *refs):
    core_ref, q_ref, ga_ref, grown_ref, gp_ref, stat_ref, bias_ref = refs[:7]
    arrived_refs = refs[7 : 6 + levels]
    w_ref, u_ref, use_ref, far_ref = refs[6 + levels : 10 + levels]
    gfar_refs = refs[10 + levels :]
    tokens = q_ref.shape[0]
    rows = tokens // STEP
    near = tokens + rows
    first = core_ref[0] == 0
    for h in range(q_ref.shape[1] // DH):
        cols = slice(h * DH, (h + 1) * DH)
        q, ga = q_ref[:, cols], ga_ref[:, cols]
        far = sort_arrived(first, *[r[:, cols] for r in arrived_refs])
        k = jnp.concatenate([f[:rows] for f in far], 0)
        v = jnp.concatenate([f[rows:] for f in far], 0)
        far_ref[0, :, cols] = k
        far_ref[1, :, cols] = v
        scores = nt(k, q) + bias_ref[near:]
        early_top = stat_ref[h, 0:1]
        top = jnp.maximum(early_top, jnp.max(scores, axis=0, keepdims=True))
        shrink = jnp.exp2((early_top - top) * POWER)
        grown = jnp.exp2((scores - top) * POWER)
        grad_prob = nt(v, ga)
        total = stat_ref[h, 1:2] * shrink + jnp.sum(grown, axis=0, keepdims=True)
        weighted = stat_ref[h, 2:3] * shrink + jnp.sum(grown * grad_prob, axis=0, keepdims=True)
        part = 1.0 / total
        delta = weighted * part
        early_part = shrink * part
        use_ref[h, 0:1] = early_part
        use_ref[h, 1:2] = delta
        prob = jnp.concatenate([grown_ref[h, tokens:] * early_part, grown * part], 0)
        grad_prob = jnp.concatenate([gp_ref[h, tokens:], grad_prob], 0)
        weights = prob.astype(BF16)
        grad_scores = (prob * (grad_prob - delta)).astype(BF16)
        w_ref[h] = weights
        u_ref[h] = grad_scores
        gk = (nn(grad_scores, q) * SCALE).astype(BF16)
        gv = nn(weights, ga).astype(BF16)
        g4, g1, g2, g8, *more = [
            jnp.concatenate([g[i * rows : (i + 1) * rows] for g in (gk, gv)], 0) for i in range(levels)
        ]
        out = [g4, jnp.where(first, g2, g1), jnp.where(first, g1, g8), jnp.where(first, g8, g2)]
        for ref, block in zip(gfar_refs, out + more):
            ref[:, cols] = block


def attention_far(core, q, ga, grown, grad_prob, stats, bias, arrived):
    tokens, width = q.shape
    levels = 1 + len(arrived)
    heads, rows = width // DH, tokens // STEP
    prob = jax.ShapeDtypeStruct((heads, levels * rows, tokens), BF16)
    return pl.pallas_call(
        functools.partial(far_kernel, levels),
        in_specs=[SMEM_BLOCK] + [VMEM_BLOCK] * (6 + len(arrived)),
        out_specs=[VMEM_BLOCK] * (4 + levels),
        out_shape=[
            prob,
            prob,
            jax.ShapeDtypeStruct(stats.shape, F32),
            jax.ShapeDtypeStruct((2, (levels - 1) * rows, width), BF16),
        ]
        + [jax.ShapeDtypeStruct((2 * rows, width), BF16)] * levels,
        compiler_params=params(),
        cost_estimate=pl.CostEstimate(
            flops=8 * tokens * levels * rows * width, bytes_accessed=16 * tokens * width, transcendentals=0
        ),
        name="attention_far",
    )(core, q, ga, grown, grad_prob, stats, bias, *arrived)


def local_kernel(
    q_ref, k_ref, v_ref, ga_ref, far4_ref, far_ref, grown_ref, gp_ref, use_ref, w_ref, u_ref,
    attn_ref, gq_ref, gk_ref, gv_ref,
):
    tokens = q_ref.shape[0]
    rows = tokens // STEP
    for h in range(q_ref.shape[1] // DH):
        cols = slice(h * DH, (h + 1) * DH)
        k = jnp.concatenate([k_ref[:, cols], far4_ref[:rows, cols], far_ref[0, :, cols]], 0)
        v = jnp.concatenate([v_ref[:, cols], far4_ref[rows:, cols], far_ref[1, :, cols]], 0)
        prob = grown_ref[h, :tokens] * use_ref[h, 0:1]
        near_weights = prob.astype(BF16)
        near_scores = (prob * (gp_ref[h, :tokens] - use_ref[h, 1:2])).astype(BF16)
        weights = jnp.concatenate([near_weights, w_ref[h]], 0)
        grad_scores = jnp.concatenate([near_scores, u_ref[h]], 0)
        attn_ref[:, cols] = tn(weights, v).astype(BF16)
        gq_ref[:, cols] = (tn(grad_scores, k) * SCALE).astype(BF16)
        gk_ref[:, cols] = nn(near_scores, q_ref[:, cols]) * SCALE
        gv_ref[:, cols] = nn(near_weights, ga_ref[:, cols])


def attention_local(q, *operands):
    tokens, width = q.shape
    bf = jax.ShapeDtypeStruct((tokens, width), BF16)
    f32 = jax.ShapeDtypeStruct((tokens, width), F32)
    return pl.pallas_call(
        local_kernel,
        in_specs=[VMEM_BLOCK] * (1 + len(operands)),
        out_specs=[VMEM_BLOCK] * 4,
        out_shape=[bf, bf, f32, f32],
        compiler_params=params(),
        cost_estimate=pl.CostEstimate(
            flops=12 * tokens * tokens * width, bytes_accessed=16 * tokens * width, transcendentals=0
        ),
        name="attention_local",
    )(q, *operands)


def lends_own(index):
    return index % 4 != 3, index % 4 < 2


def returns_own(index, first):
    own1, own2 = lends_own(index)
    rest = jnp.logical_not(first)
    return (first & own2) | (rest & (index % 2 == 0)), first & own1, rest & own2


def returns_lent(index, first):
    own1, own2 = lends_own(index)
    rest = jnp.logical_not(first)
    return first & jnp.logical_not(own2), rest | jnp.logical_not(own1), first | jnp.logical_not(own2)


def settle_kernel(me_ref, core_ref, gk_ref, gv_ref, last_ref, one_ref, two_ref, three_ref, *out_refs):
    tokens = gk_ref.shape[0]
    rows = tokens // STEP
    back = [last_ref[...]]
    for ref, own in zip((one_ref, two_ref, three_ref), returns_own(me_ref[0], core_ref[0] == 0)):
        block = ref[...]
        back.append(jnp.where(own, block, jnp.zeros_like(block)))
    at = lax.broadcasted_iota(jnp.int32, (tokens, rows), 0)
    spot = (at == lax.broadcasted_iota(jnp.int32, (tokens, rows), 1) * STEP).astype(BF16)
    spot = jnp.concatenate([spot] * len(back), 1)
    for i, (near_ref, out_ref) in enumerate(zip((gk_ref, gv_ref), out_refs)):
        extra = nn(spot, jnp.concatenate([b[i * rows : (i + 1) * rows] for b in back], 0))
        out_ref[...] = (near_ref[...] + extra).astype(BF16)


def settle(me, core, gk, gv, last, one, two, three):
    out = jax.ShapeDtypeStruct(gk.shape, BF16)
    return pl.pallas_call(
        settle_kernel,
        in_specs=[SMEM_BLOCK] * 2 + [VMEM_BLOCK] * 6,
        out_specs=[VMEM_BLOCK] * 2,
        out_shape=[out, out],
        compiler_params=params(),
        name="settle",
    )(me, core, gk, gv, last, one, two, three)


def add(*blocks):
    total = blocks[0].astype(F32)
    for block in blocks[1:]:
        total = total + block.astype(F32)
    return total.astype(BF16)


def per_device(queries, keys, values, out_weight, cotangent, bounds):
    n = lax.axis_size("ctx")
    levels = n.bit_length() - 1
    me = lax.axis_index("ctx").astype(jnp.int32).reshape(1)
    core = lax.axis_index("head").astype(jnp.int32).reshape(1)

    other_cot = swap(cotangent)
    picked = pick(keys, values)
    far4 = lax.ppermute(picked, "ctx", hop(4, n))
    ga, picked = grad_attn(core, cotangent, other_cot, picked, out_weight)

    index, first = lax.axis_index("ctx"), lax.axis_index("head") == 0
    own1, own2 = lends_own(index)
    even = index % 2 == 0
    lent1, lent2 = jnp.where(own1, picked, far4), jnp.where(own2, picked, far4)
    hops, ones, twos, nexts = hop(4, n), steps(n), pairs(n), neighbours(n)
    two, three = lax.optimization_barrier(
        (jnp.where(first, far4, lent2), jnp.where(first, lent1, far4))
    )
    two = mixed(two, (hops, twos))
    three = mixed(three, (ones, hops))
    four = mixed(jnp.where(first, lent2, jnp.where(even, picked, two)), (twos, nexts))
    arrived = [two, three, four]
    farther = jnp.where(first, two, three) if levels > 4 else None
    for i in range(4, levels):
        farther = lax.ppermute(farther, "ctx", hop(2 ** (i - 1), n))
        arrived.append(farther)

    grown, grad_prob, stats, bias = attention_near(me, bounds, queries, keys, values, ga, far4, levels)
    weights, grad_scores, use, far, g4, two, three, four, *more = attention_far(
        core, queries, ga, grown, grad_prob, stats, bias, arrived
    )
    for i in reversed(range(len(more))):
        back = lax.ppermute(more[i], "ctx", hop(-(2 ** (i + 3)), n))
        if i > 0:
            more[i - 1] = add(more[i - 1], back)
        else:
            three = jnp.where(first, three, add(three, back))
            four = jnp.where(first, add(four, back), four)
    hops, ones, twos = hop(-4, n), turned(ones), turned(twos)
    one = mixed(two, (twos, nexts))
    two = mixed(three, (ones, hops))
    zero = jnp.zeros_like(one)
    three = mixed(add(four, jnp.where(first | even, zero, one)), (hops, twos))
    attn, gq, gk, gv = attention_local(
        queries, keys, values, ga, far4, far, grown, grad_prob, use, weights, grad_scores
    )
    back = (one, two, three)
    lent = [jnp.where(w, b, zero) for w, b in zip(returns_lent(index, first), back)]
    last = lax.ppermute(add(g4, *lent), "ctx", hop(-4, n))
    other_attn = swap(attn)
    output = project(core, attn, other_attn, out_weight)
    gk, gv = settle(me, core, gk, gv, last, *back)
    return output, gq, gk, gv


def solution(mesh):
    shared = P("ctx", "head")
    return jax.shard_map(
        per_device,
        mesh=mesh,
        in_specs=(shared, shared, shared, P(), shared, P()),
        out_specs=(shared,) * 4,
        check_vma=False,
    )
```

```python
import functools
import math

import jax
import jax.numpy as jnp
from jax import lax
from jax.experimental import pallas as pl
from jax.experimental.pallas import tpu as pltpu
from jax.sharding import PartitionSpec as P

DH = 128
STEP = 4
BF16 = jnp.bfloat16
F32 = jnp.float32
HBM_BLOCK = pl.BlockSpec(memory_space=pltpu.HBM)
VMEM_BLOCK = pl.BlockSpec(memory_space=pltpu.VMEM)
SMEM_BLOCK = pl.BlockSpec(memory_space=pltpu.SMEM)


def hop(distance, n):
    return [(i, i + distance) for i in range(n) if 0 <= i + distance < n]


def pairs(n):
    return [(i, i ^ 2) for i in range(n)]


def steps(n):
    return [(i, i - 3 if i % 4 == 3 else i + 1) for i in range(n)]


def neighbours(n):
    return [(i, i ^ 1) for i in range(n)]


def turned(route):
    return [(b, a) for a, b in route]


def mixed(block, route_of_core):
    cores = len(route_of_core)
    route = [(a * cores + c, b * cores + c) for c, r in enumerate(route_of_core) for a, b in r]
    return lax.ppermute(block, ("ctx", "head"), route)


def swap(block):
    return lax.ppermute(block, "head", [(0, 1), (1, 0)])


def nt(a, b):
    return lax.dot_general(a, b, (((1,), (1,)), ((), ())), preferred_element_type=F32)


def tn(a, b):
    return lax.dot_general(a, b, (((0,), (0,)), ((), ())), preferred_element_type=F32)


def nn(a, b):
    return jnp.dot(a, b, preferred_element_type=F32)


def params(mib=24):
    return pltpu.CompilerParams(vmem_limit_bytes=int(mib * 1024 * 1024))


def pick_kernel(k_hbm, v_hbm, out_ref, held, sems):
    tokens = k_hbm.shape[0]
    rows = tokens // STEP
    copies = [pltpu.make_async_copy(x, held.at[i], sems.at[i]) for i, x in enumerate((k_hbm, v_hbm))]
    for copy in copies:
        copy.start()
    at = lax.broadcasted_iota(jnp.int32, (rows, tokens), 0) * STEP
    choose = (at == lax.broadcasted_iota(jnp.int32, (rows, tokens), 1)).astype(BF16)
    for i, copy in enumerate(copies):
        copy.wait()
        out_ref[i * rows : (i + 1) * rows] = nn(choose, held[i]).astype(BF16)


def pick(keys, values):
    tokens, width = keys.shape
    return pl.pallas_call(
        pick_kernel,
        in_specs=[HBM_BLOCK, HBM_BLOCK],
        out_shape=jax.ShapeDtypeStruct((2 * tokens // STEP, width), BF16),
        scratch_shapes=[pltpu.VMEM((2, tokens, width), BF16), pltpu.SemaphoreType.DMA((2,))],
        compiler_params=params(63.5),
        name="pick",
    )(keys, values)


def grad_attn_kernel(
    core_ref, own_hbm, other_hbm, picked_ref, w_hbm, out_ref, handed_ref, cot, held, cot_sems, sems
):
    pieces, tile, _ = held.shape
    width = own_hbm.shape[1]
    core = core_ref[0]
    copies = []
    for source, at, i in ((own_hbm, core, 0), (other_hbm, 1 - core, 1)):
        columns = pl.ds(pl.multiple_of(at * width, width), width)
        copies.append(pltpu.make_async_copy(source, cot.at[:, columns], cot_sems.at[i]))
    for i in range(pieces):
        rows = w_hbm.at[pl.ds((core * pieces + i) * tile, tile), :]
        copies.append(pltpu.make_async_copy(rows, held.at[i], sems.at[i]))
    for copy in copies:
        copy.start()
    handed_ref[...] = picked_ref[...]
    copies[0].wait()
    copies[1].wait()
    for i in range(pieces):
        copies[2 + i].wait()
        out_ref[:, i * tile : (i + 1) * tile] = nt(cot[...], held[i]).astype(BF16)


def grad_attn(core, own, other, picked, weight):
    tokens, width = own.shape
    pieces = 4
    return pl.pallas_call(
        grad_attn_kernel,
        in_specs=[SMEM_BLOCK, HBM_BLOCK, HBM_BLOCK, VMEM_BLOCK, HBM_BLOCK],
        out_specs=[VMEM_BLOCK] * 2,
        out_shape=[
            jax.ShapeDtypeStruct((tokens, width), BF16),
            jax.ShapeDtypeStruct(picked.shape, BF16),
        ],
        scratch_shapes=[
            pltpu.VMEM((tokens, weight.shape[1]), BF16),
            pltpu.VMEM((pieces, width // pieces, weight.shape[1]), BF16),
            pltpu.SemaphoreType.DMA((2,)),
            pltpu.SemaphoreType.DMA((pieces,)),
        ],
        compiler_params=params(57),
        cost_estimate=pl.CostEstimate(
            flops=4 * tokens * width * width, bytes_accessed=6 * width * width, transcendentals=0
        ),
        name="grad_attn",
    )(core, own, other, picked, weight)


def project_kernel(core_ref, own_ref, other_ref, w_hbm, out_ref, held, sems):
    pieces, tile, width = held.shape
    core = core_ref[0]
    columns = pl.ds(pl.multiple_of(core * width, width), width)
    copies = []
    for i in range(pieces):
        part = w_hbm.at[pl.ds(i * tile, tile), columns]
        copies.append(pltpu.make_async_copy(part, held.at[i], sems.at[i]))
        copies[i].start()
    own, other = own_ref[...], other_ref[...]
    whole = jnp.concatenate([jnp.where(core == 0, own, other), jnp.where(core == 0, other, own)], 1)
    total = None
    for i in range(pieces):
        copies[i].wait()
        term = nn(whole[:, i * tile : (i + 1) * tile], held[i])
        total = term if total is None else total + term
    out_ref[...] = total.astype(BF16)


def project(core, own, other, weight):
    tokens, width = own.shape
    pieces = 4
    return pl.pallas_call(
        project_kernel,
        in_specs=[SMEM_BLOCK, VMEM_BLOCK, VMEM_BLOCK, HBM_BLOCK],
        out_specs=VMEM_BLOCK,
        out_shape=jax.ShapeDtypeStruct((tokens, width), BF16),
        scratch_shapes=[
            pltpu.VMEM((pieces, weight.shape[0] // pieces, width), BF16),
            pltpu.SemaphoreType.DMA((pieces,)),
        ],
        compiler_params=params(57),
        cost_estimate=pl.CostEstimate(
            flops=4 * tokens * width * width, bytes_accessed=6 * width * width, transcendentals=0
        ),
        name="project",
    )(core, own, other, weight)


def documents(positions, bounds_ref):
    count = jnp.zeros(positions.shape, jnp.int32)
    for i in range(bounds_ref.shape[0]):
        count = count + (bounds_ref[i] <= positions).astype(jnp.int32)
    return count


def mask_bias(me, bounds_ref, tokens, order):
    rows = tokens // STEP
    own = lax.broadcasted_iota(jnp.int32, (1, tokens), 1) + me * tokens
    parts = [lax.broadcasted_iota(jnp.int32, (tokens, 1), 0) + me * tokens]
    for distance in order:
        at = lax.broadcasted_iota(jnp.int32, (rows, 1), 0) * STEP
        parts.append(at + (me - distance) * tokens)
    keys = jnp.concatenate(parts, 0)
    key_doc = jnp.where(keys >= 0, documents(keys, bounds_ref), -1)
    ok = (documents(own, bounds_ref) == key_doc) & (keys <= own)
    return jnp.where(ok, 0.0, -jnp.inf).astype(F32)


def sort_arrived(first, two, three, four, *more):
    return [jnp.where(first, three, four), jnp.where(first, four, two), jnp.where(first, two, three), *more]


def distances(levels):
    return [4, 1, 2] + [2**i for i in range(3, levels)]


SCALE = 1.0 / math.sqrt(DH)
POWER = SCALE * math.log2(math.e)


def near_kernel(
    levels, me_ref, bounds_ref, q_ref, k_ref, v_ref, ga_ref, far4_ref, grown_ref, gp_ref, stat_ref, bias_ref
):
    tokens = q_ref.shape[0]
    rows = tokens // STEP
    near = tokens + rows
    bias_ref[...] = mask_bias(me_ref[0], bounds_ref, tokens, distances(levels))
    for h in range(q_ref.shape[1] // DH):
        cols = slice(h * DH, (h + 1) * DH)
        k = jnp.concatenate([k_ref[:, cols], far4_ref[:rows, cols]], 0)
        v = jnp.concatenate([v_ref[:, cols], far4_ref[rows:, cols]], 0)
        scores = nt(k, q_ref[:, cols]) + bias_ref[:near]
        top = jnp.max(scores, axis=0, keepdims=True)
        grown = jnp.exp2((scores - top) * POWER)
        grad_prob = nt(v, ga_ref[:, cols])
        grown_ref[h] = grown
        gp_ref[h] = grad_prob
        stat_ref[h, 0:1] = top
        stat_ref[h, 1:2] = jnp.sum(grown, axis=0, keepdims=True)
        stat_ref[h, 2:3] = jnp.sum(grown * grad_prob, axis=0, keepdims=True)


def attention_near(me, bounds, q, k, v, ga, far4, levels):
    tokens, width = q.shape
    heads, rows = width // DH, tokens // STEP
    near, count = tokens + rows, tokens + levels * rows
    early = jax.ShapeDtypeStruct((heads, near, tokens), F32)
    return pl.pallas_call(
        functools.partial(near_kernel, levels),
        in_specs=[SMEM_BLOCK, SMEM_BLOCK] + [VMEM_BLOCK] * 5,
        out_specs=[VMEM_BLOCK] * 4,
        out_shape=[
            early,
            early,
            jax.ShapeDtypeStruct((heads, 8, tokens), F32),
            jax.ShapeDtypeStruct((count, tokens), F32),
        ],
        compiler_params=params(),
        cost_estimate=pl.CostEstimate(
            flops=4 * tokens * near * width, bytes_accessed=16 * tokens * width, transcendentals=0
        ),
        name="attention_near",
    )(me, bounds, q, k, v, ga, far4)


def far_kernel(levels, *refs):
    core_ref, q_ref, ga_ref, grown_ref, gp_ref, stat_ref, bias_ref = refs[:7]
    arrived_refs = refs[7 : 6 + levels]
    w_ref, u_ref, use_ref, far_ref = refs[6 + levels : 10 + levels]
    gfar_refs = refs[10 + levels :]
    tokens = q_ref.shape[0]
    rows = tokens // STEP
    near = tokens + rows
    first = core_ref[0] == 0
    for h in range(q_ref.shape[1] // DH):
        cols = slice(h * DH, (h + 1) * DH)
        q, ga = q_ref[:, cols], ga_ref[:, cols]
        far = sort_arrived(first, *[r[:, cols] for r in arrived_refs])
        k = jnp.concatenate([f[:rows] for f in far], 0)
        v = jnp.concatenate([f[rows:] for f in far], 0)
        far_ref[0, :, cols] = k
        far_ref[1, :, cols] = v
        scores = nt(k, q) + bias_ref[near:]
        early_top = stat_ref[h, 0:1]
        top = jnp.maximum(early_top, jnp.max(scores, axis=0, keepdims=True))
        shrink = jnp.exp2((early_top - top) * POWER)
        grown = jnp.exp2((scores - top) * POWER)
        grad_prob = nt(v, ga)
        total = stat_ref[h, 1:2] * shrink + jnp.sum(grown, axis=0, keepdims=True)
        weighted = stat_ref[h, 2:3] * shrink + jnp.sum(grown * grad_prob, axis=0, keepdims=True)
        part = 1.0 / total
        delta = weighted * part
        early_part = shrink * part
        use_ref[h, 0:1] = early_part
        use_ref[h, 1:2] = delta
        prob = jnp.concatenate([grown_ref[h, tokens:] * early_part, grown * part], 0)
        grad_prob = jnp.concatenate([gp_ref[h, tokens:], grad_prob], 0)
        weights = prob.astype(BF16)
        grad_scores = (prob * (grad_prob - delta)).astype(BF16)
        w_ref[h] = weights
        u_ref[h] = grad_scores
        gk = (nn(grad_scores, q) * SCALE).astype(BF16)
        gv = nn(weights, ga).astype(BF16)
        g4, g1, g2, g8, *more = [
            jnp.concatenate([g[i * rows : (i + 1) * rows] for g in (gk, gv)], 0) for i in range(levels)
        ]
        out = [g4, jnp.where(first, g2, g1), jnp.where(first, g1, g8), jnp.where(first, g8, g2)]
        for ref, block in zip(gfar_refs, out + more):
            ref[:, cols] = block


def attention_far(core, q, ga, grown, grad_prob, stats, bias, arrived):
    tokens, width = q.shape
    levels = 1 + len(arrived)
    heads, rows = width // DH, tokens // STEP
    prob = jax.ShapeDtypeStruct((heads, levels * rows, tokens), BF16)
    return pl.pallas_call(
        functools.partial(far_kernel, levels),
        in_specs=[SMEM_BLOCK] + [VMEM_BLOCK] * (6 + len(arrived)),
        out_specs=[VMEM_BLOCK] * (4 + levels),
        out_shape=[
            prob,
            prob,
            jax.ShapeDtypeStruct(stats.shape, F32),
            jax.ShapeDtypeStruct((2, (levels - 1) * rows, width), BF16),
        ]
        + [jax.ShapeDtypeStruct((2 * rows, width), BF16)] * levels,
        compiler_params=params(),
        cost_estimate=pl.CostEstimate(
            flops=8 * tokens * levels * rows * width, bytes_accessed=16 * tokens * width, transcendentals=0
        ),
        name="attention_far",
    )(core, q, ga, grown, grad_prob, stats, bias, *arrived)


def local_kernel(
    q_ref, k_ref, v_ref, ga_ref, far4_ref, far_ref, grown_ref, gp_ref, use_ref, w_ref, u_ref,
    attn_ref, gq_ref, gk_ref, gv_ref,
):
    tokens = q_ref.shape[0]
    rows = tokens // STEP
    for h in range(q_ref.shape[1] // DH):
        cols = slice(h * DH, (h + 1) * DH)
        k = jnp.concatenate([k_ref[:, cols], far4_ref[:rows, cols], far_ref[0, :, cols]], 0)
        v = jnp.concatenate([v_ref[:, cols], far4_ref[rows:, cols], far_ref[1, :, cols]], 0)
        prob = grown_ref[h, :tokens] * use_ref[h, 0:1]
        near_weights = prob.astype(BF16)
        near_scores = (prob * (gp_ref[h, :tokens] - use_ref[h, 1:2])).astype(BF16)
        weights = jnp.concatenate([near_weights, w_ref[h]], 0)
        grad_scores = jnp.concatenate([near_scores, u_ref[h]], 0)
        attn_ref[:, cols] = tn(weights, v).astype(BF16)
        gq_ref[:, cols] = (tn(grad_scores, k) * SCALE).astype(BF16)
        gk_ref[:, cols] = nn(near_scores, q_ref[:, cols]) * SCALE
        gv_ref[:, cols] = nn(near_weights, ga_ref[:, cols])


def attention_local(q, *operands):
    tokens, width = q.shape
    bf = jax.ShapeDtypeStruct((tokens, width), BF16)
    f32 = jax.ShapeDtypeStruct((tokens, width), F32)
    return pl.pallas_call(
        local_kernel,
        in_specs=[VMEM_BLOCK] * (1 + len(operands)),
        out_specs=[VMEM_BLOCK] * 4,
        out_shape=[bf, bf, f32, f32],
        compiler_params=params(),
        cost_estimate=pl.CostEstimate(
            flops=12 * tokens * tokens * width, bytes_accessed=16 * tokens * width, transcendentals=0
        ),
        name="attention_local",
    )(q, *operands)


def lends_own(index):
    return index % 4 != 3, index % 4 < 2


def returns_own(index, first):
    own1, own2 = lends_own(index)
    rest = jnp.logical_not(first)
    return (first & own2) | (rest & (index % 2 == 0)), first & own1, rest & own2


def returns_lent(index, first):
    own1, own2 = lends_own(index)
    rest = jnp.logical_not(first)
    return first & jnp.logical_not(own2), rest | jnp.logical_not(own1), first | jnp.logical_not(own2)


def settle_kernel(me_ref, core_ref, gk_ref, gv_ref, last_ref, one_ref, two_ref, three_ref, *out_refs):
    tokens = gk_ref.shape[0]
    rows = tokens // STEP
    back = [last_ref[...]]
    for ref, own in zip((one_ref, two_ref, three_ref), returns_own(me_ref[0], core_ref[0] == 0)):
        block = ref[...]
        back.append(jnp.where(own, block, jnp.zeros_like(block)))
    at = lax.broadcasted_iota(jnp.int32, (tokens, rows), 0)
    spot = (at == lax.broadcasted_iota(jnp.int32, (tokens, rows), 1) * STEP).astype(BF16)
    spot = jnp.concatenate([spot] * len(back), 1)
    for i, (near_ref, out_ref) in enumerate(zip((gk_ref, gv_ref), out_refs)):
        extra = nn(spot, jnp.concatenate([b[i * rows : (i + 1) * rows] for b in back], 0))
        out_ref[...] = (near_ref[...] + extra).astype(BF16)


def settle(me, core, gk, gv, last, one, two, three):
    out = jax.ShapeDtypeStruct(gk.shape, BF16)
    return pl.pallas_call(
        settle_kernel,
        in_specs=[SMEM_BLOCK] * 2 + [VMEM_BLOCK] * 6,
        out_specs=[VMEM_BLOCK] * 2,
        out_shape=[out, out],
        compiler_params=params(),
        name="settle",
    )(me, core, gk, gv, last, one, two, three)


def add(*blocks):
    total = blocks[0].astype(F32)
    for block in blocks[1:]:
        total = total + block.astype(F32)
    return total.astype(BF16)


def per_device(queries, keys, values, out_weight, cotangent, bounds):
    n = lax.axis_size("ctx")
    levels = n.bit_length() - 1
    me = lax.axis_index("ctx").astype(jnp.int32).reshape(1)
    core = lax.axis_index("head").astype(jnp.int32).reshape(1)

    other_cot = swap(cotangent)
    picked = pick(keys, values)
    far4 = lax.ppermute(picked, "ctx", hop(4, n))
    ga, picked = grad_attn(core, cotangent, other_cot, picked, out_weight)

    index, first = lax.axis_index("ctx"), lax.axis_index("head") == 0
    own1, own2 = lends_own(index)
    even = index % 2 == 0
    lent1, lent2 = jnp.where(own1, picked, far4), jnp.where(own2, picked, far4)
    hops, ones, twos, nexts = hop(4, n), steps(n), pairs(n), neighbours(n)
    two, three = lax.optimization_barrier(
        (jnp.where(first, far4, lent2), jnp.where(first, lent1, far4))
    )
    two = mixed(two, (hops, twos))
    three = mixed(three, (ones, hops))
    four = mixed(jnp.where(first, lent2, jnp.where(even, picked, two)), (twos, nexts))
    arrived = [two, three, four]
    farther = jnp.where(first, two, three) if levels > 4 else None
    for i in range(4, levels):
        farther = lax.ppermute(farther, "ctx", hop(2 ** (i - 1), n))
        arrived.append(farther)

    grown, grad_prob, stats, bias = attention_near(me, bounds, queries, keys, values, ga, far4, levels)
    weights, grad_scores, use, far, g4, two, three, four, *more = attention_far(
        core, queries, ga, grown, grad_prob, stats, bias, arrived
    )
    for i in reversed(range(len(more))):
        back = lax.ppermute(more[i], "ctx", hop(-(2 ** (i + 3)), n))
        if i > 0:
            more[i - 1] = add(more[i - 1], back)
        else:
            three = jnp.where(first, three, add(three, back))
            four = jnp.where(first, add(four, back), four)
    hops, ones, twos = hop(-4, n), turned(ones), turned(twos)
    one = mixed(two, (twos, nexts))
    two = mixed(three, (ones, hops))
    zero = jnp.zeros_like(one)
    three = mixed(add(four, jnp.where(first | even, zero, one)), (hops, twos))
    attn, gq, gk, gv = attention_local(
        queries, keys, values, ga, far4, far, grown, grad_prob, use, weights, grad_scores
    )
    back = (one, two, three)
    lent = [jnp.where(w, b, zero) for w, b in zip(returns_lent(index, first), back)]
    last = lax.ppermute(add(g4, *lent), "ctx", hop(-4, n))
    other_attn = swap(attn)
    output = project(core, attn, other_attn, out_weight)
    gk, gv = settle(me, core, gk, gv, last, *back)
    return output, gq, gk, gv


def solution(mesh):
    shared = P("ctx", "head")
    return jax.shard_map(
        per_device,
        mesh=mesh,
        in_specs=(shared, shared, shared, P(), shared, P()),
        out_specs=(shared,) * 4,
        check_vma=False,
    )
```

```python
import functools
import math

import jax
import jax.numpy as jnp
from jax import lax
from jax.experimental import pallas as pl
from jax.experimental.pallas import tpu as pltpu
from jax.sharding import PartitionSpec as P

DH = 128
STEP = 4
BF16 = jnp.bfloat16
F32 = jnp.float32
HBM_BLOCK = pl.BlockSpec(memory_space=pltpu.HBM)
VMEM_BLOCK = pl.BlockSpec(memory_space=pltpu.VMEM)
SMEM_BLOCK = pl.BlockSpec(memory_space=pltpu.SMEM)


def hop(distance, n):
    return [(i, i + distance) for i in range(n) if 0 <= i + distance < n]


def pairs(n):
    return [(i, i ^ 2) for i in range(n)]


def steps(n):
    return [(i, i - 3 if i % 4 == 3 else i + 1) for i in range(n)]


def neighbours(n):
    return [(i, i ^ 1) for i in range(n)]


def turned(route):
    return [(b, a) for a, b in route]


def mixed(block, route_of_core):
    cores = len(route_of_core)
    route = [(a * cores + c, b * cores + c) for c, r in enumerate(route_of_core) for a, b in r]
    return lax.ppermute(block, ("ctx", "head"), route)


def swap(block):
    return lax.ppermute(block, "head", [(0, 1), (1, 0)])


def nt(a, b):
    return lax.dot_general(a, b, (((1,), (1,)), ((), ())), preferred_element_type=F32)


def tn(a, b):
    return lax.dot_general(a, b, (((0,), (0,)), ((), ())), preferred_element_type=F32)


def nn(a, b):
    return jnp.dot(a, b, preferred_element_type=F32)


def params(mib=24):
    return pltpu.CompilerParams(vmem_limit_bytes=int(mib * 1024 * 1024))


def pick_kernel(k_hbm, v_hbm, out_ref, held, sems):
    tokens = k_hbm.shape[0]
    rows = tokens // STEP
    copies = [pltpu.make_async_copy(x, held.at[i], sems.at[i]) for i, x in enumerate((k_hbm, v_hbm))]
    for copy in copies:
        copy.start()
    at = lax.broadcasted_iota(jnp.int32, (rows, tokens), 0) * STEP
    choose = (at == lax.broadcasted_iota(jnp.int32, (rows, tokens), 1)).astype(BF16)
    for i, copy in enumerate(copies):
        copy.wait()
        out_ref[i * rows : (i + 1) * rows] = nn(choose, held[i]).astype(BF16)


def pick(keys, values):
    tokens, width = keys.shape
    return pl.pallas_call(
        pick_kernel,
        in_specs=[HBM_BLOCK, HBM_BLOCK],
        out_shape=jax.ShapeDtypeStruct((2 * tokens // STEP, width), BF16),
        scratch_shapes=[pltpu.VMEM((2, tokens, width), BF16), pltpu.SemaphoreType.DMA((2,))],
        compiler_params=params(63.5),
        name="pick",
    )(keys, values)


def grad_attn_kernel(
    core_ref, own_hbm, other_hbm, picked_ref, w_hbm, out_ref, handed_ref, cot, held, cot_sems, sems
):
    pieces, tile, _ = held.shape
    width = own_hbm.shape[1]
    core = core_ref[0]
    copies = []
    for source, at, i in ((own_hbm, core, 0), (other_hbm, 1 - core, 1)):
        columns = pl.ds(pl.multiple_of(at * width, width), width)
        copies.append(pltpu.make_async_copy(source, cot.at[:, columns], cot_sems.at[i]))
    for i in range(pieces):
        rows = w_hbm.at[pl.ds((core * pieces + i) * tile, tile), :]
        copies.append(pltpu.make_async_copy(rows, held.at[i], sems.at[i]))
    for copy in copies:
        copy.start()
    handed_ref[...] = picked_ref[...]
    copies[0].wait()
    copies[1].wait()
    for i in range(pieces):
        copies[2 + i].wait()
        out_ref[:, i * tile : (i + 1) * tile] = nt(cot[...], held[i]).astype(BF16)


def grad_attn(core, own, other, picked, weight):
    tokens, width = own.shape
    pieces = 4
    return pl.pallas_call(
        grad_attn_kernel,
        in_specs=[SMEM_BLOCK, HBM_BLOCK, HBM_BLOCK, VMEM_BLOCK, HBM_BLOCK],
        out_specs=[VMEM_BLOCK] * 2,
        out_shape=[
            jax.ShapeDtypeStruct((tokens, width), BF16),
            jax.ShapeDtypeStruct(picked.shape, BF16),
        ],
        scratch_shapes=[
            pltpu.VMEM((tokens, weight.shape[1]), BF16),
            pltpu.VMEM((pieces, width // pieces, weight.shape[1]), BF16),
            pltpu.SemaphoreType.DMA((2,)),
            pltpu.SemaphoreType.DMA((pieces,)),
        ],
        compiler_params=params(57),
        cost_estimate=pl.CostEstimate(
            flops=4 * tokens * width * width, bytes_accessed=6 * width * width, transcendentals=0
        ),
        name="grad_attn",
    )(core, own, other, picked, weight)


def project_kernel(core_ref, own_ref, other_ref, w_hbm, out_ref, held, sems):
    pieces, tile, width = held.shape
    core = core_ref[0]
    columns = pl.ds(pl.multiple_of(core * width, width), width)
    copies = []
    for i in range(pieces):
        part = w_hbm.at[pl.ds(i * tile, tile), columns]
        copies.append(pltpu.make_async_copy(part, held.at[i], sems.at[i]))
        copies[i].start()
    own, other = own_ref[...], other_ref[...]
    whole = jnp.concatenate([jnp.where(core == 0, own, other), jnp.where(core == 0, other, own)], 1)
    total = None
    for i in range(pieces):
        copies[i].wait()
        term = nn(whole[:, i * tile : (i + 1) * tile], held[i])
        total = term if total is None else total + term
    out_ref[...] = total.astype(BF16)


def project(core, own, other, weight):
    tokens, width = own.shape
    pieces = 4
    return pl.pallas_call(
        project_kernel,
        in_specs=[SMEM_BLOCK, VMEM_BLOCK, VMEM_BLOCK, HBM_BLOCK],
        out_specs=VMEM_BLOCK,
        out_shape=jax.ShapeDtypeStruct((tokens, width), BF16),
        scratch_shapes=[
            pltpu.VMEM((pieces, weight.shape[0] // pieces, width), BF16),
            pltpu.SemaphoreType.DMA((pieces,)),
        ],
        compiler_params=params(57),
        cost_estimate=pl.CostEstimate(
            flops=4 * tokens * width * width, bytes_accessed=6 * width * width, transcendentals=0
        ),
        name="project",
    )(core, own, other, weight)


def documents(positions, bounds_ref):
    count = jnp.zeros(positions.shape, jnp.int32)
    for i in range(bounds_ref.shape[0]):
        count = count + (bounds_ref[i] <= positions).astype(jnp.int32)
    return count


def mask_bias(me, bounds_ref, tokens, order):
    rows = tokens // STEP
    own = lax.broadcasted_iota(jnp.int32, (1, tokens), 1) + me * tokens
    parts = [lax.broadcasted_iota(jnp.int32, (tokens, 1), 0) + me * tokens]
    for distance in order:
        at = lax.broadcasted_iota(jnp.int32, (rows, 1), 0) * STEP
        parts.append(at + (me - distance) * tokens)
    keys = jnp.concatenate(parts, 0)
    key_doc = jnp.where(keys >= 0, documents(keys, bounds_ref), -1)
    ok = (documents(own, bounds_ref) == key_doc) & (keys <= own)
    return jnp.where(ok, 0.0, -jnp.inf).astype(F32)


def sort_arrived(first, two, three, four, *more):
    return [jnp.where(first, three, four), jnp.where(first, four, two), jnp.where(first, two, three), *more]


def distances(levels):
    return [4, 1, 2] + [2**i for i in range(3, levels)]


SCALE = 1.0 / math.sqrt(DH)
POWER = SCALE * math.log2(math.e)


def near_kernel(
    levels, me_ref, bounds_ref, q_ref, k_ref, v_ref, ga_ref, far4_ref, grown_ref, gp_ref, stat_ref, bias_ref
):
    tokens = q_ref.shape[0]
    rows = tokens // STEP
    near = tokens + rows
    bias_ref[...] = mask_bias(me_ref[0], bounds_ref, tokens, distances(levels))
    for h in range(q_ref.shape[1] // DH):
        cols = slice(h * DH, (h + 1) * DH)
        k = jnp.concatenate([k_ref[:, cols], far4_ref[:rows, cols]], 0)
        v = jnp.concatenate([v_ref[:, cols], far4_ref[rows:, cols]], 0)
        scores = nt(k, q_ref[:, cols]) + bias_ref[:near]
        top = jnp.max(scores, axis=0, keepdims=True)
        grown = jnp.exp2((scores - top) * POWER)
        grad_prob = nt(v, ga_ref[:, cols])
        grown_ref[h] = grown
        gp_ref[h] = grad_prob
        stat_ref[h, 0:1] = top
        stat_ref[h, 1:2] = jnp.sum(grown, axis=0, keepdims=True)
        stat_ref[h, 2:3] = jnp.sum(grown * grad_prob, axis=0, keepdims=True)


def attention_near(me, bounds, q, k, v, ga, far4, levels):
    tokens, width = q.shape
    heads, rows = width // DH, tokens // STEP
    near, count = tokens + rows, tokens + levels * rows
    early = jax.ShapeDtypeStruct((heads, near, tokens), F32)
    return pl.pallas_call(
        functools.partial(near_kernel, levels),
        in_specs=[SMEM_BLOCK, SMEM_BLOCK] + [VMEM_BLOCK] * 5,
        out_specs=[VMEM_BLOCK] * 4,
        out_shape=[
            early,
            early,
            jax.ShapeDtypeStruct((heads, 8, tokens), F32),
            jax.ShapeDtypeStruct((count, tokens), F32),
        ],
        compiler_params=params(),
        cost_estimate=pl.CostEstimate(
            flops=4 * tokens * near * width, bytes_accessed=16 * tokens * width, transcendentals=0
        ),
        name="attention_near",
    )(me, bounds, q, k, v, ga, far4)


def far_kernel(levels, *refs):
    core_ref, q_ref, ga_ref, grown_ref, gp_ref, stat_ref, bias_ref = refs[:7]
    arrived_refs = refs[7 : 6 + levels]
    w_ref, u_ref, use_ref, far_ref = refs[6 + levels : 10 + levels]
    gfar_refs = refs[10 + levels :]
    tokens = q_ref.shape[0]
    rows = tokens // STEP
    near = tokens + rows
    first = core_ref[0] == 0
    for h in range(q_ref.shape[1] // DH):
        cols = slice(h * DH, (h + 1) * DH)
        q, ga = q_ref[:, cols], ga_ref[:, cols]
        far = sort_arrived(first, *[r[:, cols] for r in arrived_refs])
        k = jnp.concatenate([f[:rows] for f in far], 0)
        v = jnp.concatenate([f[rows:] for f in far], 0)
        far_ref[0, :, cols] = k
        far_ref[1, :, cols] = v
        scores = nt(k, q) + bias_ref[near:]
        early_top = stat_ref[h, 0:1]
        top = jnp.maximum(early_top, jnp.max(scores, axis=0, keepdims=True))
        shrink = jnp.exp2((early_top - top) * POWER)
        grown = jnp.exp2((scores - top) * POWER)
        grad_prob = nt(v, ga)
        total = stat_ref[h, 1:2] * shrink + jnp.sum(grown, axis=0, keepdims=True)
        weighted = stat_ref[h, 2:3] * shrink + jnp.sum(grown * grad_prob, axis=0, keepdims=True)
        part = 1.0 / total
        delta = weighted * part
        early_part = shrink * part
        use_ref[h, 0:1] = early_part
        use_ref[h, 1:2] = delta
        prob = jnp.concatenate([grown_ref[h, tokens:] * early_part, grown * part], 0)
        grad_prob = jnp.concatenate([gp_ref[h, tokens:], grad_prob], 0)
        weights = prob.astype(BF16)
        grad_scores = (prob * (grad_prob - delta)).astype(BF16)
        w_ref[h] = weights
        u_ref[h] = grad_scores
        gk = (nn(grad_scores, q) * SCALE).astype(BF16)
        gv = nn(weights, ga).astype(BF16)
        g4, g1, g2, g8, *more = [
            jnp.concatenate([g[i * rows : (i + 1) * rows] for g in (gk, gv)], 0) for i in range(levels)
        ]
        out = [g4, jnp.where(first, g2, g1), jnp.where(first, g1, g8), jnp.where(first, g8, g2)]
        for ref, block in zip(gfar_refs, out + more):
            ref[:, cols] = block


def attention_far(core, q, ga, grown, grad_prob, stats, bias, arrived):
    tokens, width = q.shape
    levels = 1 + len(arrived)
    heads, rows = width // DH, tokens // STEP
    prob = jax.ShapeDtypeStruct((heads, levels * rows, tokens), BF16)
    return pl.pallas_call(
        functools.partial(far_kernel, levels),
        in_specs=[SMEM_BLOCK] + [VMEM_BLOCK] * (6 + len(arrived)),
        out_specs=[VMEM_BLOCK] * (4 + levels),
        out_shape=[
            prob,
            prob,
            jax.ShapeDtypeStruct(stats.shape, F32),
            jax.ShapeDtypeStruct((2, (levels - 1) * rows, width), BF16),
        ]
        + [jax.ShapeDtypeStruct((2 * rows, width), BF16)] * levels,
        compiler_params=params(),
        cost_estimate=pl.CostEstimate(
            flops=8 * tokens * levels * rows * width, bytes_accessed=16 * tokens * width, transcendentals=0
        ),
        name="attention_far",
    )(core, q, ga, grown, grad_prob, stats, bias, *arrived)


def local_kernel(
    q_ref, k_ref, v_ref, ga_ref, far4_ref, far_ref, grown_ref, gp_ref, use_ref, w_ref, u_ref,
    attn_ref, gq_ref, gk_ref, gv_ref,
):
    tokens = q_ref.shape[0]
    rows = tokens // STEP
    for h in range(q_ref.shape[1] // DH):
        cols = slice(h * DH, (h + 1) * DH)
        k = jnp.concatenate([k_ref[:, cols], far4_ref[:rows, cols], far_ref[0, :, cols]], 0)
        v = jnp.concatenate([v_ref[:, cols], far4_ref[rows:, cols], far_ref[1, :, cols]], 0)
        prob = grown_ref[h, :tokens] * use_ref[h, 0:1]
        near_weights = prob.astype(BF16)
        near_scores = (prob * (gp_ref[h, :tokens] - use_ref[h, 1:2])).astype(BF16)
        weights = jnp.concatenate([near_weights, w_ref[h]], 0)
        grad_scores = jnp.concatenate([near_scores, u_ref[h]], 0)
        attn_ref[:, cols] = tn(weights, v).astype(BF16)
        gq_ref[:, cols] = (tn(grad_scores, k) * SCALE).astype(BF16)
        gk_ref[:, cols] = nn(near_scores, q_ref[:, cols]) * SCALE
        gv_ref[:, cols] = nn(near_weights, ga_ref[:, cols])


def attention_local(q, *operands):
    tokens, width = q.shape
    bf = jax.ShapeDtypeStruct((tokens, width), BF16)
    f32 = jax.ShapeDtypeStruct((tokens, width), F32)
    return pl.pallas_call(
        local_kernel,
        in_specs=[VMEM_BLOCK] * (1 + len(operands)),
        out_specs=[VMEM_BLOCK] * 4,
        out_shape=[bf, bf, f32, f32],
        compiler_params=params(),
        cost_estimate=pl.CostEstimate(
            flops=12 * tokens * tokens * width, bytes_accessed=16 * tokens * width, transcendentals=0
        ),
        name="attention_local",
    )(q, *operands)


def lends_own(index):
    return index % 4 != 3, index % 4 < 2


def returns_own(index, first):
    own1, own2 = lends_own(index)
    rest = jnp.logical_not(first)
    return (first & own2) | (rest & (index % 2 == 0)), first & own1, rest & own2


def returns_lent(index, first):
    own1, own2 = lends_own(index)
    rest = jnp.logical_not(first)
    return first & jnp.logical_not(own2), rest | jnp.logical_not(own1), first | jnp.logical_not(own2)


def choose_kernel(me_ref, core_ref, picked_ref, far4_ref, two_ref, three_ref):
    first = core_ref[0] == 0
    own1, own2 = lends_own(me_ref[0])
    picked, far4 = picked_ref[...], far4_ref[...]
    two_ref[...] = jnp.where(first, far4, jnp.where(own2, picked, far4))
    three_ref[...] = jnp.where(first, jnp.where(own1, picked, far4), far4)


def choose_last_kernel(me_ref, core_ref, picked_ref, far4_ref, two_ref, out_ref):
    first = core_ref[0] == 0
    own2 = lends_own(me_ref[0])[1]
    picked = picked_ref[...]
    ahead = jnp.where(own2, picked, far4_ref[...])
    out_ref[...] = jnp.where(first, ahead, jnp.where(me_ref[0] % 2 == 0, picked, two_ref[...]))


def include(total, block, use):
    block = block.astype(F32)
    return total + jnp.where(use, block, jnp.zeros_like(block))


def pass_on_kernel(me_ref, core_ref, own_ref, one_ref, out_ref):
    use = jnp.logical_not((core_ref[0] == 0) | (me_ref[0] % 2 == 0))
    out_ref[...] = include(own_ref[...].astype(F32), one_ref[...], use).astype(BF16)


def collect_kernel(me_ref, core_ref, own_ref, one_ref, two_ref, three_ref, out_ref):
    total = own_ref[...].astype(F32)
    uses = returns_lent(me_ref[0], core_ref[0] == 0)
    for ref, use in zip((one_ref, two_ref, three_ref), uses):
        total = include(total, ref[...], use)
    out_ref[...] = total.astype(BF16)


def small(kernel, name, count, me, core, *blocks):
    shape = jax.ShapeDtypeStruct(blocks[0].shape, BF16)
    out = pl.pallas_call(
        kernel,
        in_specs=[SMEM_BLOCK] * 2 + [VMEM_BLOCK] * len(blocks),
        out_specs=[VMEM_BLOCK] * count,
        out_shape=[shape] * count,
        compiler_params=params(8),
        name=name,
    )(me, core, *blocks)
    return out if count > 1 else out[0]


def settle_kernel(me_ref, core_ref, gk_ref, gv_ref, last_ref, one_ref, two_ref, three_ref, *out_refs):
    tokens = gk_ref.shape[0]
    rows = tokens // STEP
    back = [last_ref[...]]
    for ref, own in zip((one_ref, two_ref, three_ref), returns_own(me_ref[0], core_ref[0] == 0)):
        block = ref[...]
        back.append(jnp.where(own, block, jnp.zeros_like(block)))
    at = lax.broadcasted_iota(jnp.int32, (tokens, rows), 0)
    spot = (at == lax.broadcasted_iota(jnp.int32, (tokens, rows), 1) * STEP).astype(BF16)
    spot = jnp.concatenate([spot] * len(back), 1)
    for i, (near_ref, out_ref) in enumerate(zip((gk_ref, gv_ref), out_refs)):
        extra = nn(spot, jnp.concatenate([b[i * rows : (i + 1) * rows] for b in back], 0))
        out_ref[...] = (near_ref[...] + extra).astype(BF16)


def settle(me, core, gk, gv, last, one, two, three):
    out = jax.ShapeDtypeStruct(gk.shape, BF16)
    return pl.pallas_call(
        settle_kernel,
        in_specs=[SMEM_BLOCK] * 2 + [VMEM_BLOCK] * 6,
        out_specs=[VMEM_BLOCK] * 2,
        out_shape=[out, out],
        compiler_params=params(),
        name="settle",
    )(me, core, gk, gv, last, one, two, three)


def add(*blocks):
    total = blocks[0].astype(F32)
    for block in blocks[1:]:
        total = total + block.astype(F32)
    return total.astype(BF16)


def per_device(queries, keys, values, out_weight, cotangent, bounds):
    n = lax.axis_size("ctx")
    levels = n.bit_length() - 1
    me = lax.axis_index("ctx").astype(jnp.int32).reshape(1)
    core = lax.axis_index("head").astype(jnp.int32).reshape(1)

    other_cot = swap(cotangent)
    picked = pick(keys, values)
    far4 = lax.ppermute(picked, "ctx", hop(4, n))
    ga, picked = grad_attn(core, cotangent, other_cot, picked, out_weight)

    hops, ones, twos, nexts = hop(4, n), steps(n), pairs(n), neighbours(n)
    two, three = small(choose_kernel, "choose", 2, me, core, picked, far4)
    two = mixed(two, (hops, twos))
    three = mixed(three, (ones, hops))
    four = mixed(small(choose_last_kernel, "choose_last", 1, me, core, picked, far4, two), (twos, nexts))
    first = lax.axis_index("head") == 0 if levels > 4 else None
    arrived = [two, three, four]
    farther = jnp.where(first, two, three) if levels > 4 else None
    for i in range(4, levels):
        farther = lax.ppermute(farther, "ctx", hop(2 ** (i - 1), n))
        arrived.append(farther)

    grown, grad_prob, stats, bias = attention_near(me, bounds, queries, keys, values, ga, far4, levels)
    weights, grad_scores, use, far, g4, two, three, four, *more = attention_far(
        core, queries, ga, grown, grad_prob, stats, bias, arrived
    )
    for i in reversed(range(len(more))):
        back = lax.ppermute(more[i], "ctx", hop(-(2 ** (i + 3)), n))
        if i > 0:
            more[i - 1] = add(more[i - 1], back)
        else:
            three = jnp.where(first, three, add(three, back))
            four = jnp.where(first, add(four, back), four)
    hops, ones, twos = hop(-4, n), turned(ones), turned(twos)
    one = mixed(two, (twos, nexts))
    two = mixed(three, (ones, hops))
    three = mixed(small(pass_on_kernel, "pass_on", 1, me, core, four, one), (hops, twos))
    attn, gq, gk, gv = attention_local(
        queries, keys, values, ga, far4, far, grown, grad_prob, use, weights, grad_scores
    )
    back = (one, two, three)
    g4 = small(collect_kernel, "collect", 1, me, core, g4, *back)
    last = lax.ppermute(g4, "ctx", hop(-4, n))
    other_attn = swap(attn)
    output = project(core, attn, other_attn, out_weight)
    gk, gv = settle(me, core, gk, gv, last, *back)
    return output, gq, gk, gv


def solution(mesh):
    shared = P("ctx", "head")
    return jax.shard_map(
        per_device,
        mesh=mesh,
        in_specs=(shared, shared, shared, P(), shared, P()),
        out_specs=(shared,) * 4,
        check_vma=False,
    )
```

```python
import functools
import math

import jax
import jax.numpy as jnp
from jax import lax
from jax.experimental import pallas as pl
from jax.experimental.pallas import tpu as pltpu
from jax.sharding import PartitionSpec as P

DH = 128
STEP = 4
BF16 = jnp.bfloat16
F32 = jnp.float32
HBM_BLOCK = pl.BlockSpec(memory_space=pltpu.HBM)
VMEM_BLOCK = pl.BlockSpec(memory_space=pltpu.VMEM)
SMEM_BLOCK = pl.BlockSpec(memory_space=pltpu.SMEM)


def hop(distance, n):
    return [(i, i + distance) for i in range(n) if 0 <= i + distance < n]


def pairs(n):
    return [(i, i ^ 2) for i in range(n)]


def steps(n):
    return [(i, i - 3 if i % 4 == 3 else i + 1) for i in range(n)]


def neighbours(n):
    return [(i, i ^ 1) for i in range(n)]


def turned(route):
    return [(b, a) for a, b in route]


def mixed(block, route_of_core):
    cores = len(route_of_core)
    route = [(a * cores + c, b * cores + c) for c, r in enumerate(route_of_core) for a, b in r]
    return lax.ppermute(block, ("ctx", "head"), route)


def swap(block):
    return lax.ppermute(block, "head", [(0, 1), (1, 0)])


def nt(a, b):
    return lax.dot_general(a, b, (((1,), (1,)), ((), ())), preferred_element_type=F32)


def tn(a, b):
    return lax.dot_general(a, b, (((0,), (0,)), ((), ())), preferred_element_type=F32)


def nn(a, b):
    return jnp.dot(a, b, preferred_element_type=F32)


def params(mib=24):
    return pltpu.CompilerParams(vmem_limit_bytes=int(mib * 1024 * 1024))


def pick_kernel(k_hbm, v_hbm, out_ref, held, sems):
    tokens = k_hbm.shape[0]
    rows = tokens // STEP
    copies = [pltpu.make_async_copy(x, held.at[i], sems.at[i]) for i, x in enumerate((k_hbm, v_hbm))]
    for copy in copies:
        copy.start()
    at = lax.broadcasted_iota(jnp.int32, (rows, tokens), 0) * STEP
    choose = (at == lax.broadcasted_iota(jnp.int32, (rows, tokens), 1)).astype(BF16)
    for i, copy in enumerate(copies):
        copy.wait()
        out_ref[i * rows : (i + 1) * rows] = nn(choose, held[i]).astype(BF16)


def pick(keys, values):
    tokens, width = keys.shape
    return pl.pallas_call(
        pick_kernel,
        in_specs=[HBM_BLOCK, HBM_BLOCK],
        out_shape=jax.ShapeDtypeStruct((2 * tokens // STEP, width), BF16),
        scratch_shapes=[pltpu.VMEM((2, tokens, width), BF16), pltpu.SemaphoreType.DMA((2,))],
        compiler_params=params(63.5),
        name="pick",
    )(keys, values)


def grad_attn_kernel(
    core_ref, own_hbm, other_hbm, picked_ref, w_hbm, out_ref, handed_ref, cot, held, cot_sems, sems
):
    pieces, tile, _ = held.shape
    width = own_hbm.shape[1]
    core = core_ref[0]
    copies = []
    for source, at, i in ((own_hbm, core, 0), (other_hbm, 1 - core, 1)):
        columns = pl.ds(pl.multiple_of(at * width, width), width)
        copies.append(pltpu.make_async_copy(source, cot.at[:, columns], cot_sems.at[i]))
    for i in range(pieces):
        rows = w_hbm.at[pl.ds((core * pieces + i) * tile, tile), :]
        copies.append(pltpu.make_async_copy(rows, held.at[i], sems.at[i]))
    for copy in copies:
        copy.start()
    handed_ref[...] = picked_ref[...]
    copies[0].wait()
    copies[1].wait()
    for i in range(pieces):
        copies[2 + i].wait()
        out_ref[:, i * tile : (i + 1) * tile] = nt(cot[...], held[i]).astype(BF16)


def grad_attn(core, own, other, picked, weight):
    tokens, width = own.shape
    pieces = 4
    return pl.pallas_call(
        grad_attn_kernel,
        in_specs=[SMEM_BLOCK, HBM_BLOCK, HBM_BLOCK, VMEM_BLOCK, HBM_BLOCK],
        out_specs=[VMEM_BLOCK] * 2,
        out_shape=[
            jax.ShapeDtypeStruct((tokens, width), BF16),
            jax.ShapeDtypeStruct(picked.shape, BF16),
        ],
        scratch_shapes=[
            pltpu.VMEM((tokens, weight.shape[1]), BF16),
            pltpu.VMEM((pieces, width // pieces, weight.shape[1]), BF16),
            pltpu.SemaphoreType.DMA((2,)),
            pltpu.SemaphoreType.DMA((pieces,)),
        ],
        compiler_params=params(52),
        cost_estimate=pl.CostEstimate(
            flops=4 * tokens * width * width, bytes_accessed=6 * width * width, transcendentals=0
        ),
        name="grad_attn",
    )(core, own, other, picked, weight)


def project_kernel(core_ref, own_ref, other_ref, w_hbm, out_ref, held, sems):
    pieces, tile, width = held.shape
    core = core_ref[0]
    columns = pl.ds(pl.multiple_of(core * width, width), width)
    copies = []
    for i in range(pieces):
        part = w_hbm.at[pl.ds(i * tile, tile), columns]
        copies.append(pltpu.make_async_copy(part, held.at[i], sems.at[i]))
        copies[i].start()
    own, other = own_ref[...], other_ref[...]
    whole = jnp.concatenate([jnp.where(core == 0, own, other), jnp.where(core == 0, other, own)], 1)
    total = None
    for i in range(pieces):
        copies[i].wait()
        term = nn(whole[:, i * tile : (i + 1) * tile], held[i])
        total = term if total is None else total + term
    out_ref[...] = total.astype(BF16)


def project(core, own, other, weight):
    tokens, width = own.shape
    pieces = 4
    return pl.pallas_call(
        project_kernel,
        in_specs=[SMEM_BLOCK, VMEM_BLOCK, VMEM_BLOCK, HBM_BLOCK],
        out_specs=VMEM_BLOCK,
        out_shape=jax.ShapeDtypeStruct((tokens, width), BF16),
        scratch_shapes=[
            pltpu.VMEM((pieces, weight.shape[0] // pieces, width), BF16),
            pltpu.SemaphoreType.DMA((pieces,)),
        ],
        compiler_params=params(52),
        cost_estimate=pl.CostEstimate(
            flops=4 * tokens * width * width, bytes_accessed=6 * width * width, transcendentals=0
        ),
        name="project",
    )(core, own, other, weight)


def documents(positions, bounds_ref):
    count = jnp.zeros(positions.shape, jnp.int32)
    for i in range(bounds_ref.shape[0]):
        count = count + (bounds_ref[i] <= positions).astype(jnp.int32)
    return count


def mask_bias(me, bounds_ref, tokens, order):
    rows = tokens // STEP
    own = lax.broadcasted_iota(jnp.int32, (1, tokens), 1) + me * tokens
    parts = [lax.broadcasted_iota(jnp.int32, (tokens, 1), 0) + me * tokens]
    for distance in order:
        at = lax.broadcasted_iota(jnp.int32, (rows, 1), 0) * STEP
        parts.append(at + (me - distance) * tokens)
    keys = jnp.concatenate(parts, 0)
    key_doc = jnp.where(keys >= 0, documents(keys, bounds_ref), -1)
    ok = (documents(own, bounds_ref) == key_doc) & (keys <= own)
    return jnp.where(ok, 0.0, -jnp.inf).astype(F32)


def sort_arrived(first, two, three, four, *more):
    return [jnp.where(first, three, four), jnp.where(first, four, two), jnp.where(first, two, three), *more]


def distances(levels):
    return [4, 1, 2] + [2**i for i in range(3, levels)]


SCALE = 1.0 / math.sqrt(DH)
POWER = SCALE * math.log2(math.e)


def near_kernel(
    levels, me_ref, bounds_ref, q_ref, k_ref, v_ref, ga_ref, far4_ref, grown_ref, gp_ref, stat_ref, bias_ref
):
    tokens = q_ref.shape[0]
    rows = tokens // STEP
    near = tokens + rows
    bias_ref[...] = mask_bias(me_ref[0], bounds_ref, tokens, distances(levels))
    for h in range(q_ref.shape[1] // DH):
        cols = slice(h * DH, (h + 1) * DH)
        k = jnp.concatenate([k_ref[:, cols], far4_ref[:rows, cols]], 0)
        v = jnp.concatenate([v_ref[:, cols], far4_ref[rows:, cols]], 0)
        scores = nt(k, q_ref[:, cols]) + bias_ref[:near]
        top = jnp.max(scores, axis=0, keepdims=True)
        grown = jnp.exp2((scores - top) * POWER)
        grad_prob = nt(v, ga_ref[:, cols])
        grown_ref[h] = grown
        gp_ref[h] = grad_prob
        stat_ref[h, 0:1] = top
        stat_ref[h, 1:2] = jnp.sum(grown, axis=0, keepdims=True)
        stat_ref[h, 2:3] = jnp.sum(grown * grad_prob, axis=0, keepdims=True)


def attention_near(me, bounds, q, k, v, ga, far4, levels):
    tokens, width = q.shape
    heads, rows = width // DH, tokens // STEP
    near, count = tokens + rows, tokens + levels * rows
    early = jax.ShapeDtypeStruct((heads, near, tokens), F32)
    return pl.pallas_call(
        functools.partial(near_kernel, levels),
        in_specs=[SMEM_BLOCK, SMEM_BLOCK] + [VMEM_BLOCK] * 5,
        out_specs=[VMEM_BLOCK] * 4,
        out_shape=[
            early,
            early,
            jax.ShapeDtypeStruct((heads, 8, tokens), F32),
            jax.ShapeDtypeStruct((count, tokens), F32),
        ],
        compiler_params=params(),
        cost_estimate=pl.CostEstimate(
            flops=4 * tokens * near * width, bytes_accessed=16 * tokens * width, transcendentals=0
        ),
        name="attention_near",
    )(me, bounds, q, k, v, ga, far4)


def far_kernel(levels, *refs):
    me_ref, core_ref, q_ref, ga_ref, grown_ref, gp_ref, stat_ref, bias_ref = refs[:8]
    arrived_refs = refs[8 : 7 + levels]
    w_ref, u_ref, use_ref, far_ref, pass_ref = refs[7 + levels : 12 + levels]
    gfar_refs = refs[12 + levels :]
    tokens = q_ref.shape[0]
    rows = tokens // STEP
    near = tokens + rows
    first = core_ref[0] == 0
    passes = (core_ref[0] * (me_ref[0] % 2)).astype(F32)
    pass_ref[...] = jnp.full(pass_ref.shape, passes, F32)
    for h in range(q_ref.shape[1] // DH):
        cols = slice(h * DH, (h + 1) * DH)
        q, ga = q_ref[:, cols], ga_ref[:, cols]
        far = sort_arrived(first, *[r[:, cols] for r in arrived_refs])
        k = jnp.concatenate([f[:rows] for f in far], 0)
        v = jnp.concatenate([f[rows:] for f in far], 0)
        far_ref[0, :, cols] = k
        far_ref[1, :, cols] = v
        scores = nt(k, q) + bias_ref[near:]
        early_top = stat_ref[h, 0:1]
        top = jnp.maximum(early_top, jnp.max(scores, axis=0, keepdims=True))
        shrink = jnp.exp2((early_top - top) * POWER)
        grown = jnp.exp2((scores - top) * POWER)
        grad_prob = nt(v, ga)
        total = stat_ref[h, 1:2] * shrink + jnp.sum(grown, axis=0, keepdims=True)
        weighted = stat_ref[h, 2:3] * shrink + jnp.sum(grown * grad_prob, axis=0, keepdims=True)
        part = 1.0 / total
        delta = weighted * part
        early_part = shrink * part
        use_ref[h, 0:1] = early_part
        use_ref[h, 1:2] = delta
        prob = jnp.concatenate([grown_ref[h, tokens:] * early_part, grown * part], 0)
        grad_prob = jnp.concatenate([gp_ref[h, tokens:], grad_prob], 0)
        weights = prob.astype(BF16)
        grad_scores = (prob * (grad_prob - delta)).astype(BF16)
        w_ref[h] = weights
        u_ref[h] = grad_scores
        gk = (nn(grad_scores, q) * SCALE).astype(BF16)
        gv = nn(weights, ga).astype(BF16)
        g4, g1, g2, g8, *more = [
            jnp.concatenate([g[i * rows : (i + 1) * rows] for g in (gk, gv)], 0) for i in range(levels)
        ]
        out = [g4, jnp.where(first, g2, g1), jnp.where(first, g1, g8), jnp.where(first, g8, g2)]
        for ref, block in zip(gfar_refs, out + more):
            ref[:, cols] = block


def attention_far(me, core, q, ga, grown, grad_prob, stats, bias, arrived):
    tokens, width = q.shape
    levels = 1 + len(arrived)
    heads, rows = width // DH, tokens // STEP
    prob = jax.ShapeDtypeStruct((heads, levels * rows, tokens), BF16)
    return pl.pallas_call(
        functools.partial(far_kernel, levels),
        in_specs=[SMEM_BLOCK] * 2 + [VMEM_BLOCK] * (6 + len(arrived)),
        out_specs=[VMEM_BLOCK] * (5 + levels),
        out_shape=[
            prob,
            prob,
            jax.ShapeDtypeStruct(stats.shape, F32),
            jax.ShapeDtypeStruct((2, (levels - 1) * rows, width), BF16),
            jax.ShapeDtypeStruct((1, width), F32),
        ]
        + [jax.ShapeDtypeStruct((2 * rows, width), BF16)] * levels,
        compiler_params=params(),
        cost_estimate=pl.CostEstimate(
            flops=8 * tokens * levels * rows * width, bytes_accessed=16 * tokens * width, transcendentals=0
        ),
        name="attention_far",
    )(me, core, q, ga, grown, grad_prob, stats, bias, *arrived)


def local_kernel(
    q_ref, k_ref, v_ref, ga_ref, far4_ref, far_ref, grown_ref, gp_ref, use_ref, w_ref, u_ref,
    attn_ref, gq_ref, gk_ref, gv_ref,
):
    tokens = q_ref.shape[0]
    rows = tokens // STEP
    for h in range(q_ref.shape[1] // DH):
        cols = slice(h * DH, (h + 1) * DH)
        k = jnp.concatenate([k_ref[:, cols], far4_ref[:rows, cols], far_ref[0, :, cols]], 0)
        v = jnp.concatenate([v_ref[:, cols], far4_ref[rows:, cols], far_ref[1, :, cols]], 0)
        prob = grown_ref[h, :tokens] * use_ref[h, 0:1]
        near_weights = prob.astype(BF16)
        near_scores = (prob * (gp_ref[h, :tokens] - use_ref[h, 1:2])).astype(BF16)
        weights = jnp.concatenate([near_weights, w_ref[h]], 0)
        grad_scores = jnp.concatenate([near_scores, u_ref[h]], 0)
        attn_ref[:, cols] = tn(weights, v).astype(BF16)
        gq_ref[:, cols] = (tn(grad_scores, k) * SCALE).astype(BF16)
        gk_ref[:, cols] = nn(near_scores, q_ref[:, cols]) * SCALE
        gv_ref[:, cols] = nn(near_weights, ga_ref[:, cols])


def attention_local(q, *operands):
    tokens, width = q.shape
    bf = jax.ShapeDtypeStruct((tokens, width), BF16)
    f32 = jax.ShapeDtypeStruct((tokens, width), F32)
    return pl.pallas_call(
        local_kernel,
        in_specs=[VMEM_BLOCK] * (1 + len(operands)),
        out_specs=[VMEM_BLOCK] * 4,
        out_shape=[bf, bf, f32, f32],
        compiler_params=params(),
        cost_estimate=pl.CostEstimate(
            flops=12 * tokens * tokens * width, bytes_accessed=16 * tokens * width, transcendentals=0
        ),
        name="attention_local",
    )(q, *operands)


def lends_own(index):
    return index % 4 != 3, index % 4 < 2


def returns_own(index, first):
    own1, own2 = lends_own(index)
    rest = jnp.logical_not(first)
    return (first & own2) | (rest & (index % 2 == 0)), first & own1, rest & own2


def returns_lent(index, first):
    own1, own2 = lends_own(index)
    rest = jnp.logical_not(first)
    return first & jnp.logical_not(own2), rest | jnp.logical_not(own1), first | jnp.logical_not(own2)


def choose_kernel(me_ref, core_ref, picked_ref, far4_ref, two_ref, three_ref):
    first = core_ref[0] == 0
    own1, own2 = lends_own(me_ref[0])
    picked, far4 = picked_ref[...], far4_ref[...]
    two_ref[...] = jnp.where(first, far4, jnp.where(own2, picked, far4))
    three_ref[...] = jnp.where(first, jnp.where(own1, picked, far4), far4)


def choose_last_kernel(me_ref, core_ref, picked_ref, far4_ref, two_ref, out_ref):
    first = core_ref[0] == 0
    own2 = lends_own(me_ref[0])[1]
    picked = picked_ref[...]
    ahead = jnp.where(own2, picked, far4_ref[...])
    out_ref[...] = jnp.where(first, ahead, jnp.where(me_ref[0] % 2 == 0, picked, two_ref[...]))


def include(total, block, use):
    block = block.astype(F32)
    return total + jnp.where(use, block, jnp.zeros_like(block))


def collect_kernel(me_ref, core_ref, own_ref, one_ref, two_ref, three_ref, out_ref):
    total = own_ref[...].astype(F32)
    uses = returns_lent(me_ref[0], core_ref[0] == 0)
    for ref, use in zip((one_ref, two_ref, three_ref), uses):
        total = include(total, ref[...], use)
    out_ref[...] = total.astype(BF16)


def small(kernel, name, count, me, core, *blocks):
    shape = jax.ShapeDtypeStruct(blocks[0].shape, BF16)
    out = pl.pallas_call(
        kernel,
        in_specs=[SMEM_BLOCK] * 2 + [VMEM_BLOCK] * len(blocks),
        out_specs=[VMEM_BLOCK] * count,
        out_shape=[shape] * count,
        compiler_params=params(8),
        cost_estimate=pl.CostEstimate(
            flops=blocks[0].size, bytes_accessed=2 * blocks[0].size, transcendentals=0
        ),
        name=name,
    )(me, core, *blocks)
    return out if count > 1 else out[0]


def settle_kernel(me_ref, core_ref, gk_ref, gv_ref, last_ref, one_ref, two_ref, three_ref, *out_refs):
    tokens = gk_ref.shape[0]
    rows = tokens // STEP
    back = [last_ref[...]]
    for ref, own in zip((one_ref, two_ref, three_ref), returns_own(me_ref[0], core_ref[0] == 0)):
        block = ref[...]
        back.append(jnp.where(own, block, jnp.zeros_like(block)))
    at = lax.broadcasted_iota(jnp.int32, (tokens, rows), 0)
    spot = (at == lax.broadcasted_iota(jnp.int32, (tokens, rows), 1) * STEP).astype(BF16)
    spot = jnp.concatenate([spot] * len(back), 1)
    for i, (near_ref, out_ref) in enumerate(zip((gk_ref, gv_ref), out_refs)):
        extra = nn(spot, jnp.concatenate([b[i * rows : (i + 1) * rows] for b in back], 0))
        out_ref[...] = (near_ref[...] + extra).astype(BF16)


def settle(me, core, gk, gv, last, one, two, three):
    out = jax.ShapeDtypeStruct(gk.shape, BF16)
    return pl.pallas_call(
        settle_kernel,
        in_specs=[SMEM_BLOCK] * 2 + [VMEM_BLOCK] * 6,
        out_specs=[VMEM_BLOCK] * 2,
        out_shape=[out, out],
        compiler_params=params(),
        name="settle",
    )(me, core, gk, gv, last, one, two, three)


def add(*blocks):
    total = blocks[0].astype(F32)
    for block in blocks[1:]:
        total = total + block.astype(F32)
    return total.astype(BF16)


def per_device(queries, keys, values, out_weight, cotangent, bounds):
    n = lax.axis_size("ctx")
    levels = n.bit_length() - 1
    me = lax.axis_index("ctx").astype(jnp.int32).reshape(1)
    core = lax.axis_index("head").astype(jnp.int32).reshape(1)

    other_cot = swap(cotangent)
    picked = pick(keys, values)
    far4 = lax.ppermute(picked, "ctx", hop(4, n))
    ga, picked = grad_attn(core, cotangent, other_cot, picked, out_weight)

    hops, ones, twos, nexts = hop(4, n), steps(n), pairs(n), neighbours(n)
    two, three = small(choose_kernel, "choose", 2, me, core, picked, far4)
    two = mixed(two, (hops, twos))
    three = mixed(three, (ones, hops))
    four = mixed(small(choose_last_kernel, "choose_last", 1, me, core, picked, far4, two), (twos, nexts))
    first = lax.axis_index("head") == 0 if levels > 4 else None
    arrived = [two, three, four]
    farther = jnp.where(first, two, three) if levels > 4 else None
    for i in range(4, levels):
        farther = lax.ppermute(farther, "ctx", hop(2 ** (i - 1), n))
        arrived.append(farther)

    grown, grad_prob, stats, bias = attention_near(me, bounds, queries, keys, values, ga, far4, levels)
    weights, grad_scores, use, far, passes, g4, two, three, four, *more = attention_far(
        me, core, queries, ga, grown, grad_prob, stats, bias, arrived
    )
    for i in reversed(range(len(more))):
        back = lax.ppermute(more[i], "ctx", hop(-(2 ** (i + 3)), n))
        if i > 0:
            more[i - 1] = add(more[i - 1], back)
        else:
            three = jnp.where(first, three, add(three, back))
            four = jnp.where(first, add(four, back), four)
    hops, ones, twos = hop(-4, n), turned(ones), turned(twos)
    one = mixed(two, (twos, nexts))
    two = mixed(three, (ones, hops))
    three = mixed((four.astype(F32) + one.astype(F32) * passes).astype(BF16), (hops, twos))
    attn, gq, gk, gv = attention_local(
        queries, keys, values, ga, far4, far, grown, grad_prob, use, weights, grad_scores
    )
    back = (one, two, three)
    g4 = small(collect_kernel, "collect", 1, me, core, g4, *back)
    last = lax.ppermute(g4, "ctx", hop(-4, n))
    other_attn = swap(attn)
    output = project(core, attn, other_attn, out_weight)
    gk, gv = settle(me, core, gk, gv, last, *back)
    return output, gq, gk, gv


def solution(mesh):
    shared = P("ctx", "head")
    return jax.shard_map(
        per_device,
        mesh=mesh,
        in_specs=(shared, shared, shared, P(), shared, P()),
        out_specs=(shared,) * 4,
        check_vma=False,
    )
```

```python
import functools
import math

import jax
import jax.numpy as jnp
from jax import lax
from jax.experimental import pallas as pl
from jax.experimental.pallas import tpu as pltpu
from jax.sharding import PartitionSpec as P

DH = 128
STEP = 4
BF16 = jnp.bfloat16
F32 = jnp.float32
HBM_BLOCK = pl.BlockSpec(memory_space=pltpu.HBM)
VMEM_BLOCK = pl.BlockSpec(memory_space=pltpu.VMEM)
SMEM_BLOCK = pl.BlockSpec(memory_space=pltpu.SMEM)


def hop(distance, n):
    return [(i, i + distance) for i in range(n) if 0 <= i + distance < n]


def pairs(n):
    return [(i, i ^ 2) for i in range(n)]


def steps(n):
    return [(i, i - 3 if i % 4 == 3 else i + 1) for i in range(n)]


def neighbours(n):
    return [(i, i ^ 1) for i in range(n)]


def turned(route):
    return [(b, a) for a, b in route]


def mixed(block, route_of_core):
    cores = len(route_of_core)
    route = [(a * cores + c, b * cores + c) for c, r in enumerate(route_of_core) for a, b in r]
    return lax.ppermute(block, ("ctx", "head"), route)


def swap(block):
    return lax.ppermute(block, "head", [(0, 1), (1, 0)])


def nt(a, b):
    return lax.dot_general(a, b, (((1,), (1,)), ((), ())), preferred_element_type=F32)


def tn(a, b):
    return lax.dot_general(a, b, (((0,), (0,)), ((), ())), preferred_element_type=F32)


def nn(a, b):
    return jnp.dot(a, b, preferred_element_type=F32)


def params(mib=24):
    return pltpu.CompilerParams(vmem_limit_bytes=int(mib * 1024 * 1024))


def pick_kernel(k_hbm, v_hbm, out_ref, held, sems):
    tokens = k_hbm.shape[0]
    rows = tokens // STEP
    copies = [pltpu.make_async_copy(x, held.at[i], sems.at[i]) for i, x in enumerate((k_hbm, v_hbm))]
    for copy in copies:
        copy.start()
    at = lax.broadcasted_iota(jnp.int32, (rows, tokens), 0) * STEP
    choose = (at == lax.broadcasted_iota(jnp.int32, (rows, tokens), 1)).astype(BF16)
    for i, copy in enumerate(copies):
        copy.wait()
        out_ref[i * rows : (i + 1) * rows] = nn(choose, held[i]).astype(BF16)


def pick(keys, values):
    tokens, width = keys.shape
    return pl.pallas_call(
        pick_kernel,
        in_specs=[HBM_BLOCK, HBM_BLOCK],
        out_shape=jax.ShapeDtypeStruct((2 * tokens // STEP, width), BF16),
        scratch_shapes=[pltpu.VMEM((2, tokens, width), BF16), pltpu.SemaphoreType.DMA((2,))],
        compiler_params=params(63.5),
        name="pick",
    )(keys, values)


def grad_attn_kernel(
    core_ref, own_hbm, other_hbm, picked_ref, w_hbm, out_ref, handed_ref, cot, held, cot_sems, sems
):
    pieces, tile, _ = held.shape
    width = own_hbm.shape[1]
    core = core_ref[0]
    copies = []
    for source, at, i in ((own_hbm, core, 0), (other_hbm, 1 - core, 1)):
        columns = pl.ds(pl.multiple_of(at * width, width), width)
        copies.append(pltpu.make_async_copy(source, cot.at[:, columns], cot_sems.at[i]))
    for i in range(pieces):
        rows = w_hbm.at[pl.ds((core * pieces + i) * tile, tile), :]
        copies.append(pltpu.make_async_copy(rows, held.at[i], sems.at[i]))
    for copy in copies:
        copy.start()
    handed_ref[...] = picked_ref[...]
    copies[0].wait()
    copies[1].wait()
    for i in range(pieces):
        copies[2 + i].wait()
        out_ref[:, i * tile : (i + 1) * tile] = nt(cot[...], held[i]).astype(BF16)


def grad_attn(core, own, other, picked, weight):
    tokens, width = own.shape
    pieces = 4
    return pl.pallas_call(
        grad_attn_kernel,
        in_specs=[SMEM_BLOCK, HBM_BLOCK, HBM_BLOCK, VMEM_BLOCK, HBM_BLOCK],
        out_specs=[VMEM_BLOCK] * 2,
        out_shape=[
            jax.ShapeDtypeStruct((tokens, width), BF16),
            jax.ShapeDtypeStruct(picked.shape, BF16),
        ],
        scratch_shapes=[
            pltpu.VMEM((tokens, weight.shape[1]), BF16),
            pltpu.VMEM((pieces, width // pieces, weight.shape[1]), BF16),
            pltpu.SemaphoreType.DMA((2,)),
            pltpu.SemaphoreType.DMA((pieces,)),
        ],
        compiler_params=params(52),
        cost_estimate=pl.CostEstimate(
            flops=4 * tokens * width * width, bytes_accessed=6 * width * width, transcendentals=0
        ),
        name="grad_attn",
    )(core, own, other, picked, weight)


def project_kernel(core_ref, own_ref, other_ref, w_hbm, out_ref, held, sems):
    pieces, tile, width = held.shape
    core = core_ref[0]
    columns = pl.ds(pl.multiple_of(core * width, width), width)
    copies = []
    for i in range(pieces):
        part = w_hbm.at[pl.ds(i * tile, tile), columns]
        copies.append(pltpu.make_async_copy(part, held.at[i], sems.at[i]))
        copies[i].start()
    own, other = own_ref[...], other_ref[...]
    whole = jnp.concatenate([jnp.where(core == 0, own, other), jnp.where(core == 0, other, own)], 1)
    total = None
    for i in range(pieces):
        copies[i].wait()
        term = nn(whole[:, i * tile : (i + 1) * tile], held[i])
        total = term if total is None else total + term
    out_ref[...] = total.astype(BF16)


def project(core, own, other, weight):
    tokens, width = own.shape
    pieces = 4
    return pl.pallas_call(
        project_kernel,
        in_specs=[SMEM_BLOCK, VMEM_BLOCK, VMEM_BLOCK, HBM_BLOCK],
        out_specs=VMEM_BLOCK,
        out_shape=jax.ShapeDtypeStruct((tokens, width), BF16),
        scratch_shapes=[
            pltpu.VMEM((pieces, weight.shape[0] // pieces, width), BF16),
            pltpu.SemaphoreType.DMA((pieces,)),
        ],
        compiler_params=params(52),
        cost_estimate=pl.CostEstimate(
            flops=4 * tokens * width * width, bytes_accessed=6 * width * width, transcendentals=0
        ),
        name="project",
    )(core, own, other, weight)


def documents(positions, bounds_ref):
    count = jnp.zeros(positions.shape, jnp.int32)
    for i in range(bounds_ref.shape[0]):
        count = count + (bounds_ref[i] <= positions).astype(jnp.int32)
    return count


def mask_bias(me, bounds_ref, tokens, order):
    rows = tokens // STEP
    own = lax.broadcasted_iota(jnp.int32, (1, tokens), 1) + me * tokens
    parts = [lax.broadcasted_iota(jnp.int32, (tokens, 1), 0) + me * tokens]
    for distance in order:
        at = lax.broadcasted_iota(jnp.int32, (rows, 1), 0) * STEP
        parts.append(at + (me - distance) * tokens)
    keys = jnp.concatenate(parts, 0)
    key_doc = jnp.where(keys >= 0, documents(keys, bounds_ref), -1)
    ok = (documents(own, bounds_ref) == key_doc) & (keys <= own)
    return jnp.where(ok, 0.0, -jnp.inf).astype(F32)


def sort_arrived(first, two, three, *more):
    return [jnp.where(first, three, two), jnp.where(first, two, three), *more]


def distances(levels):
    return [4, 1, 2] + [2**i for i in range(3, levels)]


SCALE = 1.0 / math.sqrt(DH)
POWER = SCALE * math.log2(math.e)


def near_kernel(
    levels, me_ref, bounds_ref, q_ref, k_ref, v_ref, ga_ref, far4_ref, far1_ref,
    grown_ref, gp_ref, stat_ref, bias_ref,
):
    tokens = q_ref.shape[0]
    rows = tokens // STEP
    near = tokens + 2 * rows
    bias_ref[...] = mask_bias(me_ref[0], bounds_ref, tokens, distances(levels))
    for h in range(q_ref.shape[1] // DH):
        cols = slice(h * DH, (h + 1) * DH)
        k = jnp.concatenate([k_ref[:, cols], far4_ref[:rows, cols], far1_ref[:rows, cols]], 0)
        v = jnp.concatenate([v_ref[:, cols], far4_ref[rows:, cols], far1_ref[rows:, cols]], 0)
        scores = nt(k, q_ref[:, cols]) + bias_ref[:near]
        top = jnp.max(scores, axis=0, keepdims=True)
        grown = jnp.exp2((scores - top) * POWER)
        grad_prob = nt(v, ga_ref[:, cols])
        grown_ref[h] = grown
        gp_ref[h] = grad_prob
        stat_ref[h, 0:1] = top
        stat_ref[h, 1:2] = jnp.sum(grown, axis=0, keepdims=True)
        stat_ref[h, 2:3] = jnp.sum(grown * grad_prob, axis=0, keepdims=True)


def attention_near(me, bounds, q, k, v, ga, far4, far1, levels):
    tokens, width = q.shape
    heads, rows = width // DH, tokens // STEP
    near, count = tokens + 2 * rows, tokens + levels * rows
    early = jax.ShapeDtypeStruct((heads, near, tokens), F32)
    return pl.pallas_call(
        functools.partial(near_kernel, levels),
        in_specs=[SMEM_BLOCK, SMEM_BLOCK] + [VMEM_BLOCK] * 6,
        out_specs=[VMEM_BLOCK] * 4,
        out_shape=[
            early,
            early,
            jax.ShapeDtypeStruct((heads, 8, tokens), F32),
            jax.ShapeDtypeStruct((count, tokens), F32),
        ],
        compiler_params=params(),
        cost_estimate=pl.CostEstimate(
            flops=4 * tokens * near * width, bytes_accessed=16 * tokens * width, transcendentals=0
        ),
        name="attention_near",
    )(me, bounds, q, k, v, ga, far4, far1)


def far_kernel(levels, *refs):
    me_ref, core_ref, q_ref, ga_ref, grown_ref, gp_ref, stat_ref, bias_ref = refs[:8]
    arrived_refs = refs[8 : 6 + levels]
    w_ref, u_ref, use_ref, far_ref, pass_ref = refs[6 + levels : 11 + levels]
    gfar_refs = refs[11 + levels :]
    tokens = q_ref.shape[0]
    rows = tokens // STEP
    near = tokens + 2 * rows
    first = core_ref[0] == 0
    passes = (core_ref[0] * (me_ref[0] % 2)).astype(F32)
    pass_ref[...] = jnp.full(pass_ref.shape, passes, F32)
    for h in range(q_ref.shape[1] // DH):
        cols = slice(h * DH, (h + 1) * DH)
        q, ga = q_ref[:, cols], ga_ref[:, cols]
        far = sort_arrived(first, *[r[:, cols] for r in arrived_refs])
        k = jnp.concatenate([f[:rows] for f in far], 0)
        v = jnp.concatenate([f[rows:] for f in far], 0)
        far_ref[0, :, cols] = k
        far_ref[1, :, cols] = v
        scores = nt(k, q) + bias_ref[near:]
        early_top = stat_ref[h, 0:1]
        top = jnp.maximum(early_top, jnp.max(scores, axis=0, keepdims=True))
        shrink = jnp.exp2((early_top - top) * POWER)
        grown = jnp.exp2((scores - top) * POWER)
        grad_prob = nt(v, ga)
        total = stat_ref[h, 1:2] * shrink + jnp.sum(grown, axis=0, keepdims=True)
        weighted = stat_ref[h, 2:3] * shrink + jnp.sum(grown * grad_prob, axis=0, keepdims=True)
        part = 1.0 / total
        delta = weighted * part
        early_part = shrink * part
        use_ref[h, 0:1] = early_part
        use_ref[h, 1:2] = delta
        prob = jnp.concatenate([grown_ref[h, tokens:] * early_part, grown * part], 0)
        grad_prob = jnp.concatenate([gp_ref[h, tokens:], grad_prob], 0)
        weights = prob.astype(BF16)
        grad_scores = (prob * (grad_prob - delta)).astype(BF16)
        w_ref[h] = weights
        u_ref[h] = grad_scores
        gk = (nn(grad_scores, q) * SCALE).astype(BF16)
        gv = nn(weights, ga).astype(BF16)
        g4, g1, g2, g8, *more = [
            jnp.concatenate([g[i * rows : (i + 1) * rows] for g in (gk, gv)], 0) for i in range(levels)
        ]
        out = [g4, jnp.where(first, g2, g1), jnp.where(first, g1, g8), jnp.where(first, g8, g2)]
        for ref, block in zip(gfar_refs, out + more):
            ref[:, cols] = block


def attention_far(me, core, q, ga, grown, grad_prob, stats, bias, arrived):
    tokens, width = q.shape
    levels = 2 + len(arrived)
    heads, rows = width // DH, tokens // STEP
    prob = jax.ShapeDtypeStruct((heads, levels * rows, tokens), BF16)
    return pl.pallas_call(
        functools.partial(far_kernel, levels),
        in_specs=[SMEM_BLOCK] * 2 + [VMEM_BLOCK] * (6 + len(arrived)),
        out_specs=[VMEM_BLOCK] * (5 + levels),
        out_shape=[
            prob,
            prob,
            jax.ShapeDtypeStruct(stats.shape, F32),
            jax.ShapeDtypeStruct((2, (levels - 2) * rows, width), BF16),
            jax.ShapeDtypeStruct((1, width), F32),
        ]
        + [jax.ShapeDtypeStruct((2 * rows, width), BF16)] * levels,
        compiler_params=params(),
        cost_estimate=pl.CostEstimate(
            flops=8 * tokens * levels * rows * width, bytes_accessed=16 * tokens * width, transcendentals=0
        ),
        name="attention_far",
    )(me, core, q, ga, grown, grad_prob, stats, bias, *arrived)


def local_kernel(
    q_ref, k_ref, v_ref, ga_ref, far4_ref, far1_ref, far_ref, grown_ref, gp_ref, use_ref, w_ref, u_ref,
    attn_ref, gq_ref, gk_ref, gv_ref,
):
    tokens = q_ref.shape[0]
    rows = tokens // STEP
    for h in range(q_ref.shape[1] // DH):
        cols = slice(h * DH, (h + 1) * DH)
        k = jnp.concatenate(
            [k_ref[:, cols], far4_ref[:rows, cols], far1_ref[:rows, cols], far_ref[0, :, cols]], 0
        )
        v = jnp.concatenate(
            [v_ref[:, cols], far4_ref[rows:, cols], far1_ref[rows:, cols], far_ref[1, :, cols]], 0
        )
        prob = grown_ref[h, :tokens] * use_ref[h, 0:1]
        near_weights = prob.astype(BF16)
        near_scores = (prob * (gp_ref[h, :tokens] - use_ref[h, 1:2])).astype(BF16)
        weights = jnp.concatenate([near_weights, w_ref[h]], 0)
        grad_scores = jnp.concatenate([near_scores, u_ref[h]], 0)
        attn_ref[:, cols] = tn(weights, v).astype(BF16)
        gq_ref[:, cols] = (tn(grad_scores, k) * SCALE).astype(BF16)
        gk_ref[:, cols] = nn(near_scores, q_ref[:, cols]) * SCALE
        gv_ref[:, cols] = nn(near_weights, ga_ref[:, cols])


def attention_local(q, *operands):
    tokens, width = q.shape
    bf = jax.ShapeDtypeStruct((tokens, width), BF16)
    f32 = jax.ShapeDtypeStruct((tokens, width), F32)
    return pl.pallas_call(
        local_kernel,
        in_specs=[VMEM_BLOCK] * (1 + len(operands)),
        out_specs=[VMEM_BLOCK] * 4,
        out_shape=[bf, bf, f32, f32],
        compiler_params=params(),
        cost_estimate=pl.CostEstimate(
            flops=12 * tokens * tokens * width, bytes_accessed=16 * tokens * width, transcendentals=0
        ),
        name="attention_local",
    )(q, *operands)


def lends_own(index):
    return index % 4 != 3, index % 4 < 2


def returns_own(index, first):
    own1, own2 = lends_own(index)
    rest = jnp.logical_not(first)
    return (first & own2) | (rest & (index % 2 == 0)), first & own1, rest & own2


def returns_lent(index, first):
    own1, own2 = lends_own(index)
    rest = jnp.logical_not(first)
    return first & jnp.logical_not(own2), rest | jnp.logical_not(own1), first | jnp.logical_not(own2)


def choose_kernel(me_ref, core_ref, picked_ref, far4_ref, two_ref, three_ref):
    first = core_ref[0] == 0
    picked, far4 = picked_ref[...], far4_ref[...]
    lent = jnp.where(lends_own(me_ref[0])[1], picked, far4)
    two_ref[...] = jnp.where(first, far4, lent)
    three_ref[...] = jnp.where(first, lent, far4)


def include(total, block, use):
    block = block.astype(F32)
    return total + jnp.where(use, block, jnp.zeros_like(block))


def collect_kernel(me_ref, core_ref, own_ref, one_ref, two_ref, three_ref, out_ref):
    total = own_ref[...].astype(F32)
    uses = returns_lent(me_ref[0], core_ref[0] == 0)
    for ref, use in zip((one_ref, two_ref, three_ref), uses):
        total = include(total, ref[...], use)
    out_ref[...] = total.astype(BF16)


def small(kernel, name, count, me, core, *blocks):
    shape = jax.ShapeDtypeStruct(blocks[0].shape, BF16)
    out = pl.pallas_call(
        kernel,
        in_specs=[SMEM_BLOCK] * 2 + [VMEM_BLOCK] * len(blocks),
        out_specs=[VMEM_BLOCK] * count,
        out_shape=[shape] * count,
        compiler_params=params(8),
        cost_estimate=pl.CostEstimate(
            flops=blocks[0].size, bytes_accessed=2 * blocks[0].size, transcendentals=0
        ),
        name=name,
    )(me, core, *blocks)
    return out if count > 1 else out[0]


def settle_kernel(me_ref, core_ref, gk_ref, gv_ref, last_ref, one_ref, two_ref, three_ref, *out_refs):
    tokens = gk_ref.shape[0]
    rows = tokens // STEP
    back = [last_ref[...]]
    for ref, own in zip((one_ref, two_ref, three_ref), returns_own(me_ref[0], core_ref[0] == 0)):
        block = ref[...]
        back.append(jnp.where(own, block, jnp.zeros_like(block)))
    at = lax.broadcasted_iota(jnp.int32, (tokens, rows), 0)
    spot = (at == lax.broadcasted_iota(jnp.int32, (tokens, rows), 1) * STEP).astype(BF16)
    spot = jnp.concatenate([spot] * len(back), 1)
    for i, (near_ref, out_ref) in enumerate(zip((gk_ref, gv_ref), out_refs)):
        extra = nn(spot, jnp.concatenate([b[i * rows : (i + 1) * rows] for b in back], 0))
        out_ref[...] = (near_ref[...] + extra).astype(BF16)


def settle(me, core, gk, gv, last, one, two, three):
    out = jax.ShapeDtypeStruct(gk.shape, BF16)
    return pl.pallas_call(
        settle_kernel,
        in_specs=[SMEM_BLOCK] * 2 + [VMEM_BLOCK] * 6,
        out_specs=[VMEM_BLOCK] * 2,
        out_shape=[out, out],
        compiler_params=params(),
        name="settle",
    )(me, core, gk, gv, last, one, two, three)


def add(*blocks):
    total = blocks[0].astype(F32)
    for block in blocks[1:]:
        total = total + block.astype(F32)
    return total.astype(BF16)


def per_device(queries, keys, values, out_weight, cotangent, bounds):
    n = lax.axis_size("ctx")
    levels = n.bit_length() - 1
    me = lax.axis_index("ctx").astype(jnp.int32).reshape(1)
    core = lax.axis_index("head").astype(jnp.int32).reshape(1)

    other_cot = swap(cotangent)
    picked = pick(keys, values)
    far4 = lax.ppermute(picked, "ctx", hop(4, n))
    far1 = lax.ppermute(picked, "ctx", hop(1, n))
    ga, picked = grad_attn(core, cotangent, other_cot, picked, out_weight)

    hops, twos = hop(4, n), pairs(n)
    two, three = small(choose_kernel, "choose", 2, me, core, picked, far4)
    two = mixed(two, (hops, twos))
    three = mixed(three, (twos, hops))
    arrived = [two, three]
    first = lax.axis_index("head") == 0 if levels > 4 else None
    farther = jnp.where(first, two, three) if levels > 4 else None
    for i in range(4, levels):
        farther = lax.ppermute(farther, "ctx", hop(2 ** (i - 1), n))
        arrived.append(farther)

    grown, grad_prob, stats, bias = attention_near(
        me, bounds, queries, keys, values, ga, far4, far1, levels
    )
    weights, grad_scores, use, far, passes, g4, two, three, four, *more = attention_far(
        me, core, queries, ga, grown, grad_prob, stats, bias, arrived
    )
    for i in reversed(range(len(more))):
        back = lax.ppermute(more[i], "ctx", hop(-(2 ** (i + 3)), n))
        if i > 0:
            more[i - 1] = add(more[i - 1], back)
        else:
            three = jnp.where(first, three, add(three, back))
            four = jnp.where(first, add(four, back), four)
    hops, ones, twos, nexts = hop(-4, n), turned(steps(n)), turned(twos), neighbours(n)
    one = mixed(two, (twos, nexts))
    two = mixed(three, (ones, hops))
    three = mixed((four.astype(F32) + one.astype(F32) * passes).astype(BF16), (hops, twos))
    attn, gq, gk, gv = attention_local(
        queries, keys, values, ga, far4, far1, far, grown, grad_prob, use, weights, grad_scores
    )
    back = (one, two, three)
    g4 = small(collect_kernel, "collect", 1, me, core, g4, *back)
    last = lax.ppermute(g4, "ctx", hop(-4, n))
    other_attn = swap(attn)
    output = project(core, attn, other_attn, out_weight)
    gk, gv = settle(me, core, gk, gv, last, *back)
    return output, gq, gk, gv


def solution(mesh):
    shared = P("ctx", "head")
    return jax.shard_map(
        per_device,
        mesh=mesh,
        in_specs=(shared, shared, shared, P(), shared, P()),
        out_specs=(shared,) * 4,
        check_vma=False,
    )
```

```python
import functools
import math

import jax
import jax.numpy as jnp
from jax import lax
from jax.experimental import pallas as pl
from jax.experimental.pallas import tpu as pltpu
from jax.sharding import PartitionSpec as P

DH = 128
STEP = 4
BF16 = jnp.bfloat16
F32 = jnp.float32
HBM_BLOCK = pl.BlockSpec(memory_space=pltpu.HBM)
VMEM_BLOCK = pl.BlockSpec(memory_space=pltpu.VMEM)
SMEM_BLOCK = pl.BlockSpec(memory_space=pltpu.SMEM)


def hop(distance, n):
    return [(i, i + distance) for i in range(n) if 0 <= i + distance < n]


def pairs(n):
    return [(i, i ^ 2) for i in range(n)]


def steps(n):
    return [(i, i - 3 if i % 4 == 3 else i + 1) for i in range(n)]


def neighbours(n):
    return [(i, i ^ 1) for i in range(n)]


def turned(route):
    return [(b, a) for a, b in route]


def mixed(block, route_of_core):
    cores = len(route_of_core)
    route = [(a * cores + c, b * cores + c) for c, r in enumerate(route_of_core) for a, b in r]
    return lax.ppermute(block, ("ctx", "head"), route)


def swap(block):
    return lax.ppermute(block, "head", [(0, 1), (1, 0)])


def nt(a, b):
    return lax.dot_general(a, b, (((1,), (1,)), ((), ())), preferred_element_type=F32)


def tn(a, b):
    return lax.dot_general(a, b, (((0,), (0,)), ((), ())), preferred_element_type=F32)


def nn(a, b):
    return jnp.dot(a, b, preferred_element_type=F32)


def params(mib=24):
    return pltpu.CompilerParams(vmem_limit_bytes=int(mib * 1024 * 1024))


def pick_kernel(k_hbm, v_hbm, out_ref, held, sems):
    tokens = k_hbm.shape[0]
    rows = tokens // STEP
    copies = [pltpu.make_async_copy(x, held.at[i], sems.at[i]) for i, x in enumerate((k_hbm, v_hbm))]
    for copy in copies:
        copy.start()
    at = lax.broadcasted_iota(jnp.int32, (rows, tokens), 0) * STEP
    choose = (at == lax.broadcasted_iota(jnp.int32, (rows, tokens), 1)).astype(BF16)
    for i, copy in enumerate(copies):
        copy.wait()
        out_ref[i * rows : (i + 1) * rows] = nn(choose, held[i]).astype(BF16)


def pick(keys, values):
    tokens, width = keys.shape
    return pl.pallas_call(
        pick_kernel,
        in_specs=[HBM_BLOCK, HBM_BLOCK],
        out_shape=jax.ShapeDtypeStruct((2 * tokens // STEP, width), BF16),
        scratch_shapes=[pltpu.VMEM((2, tokens, width), BF16), pltpu.SemaphoreType.DMA((2,))],
        compiler_params=params(63.5),
        name="pick",
    )(keys, values)


def grad_attn_kernel(core_ref, own_ref, other_hbm, w_hbm, out_ref, done_ref, got, held, got_sem, sems):
    pieces, tile, _ = held.shape
    core = core_ref[0]
    fetch = pltpu.make_async_copy(other_hbm, got, got_sem)
    fetch.start()
    copies = []
    for i in range(pieces):
        rows = w_hbm.at[pl.ds((core * pieces + i) * tile, tile), :]
        copies.append(pltpu.make_async_copy(rows, held.at[i], sems.at[i]))
        copies[i].start()
    done_ref[...] = jnp.zeros_like(done_ref)
    fetch.wait()
    own, other = own_ref[...], got[...]
    cot = jnp.concatenate([jnp.where(core == 0, own, other), jnp.where(core == 0, other, own)], 1)
    for i in range(pieces):
        copies[i].wait()
        out_ref[:, i * tile : (i + 1) * tile] = nt(cot, held[i]).astype(BF16)


def grad_attn(core, own, other, weight):
    tokens, width = own.shape
    pieces = 4
    return pl.pallas_call(
        grad_attn_kernel,
        in_specs=[SMEM_BLOCK, VMEM_BLOCK, HBM_BLOCK, HBM_BLOCK],
        out_specs=[VMEM_BLOCK] * 2,
        out_shape=[
            jax.ShapeDtypeStruct((tokens, width), BF16),
            jax.ShapeDtypeStruct((8, DH), F32),
        ],
        scratch_shapes=[
            pltpu.VMEM((tokens, width), BF16),
            pltpu.VMEM((pieces, width // pieces, weight.shape[1]), BF16),
            pltpu.SemaphoreType.DMA,
            pltpu.SemaphoreType.DMA((pieces,)),
        ],
        compiler_params=params(52),
        cost_estimate=pl.CostEstimate(
            flops=4 * tokens * width * width, bytes_accessed=6 * width * width, transcendentals=0
        ),
        name="grad_attn",
    )(core, own, other, weight)


def project_kernel(core_ref, own_ref, other_ref, w_hbm, out_ref, held, sems):
    pieces, tile, width = held.shape
    core = core_ref[0]
    columns = pl.ds(pl.multiple_of(core * width, width), width)
    copies = []
    for i in range(pieces):
        part = w_hbm.at[pl.ds(i * tile, tile), columns]
        copies.append(pltpu.make_async_copy(part, held.at[i], sems.at[i]))
        copies[i].start()
    own, other = own_ref[...], other_ref[...]
    whole = jnp.concatenate([jnp.where(core == 0, own, other), jnp.where(core == 0, other, own)], 1)
    total = None
    for i in range(pieces):
        copies[i].wait()
        term = nn(whole[:, i * tile : (i + 1) * tile], held[i])
        total = term if total is None else total + term
    out_ref[...] = total.astype(BF16)


def project(core, own, other, weight):
    tokens, width = own.shape
    pieces = 4
    return pl.pallas_call(
        project_kernel,
        in_specs=[SMEM_BLOCK, VMEM_BLOCK, VMEM_BLOCK, HBM_BLOCK],
        out_specs=VMEM_BLOCK,
        out_shape=jax.ShapeDtypeStruct((tokens, width), BF16),
        scratch_shapes=[
            pltpu.VMEM((pieces, weight.shape[0] // pieces, width), BF16),
            pltpu.SemaphoreType.DMA((pieces,)),
        ],
        compiler_params=params(52),
        cost_estimate=pl.CostEstimate(
            flops=4 * tokens * width * width, bytes_accessed=6 * width * width, transcendentals=0
        ),
        name="project",
    )(core, own, other, weight)


def documents(positions, bounds_ref):
    count = jnp.zeros(positions.shape, jnp.int32)
    for i in range(bounds_ref.shape[0]):
        count = count + (bounds_ref[i] <= positions).astype(jnp.int32)
    return count


def mask_bias(me, bounds_ref, tokens, order):
    rows = tokens // STEP
    own = lax.broadcasted_iota(jnp.int32, (1, tokens), 1) + me * tokens
    parts = [lax.broadcasted_iota(jnp.int32, (tokens, 1), 0) + me * tokens]
    for distance in order:
        at = lax.broadcasted_iota(jnp.int32, (rows, 1), 0) * STEP
        parts.append(at + (me - distance) * tokens)
    keys = jnp.concatenate(parts, 0)
    key_doc = jnp.where(keys >= 0, documents(keys, bounds_ref), -1)
    ok = (documents(own, bounds_ref) == key_doc) & (keys <= own)
    return jnp.where(ok, 0.0, -jnp.inf).astype(F32)


def sort_arrived(first, two, three, *more):
    return [jnp.where(first, three, two), jnp.where(first, two, three), *more]


def distances(levels):
    return [4, 1, 2] + [2**i for i in range(3, levels)]


SCALE = 1.0 / math.sqrt(DH)
POWER = SCALE * math.log2(math.e)


def near_kernel(
    levels, me_ref, bounds_ref, q_ref, k_ref, v_ref, ga_ref, far4_ref, far1_ref,
    grown_ref, gp_ref, stat_ref, bias_ref,
):
    tokens = q_ref.shape[0]
    rows = tokens // STEP
    near = tokens + 2 * rows
    bias_ref[...] = mask_bias(me_ref[0], bounds_ref, tokens, distances(levels))
    for h in range(q_ref.shape[1] // DH):
        cols = slice(h * DH, (h + 1) * DH)
        k = jnp.concatenate([k_ref[:, cols], far4_ref[:rows, cols], far1_ref[:rows, cols]], 0)
        v = jnp.concatenate([v_ref[:, cols], far4_ref[rows:, cols], far1_ref[rows:, cols]], 0)
        scores = nt(k, q_ref[:, cols]) + bias_ref[:near]
        top = jnp.max(scores, axis=0, keepdims=True)
        grown = jnp.exp2((scores - top) * POWER)
        grad_prob = nt(v, ga_ref[:, cols])
        grown_ref[h] = grown
        gp_ref[h] = grad_prob
        stat_ref[h, 0:1] = top
        stat_ref[h, 1:2] = jnp.sum(grown, axis=0, keepdims=True)
        stat_ref[h, 2:3] = jnp.sum(grown * grad_prob, axis=0, keepdims=True)


def attention_near(me, bounds, q, k, v, ga, far4, far1, levels):
    tokens, width = q.shape
    heads, rows = width // DH, tokens // STEP
    near, count = tokens + 2 * rows, tokens + levels * rows
    early = jax.ShapeDtypeStruct((heads, near, tokens), F32)
    return pl.pallas_call(
        functools.partial(near_kernel, levels),
        in_specs=[SMEM_BLOCK, SMEM_BLOCK] + [VMEM_BLOCK] * 6,
        out_specs=[VMEM_BLOCK] * 4,
        out_shape=[
            early,
            early,
            jax.ShapeDtypeStruct((heads, 8, tokens), F32),
            jax.ShapeDtypeStruct((count, tokens), F32),
        ],
        compiler_params=params(),
        cost_estimate=pl.CostEstimate(
            flops=4 * tokens * near * width, bytes_accessed=16 * tokens * width, transcendentals=0
        ),
        name="attention_near",
    )(me, bounds, q, k, v, ga, far4, far1)


def far_kernel(levels, *refs):
    me_ref, core_ref, q_ref, ga_ref, grown_ref, gp_ref, stat_ref, bias_ref = refs[:8]
    arrived_refs = refs[8 : 6 + levels]
    w_ref, u_ref, use_ref, far_ref, pass_ref = refs[6 + levels : 11 + levels]
    gfar_refs = refs[11 + levels :]
    tokens = q_ref.shape[0]
    rows = tokens // STEP
    near = tokens + 2 * rows
    first = core_ref[0] == 0
    passes = (core_ref[0] * (me_ref[0] % 2)).astype(F32)
    pass_ref[...] = jnp.full(pass_ref.shape, passes, F32)
    for h in range(q_ref.shape[1] // DH):
        cols = slice(h * DH, (h + 1) * DH)
        q, ga = q_ref[:, cols], ga_ref[:, cols]
        far = sort_arrived(first, *[r[:, cols] for r in arrived_refs])
        k = jnp.concatenate([f[:rows] for f in far], 0)
        v = jnp.concatenate([f[rows:] for f in far], 0)
        far_ref[0, :, cols] = k
        far_ref[1, :, cols] = v
        scores = nt(k, q) + bias_ref[near:]
        early_top = stat_ref[h, 0:1]
        top = jnp.maximum(early_top, jnp.max(scores, axis=0, keepdims=True))
        shrink = jnp.exp2((early_top - top) * POWER)
        grown = jnp.exp2((scores - top) * POWER)
        grad_prob = nt(v, ga)
        total = stat_ref[h, 1:2] * shrink + jnp.sum(grown, axis=0, keepdims=True)
        weighted = stat_ref[h, 2:3] * shrink + jnp.sum(grown * grad_prob, axis=0, keepdims=True)
        part = 1.0 / total
        delta = weighted * part
        early_part = shrink * part
        use_ref[h, 0:1] = early_part
        use_ref[h, 1:2] = delta
        prob = jnp.concatenate([grown_ref[h, tokens:] * early_part, grown * part], 0)
        grad_prob = jnp.concatenate([gp_ref[h, tokens:], grad_prob], 0)
        weights = prob.astype(BF16)
        grad_scores = (prob * (grad_prob - delta)).astype(BF16)
        w_ref[h] = weights
        u_ref[h] = grad_scores
        gk = (nn(grad_scores, q) * SCALE).astype(BF16)
        gv = nn(weights, ga).astype(BF16)
        g4, g1, g2, g8, *more = [
            jnp.concatenate([g[i * rows : (i + 1) * rows] for g in (gk, gv)], 0) for i in range(levels)
        ]
        out = [g4, jnp.where(first, g2, g1), jnp.where(first, g1, g8), jnp.where(first, g8, g2)]
        for ref, block in zip(gfar_refs, out + more):
            ref[:, cols] = block


def attention_far(me, core, q, ga, grown, grad_prob, stats, bias, arrived):
    tokens, width = q.shape
    levels = 2 + len(arrived)
    heads, rows = width // DH, tokens // STEP
    prob = jax.ShapeDtypeStruct((heads, levels * rows, tokens), BF16)
    return pl.pallas_call(
        functools.partial(far_kernel, levels),
        in_specs=[SMEM_BLOCK] * 2 + [VMEM_BLOCK] * (6 + len(arrived)),
        out_specs=[VMEM_BLOCK] * (5 + levels),
        out_shape=[
            prob,
            prob,
            jax.ShapeDtypeStruct(stats.shape, F32),
            jax.ShapeDtypeStruct((2, (levels - 2) * rows, width), BF16),
            jax.ShapeDtypeStruct((1, width), F32),
        ]
        + [jax.ShapeDtypeStruct((2 * rows, width), BF16)] * levels,
        compiler_params=params(),
        cost_estimate=pl.CostEstimate(
            flops=8 * tokens * levels * rows * width, bytes_accessed=16 * tokens * width, transcendentals=0
        ),
        name="attention_far",
    )(me, core, q, ga, grown, grad_prob, stats, bias, *arrived)


def local_kernel(
    q_ref, k_ref, v_ref, ga_ref, far4_ref, far1_ref, far_ref, grown_ref, gp_ref, use_ref, w_ref, u_ref,
    attn_ref, gq_ref, gk_ref, gv_ref,
):
    tokens = q_ref.shape[0]
    rows = tokens // STEP
    for h in range(q_ref.shape[1] // DH):
        cols = slice(h * DH, (h + 1) * DH)
        k = jnp.concatenate(
            [k_ref[:, cols], far4_ref[:rows, cols], far1_ref[:rows, cols], far_ref[0, :, cols]], 0
        )
        v = jnp.concatenate(
            [v_ref[:, cols], far4_ref[rows:, cols], far1_ref[rows:, cols], far_ref[1, :, cols]], 0
        )
        prob = grown_ref[h, :tokens] * use_ref[h, 0:1]
        near_weights = prob.astype(BF16)
        near_scores = (prob * (gp_ref[h, :tokens] - use_ref[h, 1:2])).astype(BF16)
        weights = jnp.concatenate([near_weights, w_ref[h]], 0)
        grad_scores = jnp.concatenate([near_scores, u_ref[h]], 0)
        attn_ref[:, cols] = tn(weights, v).astype(BF16)
        gq_ref[:, cols] = (tn(grad_scores, k) * SCALE).astype(BF16)
        gk_ref[:, cols] = nn(near_scores, q_ref[:, cols]) * SCALE
        gv_ref[:, cols] = nn(near_weights, ga_ref[:, cols])


def attention_local(q, *operands):
    tokens, width = q.shape
    bf = jax.ShapeDtypeStruct((tokens, width), BF16)
    f32 = jax.ShapeDtypeStruct((tokens, width), F32)
    return pl.pallas_call(
        local_kernel,
        in_specs=[VMEM_BLOCK] * (1 + len(operands)),
        out_specs=[VMEM_BLOCK] * 4,
        out_shape=[bf, bf, f32, f32],
        compiler_params=params(),
        cost_estimate=pl.CostEstimate(
            flops=12 * tokens * tokens * width, bytes_accessed=16 * tokens * width, transcendentals=0
        ),
        name="attention_local",
    )(q, *operands)


def lends_own(index):
    return index % 4 != 3, index % 4 < 2


def returns_own(index, first):
    own1, own2 = lends_own(index)
    rest = jnp.logical_not(first)
    return (first & own2) | (rest & (index % 2 == 0)), first & own1, rest & own2


def returns_lent(index, first):
    own1, own2 = lends_own(index)
    rest = jnp.logical_not(first)
    return first & jnp.logical_not(own2), rest | jnp.logical_not(own1), first | jnp.logical_not(own2)


def choose_kernel(me_ref, core_ref, picked_ref, far4_ref, after, two_ref, three_ref):
    first = core_ref[0] == 0
    picked, far4 = picked_ref[...], far4_ref[...]
    lent = jnp.where(lends_own(me_ref[0])[1], picked, far4)
    two_ref[...] = jnp.where(first, far4, lent)
    three_ref[...] = jnp.where(first, lent, far4)


def include(total, block, use):
    block = block.astype(F32)
    return total + jnp.where(use, block, jnp.zeros_like(block))


def collect_kernel(me_ref, core_ref, own_ref, one_ref, two_ref, three_ref, out_ref):
    total = own_ref[...].astype(F32)
    uses = returns_lent(me_ref[0], core_ref[0] == 0)
    for ref, use in zip((one_ref, two_ref, three_ref), uses):
        total = include(total, ref[...], use)
    out_ref[...] = total.astype(BF16)


def small(kernel, name, count, me, core, *blocks):
    shape = jax.ShapeDtypeStruct(blocks[0].shape, BF16)
    out = pl.pallas_call(
        kernel,
        in_specs=[SMEM_BLOCK] * 2 + [VMEM_BLOCK] * len(blocks),
        out_specs=[VMEM_BLOCK] * count,
        out_shape=[shape] * count,
        compiler_params=params(8),
        cost_estimate=pl.CostEstimate(
            flops=blocks[0].size, bytes_accessed=2 * blocks[0].size, transcendentals=0
        ),
        name=name,
    )(me, core, *blocks)
    return out if count > 1 else out[0]


def settle_kernel(me_ref, core_ref, gk_ref, gv_ref, last_ref, one_ref, two_ref, three_ref, *out_refs):
    tokens = gk_ref.shape[0]
    rows = tokens // STEP
    back = [last_ref[...]]
    for ref, own in zip((one_ref, two_ref, three_ref), returns_own(me_ref[0], core_ref[0] == 0)):
        block = ref[...]
        back.append(jnp.where(own, block, jnp.zeros_like(block)))
    at = lax.broadcasted_iota(jnp.int32, (tokens, rows), 0)
    spot = (at == lax.broadcasted_iota(jnp.int32, (tokens, rows), 1) * STEP).astype(BF16)
    spot = jnp.concatenate([spot] * len(back), 1)
    for i, (near_ref, out_ref) in enumerate(zip((gk_ref, gv_ref), out_refs)):
        extra = nn(spot, jnp.concatenate([b[i * rows : (i + 1) * rows] for b in back], 0))
        out_ref[...] = (near_ref[...] + extra).astype(BF16)


def settle(me, core, gk, gv, last, one, two, three):
    out = jax.ShapeDtypeStruct(gk.shape, BF16)
    return pl.pallas_call(
        settle_kernel,
        in_specs=[SMEM_BLOCK] * 2 + [VMEM_BLOCK] * 6,
        out_specs=[VMEM_BLOCK] * 2,
        out_shape=[out, out],
        compiler_params=params(),
        name="settle",
    )(me, core, gk, gv, last, one, two, three)


def add(*blocks):
    total = blocks[0].astype(F32)
    for block in blocks[1:]:
        total = total + block.astype(F32)
    return total.astype(BF16)


def per_device(queries, keys, values, out_weight, cotangent, bounds):
    n = lax.axis_size("ctx")
    levels = n.bit_length() - 1
    me = lax.axis_index("ctx").astype(jnp.int32).reshape(1)
    core = lax.axis_index("head").astype(jnp.int32).reshape(1)

    other_cot = swap(cotangent)
    picked = pick(keys, values)
    far4 = lax.ppermute(picked, "ctx", hop(4, n))
    far1 = lax.ppermute(picked, "ctx", hop(1, n))
    ga, done = grad_attn(core, cotangent, other_cot, out_weight)

    hops, twos = hop(4, n), pairs(n)
    two, three = small(choose_kernel, "choose", 2, me, core, picked, far4, done)
    two = mixed(two, (hops, twos))
    three = mixed(three, (twos, hops))
    arrived = [two, three]
    first = lax.axis_index("head") == 0 if levels > 4 else None
    farther = jnp.where(first, two, three) if levels > 4 else None
    for i in range(4, levels):
        farther = lax.ppermute(farther, "ctx", hop(2 ** (i - 1), n))
        arrived.append(farther)

    grown, grad_prob, stats, bias = attention_near(
        me, bounds, queries, keys, values, ga, far4, far1, levels
    )
    weights, grad_scores, use, far, passes, g4, two, three, four, *more = attention_far(
        me, core, queries, ga, grown, grad_prob, stats, bias, arrived
    )
    for i in reversed(range(len(more))):
        back = lax.ppermute(more[i], "ctx", hop(-(2 ** (i + 3)), n))
        if i > 0:
            more[i - 1] = add(more[i - 1], back)
        else:
            three = jnp.where(first, three, add(three, back))
            four = jnp.where(first, add(four, back), four)
    hops, ones, twos, nexts = hop(-4, n), turned(steps(n)), turned(twos), neighbours(n)
    one = mixed(two, (twos, nexts))
    two = mixed(three, (ones, hops))
    three = mixed((four.astype(F32) + one.astype(F32) * passes).astype(BF16), (hops, twos))
    attn, gq, gk, gv = attention_local(
        queries, keys, values, ga, far4, far1, far, grown, grad_prob, use, weights, grad_scores
    )
    back = (one, two, three)
    g4 = small(collect_kernel, "collect", 1, me, core, g4, *back)
    last = lax.ppermute(g4, "ctx", hop(-4, n))
    other_attn = swap(attn)
    output = project(core, attn, other_attn, out_weight)
    gk, gv = settle(me, core, gk, gv, last, *back)
    return output, gq, gk, gv


def solution(mesh):
    shared = P("ctx", "head")
    return jax.shard_map(
        per_device,
        mesh=mesh,
        in_specs=(shared, shared, shared, P(), shared, P()),
        out_specs=(shared,) * 4,
        check_vma=False,
    )
```

```python
import functools
import math

import jax
import jax.numpy as jnp
from jax import lax
from jax.experimental import pallas as pl
from jax.experimental.pallas import tpu as pltpu
from jax.sharding import PartitionSpec as P

DH = 128
STEP = 4
BF16 = jnp.bfloat16
F32 = jnp.float32
HBM_BLOCK = pl.BlockSpec(memory_space=pltpu.HBM)
VMEM_BLOCK = pl.BlockSpec(memory_space=pltpu.VMEM)
SMEM_BLOCK = pl.BlockSpec(memory_space=pltpu.SMEM)


def hop(distance, n):
    return [(i, i + distance) for i in range(n) if 0 <= i + distance < n]


def pairs(n):
    return [(i, i ^ 2) for i in range(n)]


def steps(n):
    return [(i, i - 3 if i % 4 == 3 else i + 1) for i in range(n)]


def neighbours(n):
    return [(i, i ^ 1) for i in range(n)]


def turned(route):
    return [(b, a) for a, b in route]


def mixed(block, route_of_core):
    cores = len(route_of_core)
    route = [(a * cores + c, b * cores + c) for c, r in enumerate(route_of_core) for a, b in r]
    return lax.ppermute(block, ("ctx", "head"), route)


def swap(block):
    return lax.ppermute(block, "head", [(0, 1), (1, 0)])


def nt(a, b):
    return lax.dot_general(a, b, (((1,), (1,)), ((), ())), preferred_element_type=F32)


def tn(a, b):
    return lax.dot_general(a, b, (((0,), (0,)), ((), ())), preferred_element_type=F32)


def nn(a, b):
    return jnp.dot(a, b, preferred_element_type=F32)


def params(mib=24):
    return pltpu.CompilerParams(vmem_limit_bytes=int(mib * 1024 * 1024))


def pick_kernel(k_hbm, v_hbm, out_hbm, held, ready, in_sems, out_sems):
    tokens, width = k_hbm.shape
    rows, half = tokens // STEP, width // 2
    parts = [(i, x, slice(c * half, (c + 1) * half)) for i, x in enumerate((k_hbm, v_hbm)) for c in (0, 1)]
    copies = []
    for n, (i, x, cols) in enumerate(parts):
        copies.append(pltpu.make_async_copy(x.at[:, cols], held.at[i, :, cols], in_sems.at[n]))
        copies[n].start()
    at = lax.broadcasted_iota(jnp.int32, (rows, tokens), 0) * STEP
    choose = (at == lax.broadcasted_iota(jnp.int32, (rows, tokens), 1)).astype(BF16)
    sent = []
    for n, (i, x, cols) in enumerate(parts):
        copies[n].wait()
        ready[i * rows : (i + 1) * rows, cols] = nn(choose, held[i, :, cols]).astype(BF16)
        block = pl.ds(i * rows, rows), cols
        sent.append(pltpu.make_async_copy(ready.at[block], out_hbm.at[block], out_sems.at[n]))
        sent[n].start()
    for copy in sent:
        copy.wait()


def pick(keys, values):
    tokens, width = keys.shape
    shape = (2 * tokens // STEP, width)
    return pl.pallas_call(
        pick_kernel,
        in_specs=[HBM_BLOCK, HBM_BLOCK],
        out_specs=HBM_BLOCK,
        out_shape=jax.ShapeDtypeStruct(shape, BF16),
        scratch_shapes=[
            pltpu.VMEM((2, tokens, width), BF16),
            pltpu.VMEM(shape, BF16),
            pltpu.SemaphoreType.DMA((4,)),
            pltpu.SemaphoreType.DMA((4,)),
        ],
        compiler_params=params(63.5),
        name="pick",
    )(keys, values)


def grad_attn_kernel(core_ref, own_ref, other_hbm, w_hbm, out_ref, done_ref, got, held, got_sem, sems):
    pieces, tile, _ = held.shape
    core = core_ref[0]
    fetch = pltpu.make_async_copy(other_hbm, got, got_sem)
    fetch.start()
    copies = []
    for i in range(pieces):
        rows = w_hbm.at[pl.ds((core * pieces + i) * tile, tile), :]
        copies.append(pltpu.make_async_copy(rows, held.at[i], sems.at[i]))
        copies[i].start()
    done_ref[...] = jnp.zeros_like(done_ref)
    fetch.wait()
    own, other = own_ref[...], got[...]
    cot = jnp.concatenate([jnp.where(core == 0, own, other), jnp.where(core == 0, other, own)], 1)
    for i in range(pieces):
        copies[i].wait()
        out_ref[:, i * tile : (i + 1) * tile] = nt(cot, held[i]).astype(BF16)


def grad_attn(core, own, other, weight):
    tokens, width = own.shape
    pieces = 4
    return pl.pallas_call(
        grad_attn_kernel,
        in_specs=[SMEM_BLOCK, VMEM_BLOCK, HBM_BLOCK, HBM_BLOCK],
        out_specs=[VMEM_BLOCK] * 2,
        out_shape=[
            jax.ShapeDtypeStruct((tokens, width), BF16),
            jax.ShapeDtypeStruct((8, DH), F32),
        ],
        scratch_shapes=[
            pltpu.VMEM((tokens, width), BF16),
            pltpu.VMEM((pieces, width // pieces, weight.shape[1]), BF16),
            pltpu.SemaphoreType.DMA,
            pltpu.SemaphoreType.DMA((pieces,)),
        ],
        compiler_params=params(52),
        cost_estimate=pl.CostEstimate(
            flops=4 * tokens * width * width, bytes_accessed=6 * width * width, transcendentals=0
        ),
        name="grad_attn",
    )(core, own, other, weight)


def project_kernel(core_ref, own_ref, other_ref, w_hbm, out_ref, held, sems):
    pieces, tile, width = held.shape
    core = core_ref[0]
    columns = pl.ds(pl.multiple_of(core * width, width), width)
    copies = []
    for i in range(pieces):
        part = w_hbm.at[pl.ds(i * tile, tile), columns]
        copies.append(pltpu.make_async_copy(part, held.at[i], sems.at[i]))
        copies[i].start()
    own, other = own_ref[...], other_ref[...]
    whole = jnp.concatenate([jnp.where(core == 0, own, other), jnp.where(core == 0, other, own)], 1)
    total = None
    for i in range(pieces):
        copies[i].wait()
        term = nn(whole[:, i * tile : (i + 1) * tile], held[i])
        total = term if total is None else total + term
    out_ref[...] = total.astype(BF16)


def project(core, own, other, weight):
    tokens, width = own.shape
    pieces = 4
    return pl.pallas_call(
        project_kernel,
        in_specs=[SMEM_BLOCK, VMEM_BLOCK, VMEM_BLOCK, HBM_BLOCK],
        out_specs=VMEM_BLOCK,
        out_shape=jax.ShapeDtypeStruct((tokens, width), BF16),
        scratch_shapes=[
            pltpu.VMEM((pieces, weight.shape[0] // pieces, width), BF16),
            pltpu.SemaphoreType.DMA((pieces,)),
        ],
        compiler_params=params(52),
        cost_estimate=pl.CostEstimate(
            flops=4 * tokens * width * width, bytes_accessed=6 * width * width, transcendentals=0
        ),
        name="project",
    )(core, own, other, weight)


def documents(positions, bounds_ref):
    count = jnp.zeros(positions.shape, jnp.int32)
    for i in range(bounds_ref.shape[0]):
        count = count + (bounds_ref[i] <= positions).astype(jnp.int32)
    return count


def mask_bias(me, bounds_ref, tokens, order):
    rows = tokens // STEP
    own = lax.broadcasted_iota(jnp.int32, (1, tokens), 1) + me * tokens
    parts = [lax.broadcasted_iota(jnp.int32, (tokens, 1), 0) + me * tokens]
    for distance in order:
        at = lax.broadcasted_iota(jnp.int32, (rows, 1), 0) * STEP
        parts.append(at + (me - distance) * tokens)
    keys = jnp.concatenate(parts, 0)
    key_doc = jnp.where(keys >= 0, documents(keys, bounds_ref), -1)
    ok = (documents(own, bounds_ref) == key_doc) & (keys <= own)
    return jnp.where(ok, 0.0, -jnp.inf).astype(F32)


def sort_arrived(first, two, three, *more):
    return [jnp.where(first, three, two), jnp.where(first, two, three), *more]


def distances(levels):
    return [4, 1, 2] + [2**i for i in range(3, levels)]


SCALE = 1.0 / math.sqrt(DH)
POWER = SCALE * math.log2(math.e)


def near_kernel(
    levels, me_ref, bounds_ref, q_ref, k_ref, v_ref, ga_ref, far4_ref, far1_ref,
    grown_ref, gp_ref, stat_ref, bias_ref,
):
    tokens = q_ref.shape[0]
    rows = tokens // STEP
    near = tokens + 2 * rows
    bias_ref[...] = mask_bias(me_ref[0], bounds_ref, tokens, distances(levels))
    for h in range(q_ref.shape[1] // DH):
        cols = slice(h * DH, (h + 1) * DH)
        k = jnp.concatenate([k_ref[:, cols], far4_ref[:rows, cols], far1_ref[:rows, cols]], 0)
        v = jnp.concatenate([v_ref[:, cols], far4_ref[rows:, cols], far1_ref[rows:, cols]], 0)
        scores = nt(k, q_ref[:, cols]) + bias_ref[:near]
        top = jnp.max(scores, axis=0, keepdims=True)
        grown = jnp.exp2((scores - top) * POWER)
        grad_prob = nt(v, ga_ref[:, cols])
        grown_ref[h] = grown
        gp_ref[h] = grad_prob
        stat_ref[h, 0:1] = top
        stat_ref[h, 1:2] = jnp.sum(grown, axis=0, keepdims=True)
        stat_ref[h, 2:3] = jnp.sum(grown * grad_prob, axis=0, keepdims=True)


def attention_near(me, bounds, q, k, v, ga, far4, far1, levels):
    tokens, width = q.shape
    heads, rows = width // DH, tokens // STEP
    near, count = tokens + 2 * rows, tokens + levels * rows
    early = jax.ShapeDtypeStruct((heads, near, tokens), F32)
    return pl.pallas_call(
        functools.partial(near_kernel, levels),
        in_specs=[SMEM_BLOCK, SMEM_BLOCK] + [VMEM_BLOCK] * 6,
        out_specs=[VMEM_BLOCK] * 4,
        out_shape=[
            early,
            early,
            jax.ShapeDtypeStruct((heads, 8, tokens), F32),
            jax.ShapeDtypeStruct((count, tokens), F32),
        ],
        compiler_params=params(),
        cost_estimate=pl.CostEstimate(
            flops=4 * tokens * near * width, bytes_accessed=16 * tokens * width, transcendentals=0
        ),
        name="attention_near",
    )(me, bounds, q, k, v, ga, far4, far1)


def far_kernel(levels, *refs):
    me_ref, core_ref, q_ref, ga_ref, grown_ref, gp_ref, stat_ref, bias_ref = refs[:8]
    arrived_refs = refs[8 : 6 + levels]
    w_ref, u_ref, use_ref, far_ref, pass_ref = refs[6 + levels : 11 + levels]
    gfar_refs = refs[11 + levels :]
    tokens = q_ref.shape[0]
    rows = tokens // STEP
    near = tokens + 2 * rows
    first = core_ref[0] == 0
    passes = (core_ref[0] * (me_ref[0] % 2)).astype(F32)
    pass_ref[...] = jnp.full(pass_ref.shape, passes, F32)
    for h in range(q_ref.shape[1] // DH):
        cols = slice(h * DH, (h + 1) * DH)
        q, ga = q_ref[:, cols], ga_ref[:, cols]
        far = sort_arrived(first, *[r[:, cols] for r in arrived_refs])
        k = jnp.concatenate([f[:rows] for f in far], 0)
        v = jnp.concatenate([f[rows:] for f in far], 0)
        far_ref[0, :, cols] = k
        far_ref[1, :, cols] = v
        scores = nt(k, q) + bias_ref[near:]
        early_top = stat_ref[h, 0:1]
        top = jnp.maximum(early_top, jnp.max(scores, axis=0, keepdims=True))
        shrink = jnp.exp2((early_top - top) * POWER)
        grown = jnp.exp2((scores - top) * POWER)
        grad_prob = nt(v, ga)
        total = stat_ref[h, 1:2] * shrink + jnp.sum(grown, axis=0, keepdims=True)
        weighted = stat_ref[h, 2:3] * shrink + jnp.sum(grown * grad_prob, axis=0, keepdims=True)
        part = 1.0 / total
        delta = weighted * part
        early_part = shrink * part
        use_ref[h, 0:1] = early_part
        use_ref[h, 1:2] = delta
        prob = jnp.concatenate([grown_ref[h, tokens + rows :] * early_part, grown * part], 0)
        grad_prob = jnp.concatenate([gp_ref[h, tokens + rows :], grad_prob], 0)
        weights = prob.astype(BF16)
        grad_scores = (prob * (grad_prob - delta)).astype(BF16)
        w_ref[h] = weights
        u_ref[h] = grad_scores
        gk = (nn(grad_scores, q) * SCALE).astype(BF16)
        gv = nn(weights, ga).astype(BF16)
        g1, g2, g8, *more = [
            jnp.concatenate([g[i * rows : (i + 1) * rows] for g in (gk, gv)], 0) for i in range(levels - 1)
        ]
        out = [jnp.where(first, g2, g1), jnp.where(first, g1, g8), jnp.where(first, g8, g2)]
        for ref, block in zip(gfar_refs, out + more):
            ref[:, cols] = block


def attention_far(me, core, q, ga, grown, grad_prob, stats, bias, arrived):
    tokens, width = q.shape
    levels = 2 + len(arrived)
    heads, rows = width // DH, tokens // STEP
    prob = jax.ShapeDtypeStruct((heads, (levels - 1) * rows, tokens), BF16)
    return pl.pallas_call(
        functools.partial(far_kernel, levels),
        in_specs=[SMEM_BLOCK] * 2 + [VMEM_BLOCK] * (6 + len(arrived)),
        out_specs=[VMEM_BLOCK] * (4 + levels),
        out_shape=[
            prob,
            prob,
            jax.ShapeDtypeStruct(stats.shape, F32),
            jax.ShapeDtypeStruct((2, (levels - 2) * rows, width), BF16),
            jax.ShapeDtypeStruct((1, width), F32),
        ]
        + [jax.ShapeDtypeStruct((2 * rows, width), BF16)] * (levels - 1),
        compiler_params=params(),
        cost_estimate=pl.CostEstimate(
            flops=8 * tokens * levels * rows * width, bytes_accessed=16 * tokens * width, transcendentals=0
        ),
        name="attention_far",
    )(me, core, q, ga, grown, grad_prob, stats, bias, *arrived)


def local_kernel(
    q_ref, k_ref, v_ref, ga_ref, far4_ref, far1_ref, far_ref, grown_ref, gp_ref, use_ref, w_ref, u_ref,
    attn_ref, gq_ref, gk_ref, gv_ref, g4_ref,
):
    tokens = q_ref.shape[0]
    rows = tokens // STEP
    near = tokens + rows
    for h in range(q_ref.shape[1] // DH):
        cols = slice(h * DH, (h + 1) * DH)
        k = jnp.concatenate(
            [k_ref[:, cols], far4_ref[:rows, cols], far1_ref[:rows, cols], far_ref[0, :, cols]], 0
        )
        v = jnp.concatenate(
            [v_ref[:, cols], far4_ref[rows:, cols], far1_ref[rows:, cols], far_ref[1, :, cols]], 0
        )
        prob = grown_ref[h, :near] * use_ref[h, 0:1]
        near_weights = prob.astype(BF16)
        near_scores = (prob * (gp_ref[h, :near] - use_ref[h, 1:2])).astype(BF16)
        weights = jnp.concatenate([near_weights, w_ref[h]], 0)
        grad_scores = jnp.concatenate([near_scores, u_ref[h]], 0)
        attn_ref[:, cols] = tn(weights, v).astype(BF16)
        gq_ref[:, cols] = (tn(grad_scores, k) * SCALE).astype(BF16)
        gk = nn(near_scores, q_ref[:, cols]) * SCALE
        gv = nn(near_weights, ga_ref[:, cols])
        gk_ref[:, cols] = gk[:tokens]
        gv_ref[:, cols] = gv[:tokens]
        g4_ref[:rows, cols] = gk[tokens:].astype(BF16)
        g4_ref[rows:, cols] = gv[tokens:].astype(BF16)


def attention_local(q, *operands):
    tokens, width = q.shape
    bf = jax.ShapeDtypeStruct((tokens, width), BF16)
    f32 = jax.ShapeDtypeStruct((tokens, width), F32)
    return pl.pallas_call(
        local_kernel,
        in_specs=[VMEM_BLOCK] * (1 + len(operands)),
        out_specs=[VMEM_BLOCK] * 5,
        out_shape=[bf, bf, f32, f32, jax.ShapeDtypeStruct((2 * tokens // STEP, width), BF16)],
        compiler_params=params(),
        cost_estimate=pl.CostEstimate(
            flops=12 * tokens * tokens * width, bytes_accessed=16 * tokens * width, transcendentals=0
        ),
        name="attention_local",
    )(q, *operands)


def lends_own(index):
    return index % 4 != 3, index % 4 < 2


def returns_own(index, first):
    own1, own2 = lends_own(index)
    rest = jnp.logical_not(first)
    return (first & own2) | (rest & (index % 2 == 0)), first & own1, rest & own2


def returns_lent(index, first):
    own1, own2 = lends_own(index)
    rest = jnp.logical_not(first)
    return first & jnp.logical_not(own2), rest | jnp.logical_not(own1), first | jnp.logical_not(own2)


def choose_kernel(me_ref, core_ref, picked_ref, far4_ref, after, two_ref, three_ref):
    first = core_ref[0] == 0
    picked, far4 = picked_ref[...], far4_ref[...]
    lent = jnp.where(lends_own(me_ref[0])[1], picked, far4)
    two_ref[...] = jnp.where(first, far4, lent)
    three_ref[...] = jnp.where(first, lent, far4)


def include(total, block, use):
    block = block.astype(F32)
    return total + jnp.where(use, block, jnp.zeros_like(block))


def collect_kernel(me_ref, core_ref, own_ref, one_ref, two_ref, three_ref, out_ref):
    total = own_ref[...].astype(F32)
    uses = returns_lent(me_ref[0], core_ref[0] == 0)
    for ref, use in zip((one_ref, two_ref, three_ref), uses):
        total = include(total, ref[...], use)
    out_ref[...] = total.astype(BF16)


def small(kernel, name, count, me, core, *blocks):
    shape = jax.ShapeDtypeStruct(blocks[0].shape, BF16)
    out = pl.pallas_call(
        kernel,
        in_specs=[SMEM_BLOCK] * 2 + [VMEM_BLOCK] * len(blocks),
        out_specs=[VMEM_BLOCK] * count,
        out_shape=[shape] * count,
        compiler_params=params(8),
        cost_estimate=pl.CostEstimate(
            flops=blocks[0].size, bytes_accessed=2 * blocks[0].size, transcendentals=0
        ),
        name=name,
    )(me, core, *blocks)
    return out if count > 1 else out[0]


def settle_kernel(me_ref, core_ref, gk_ref, gv_ref, last_ref, one_ref, two_ref, three_ref, *rest):
    tokens = gk_ref.shape[0]
    rows = tokens // STEP
    back = [last_ref[...]]
    for ref, own in zip((one_ref, two_ref, three_ref), returns_own(me_ref[0], core_ref[0] == 0)):
        block = ref[...]
        back.append(jnp.where(own, block, jnp.zeros_like(block)))
    at = lax.broadcasted_iota(jnp.int32, (tokens, rows), 0)
    spot = (at == lax.broadcasted_iota(jnp.int32, (tokens, rows), 1) * STEP).astype(BF16)
    spot = jnp.concatenate([spot] * len(back), 1)
    out_hbms, (ready, sems) = rest[:2], rest[2:]
    half = gk_ref.shape[1] // 2
    sent = []
    for i, (near_ref, out_hbm) in enumerate(zip((gk_ref, gv_ref), out_hbms)):
        for c in (0, 1):
            cols = slice(c * half, (c + 1) * half)
            extra = nn(spot, jnp.concatenate([b[i * rows : (i + 1) * rows, cols] for b in back], 0))
            ready[i, :, cols] = (near_ref[:, cols] + extra).astype(BF16)
            copy = pltpu.make_async_copy(ready.at[i, :, cols], out_hbm.at[:, cols], sems.at[2 * i + c])
            copy.start()
            sent.append(copy)
    for copy in sent:
        copy.wait()


def settle(me, core, gk, gv, last, one, two, three):
    out = jax.ShapeDtypeStruct(gk.shape, BF16)
    return pl.pallas_call(
        settle_kernel,
        in_specs=[SMEM_BLOCK] * 2 + [VMEM_BLOCK] * 6,
        out_specs=[HBM_BLOCK] * 2,
        out_shape=[out, out],
        scratch_shapes=[pltpu.VMEM((2,) + gk.shape, BF16), pltpu.SemaphoreType.DMA((4,))],
        compiler_params=params(),
        name="settle",
    )(me, core, gk, gv, last, one, two, three)


def add(*blocks):
    total = blocks[0].astype(F32)
    for block in blocks[1:]:
        total = total + block.astype(F32)
    return total.astype(BF16)


def per_device(queries, keys, values, out_weight, cotangent, bounds):
    n = lax.axis_size("ctx")
    levels = n.bit_length() - 1
    me = lax.axis_index("ctx").astype(jnp.int32).reshape(1)
    core = lax.axis_index("head").astype(jnp.int32).reshape(1)

    other_cot = swap(cotangent)
    picked = pick(keys, values)
    far4 = lax.ppermute(picked, "ctx", hop(4, n))
    far1 = lax.ppermute(picked, "ctx", hop(1, n))
    ga, done = grad_attn(core, cotangent, other_cot, out_weight)

    hops, twos = hop(4, n), pairs(n)
    two, three = small(choose_kernel, "choose", 2, me, core, picked, far4, done)
    two = mixed(two, (hops, twos))
    three = mixed(three, (twos, hops))
    arrived = [two, three]
    first = lax.axis_index("head") == 0 if levels > 4 else None
    farther = jnp.where(first, two, three) if levels > 4 else None
    for i in range(4, levels):
        farther = lax.ppermute(farther, "ctx", hop(2 ** (i - 1), n))
        arrived.append(farther)

    grown, grad_prob, stats, bias = attention_near(
        me, bounds, queries, keys, values, ga, far4, far1, levels
    )
    weights, grad_scores, use, far, passes, two, three, four, *more = attention_far(
        me, core, queries, ga, grown, grad_prob, stats, bias, arrived
    )
    for i in reversed(range(len(more))):
        back = lax.ppermute(more[i], "ctx", hop(-(2 ** (i + 3)), n))
        if i > 0:
            more[i - 1] = add(more[i - 1], back)
        else:
            three = jnp.where(first, three, add(three, back))
            four = jnp.where(first, add(four, back), four)
    hops, ones, twos, nexts = hop(-4, n), turned(steps(n)), turned(twos), neighbours(n)
    one = mixed(two, (twos, nexts))
    two = mixed(three, (ones, hops))
    three = mixed((four.astype(F32) + one.astype(F32) * passes).astype(BF16), (hops, twos))
    attn, gq, gk, gv, g4 = attention_local(
        queries, keys, values, ga, far4, far1, far, grown, grad_prob, use, weights, grad_scores
    )
    back = (one, two, three)
    g4 = small(collect_kernel, "collect", 1, me, core, g4, *back)
    last = lax.ppermute(g4, "ctx", hop(-4, n))
    other_attn = swap(attn)
    output = project(core, attn, other_attn, out_weight)
    gk, gv = settle(me, core, gk, gv, last, *back)
    return output, gq, gk, gv


def solution(mesh):
    shared = P("ctx", "head")
    return jax.shard_map(
        per_device,
        mesh=mesh,
        in_specs=(shared, shared, shared, P(), shared, P()),
        out_specs=(shared,) * 4,
        check_vma=False,
    )
```

```python
import functools
import math

import jax
import jax.numpy as jnp
from jax import lax
from jax.experimental import pallas as pl
from jax.experimental.pallas import tpu as pltpu
from jax.sharding import PartitionSpec as P

DH = 128
STEP = 4
BF16 = jnp.bfloat16
F32 = jnp.float32
HBM_BLOCK = pl.BlockSpec(memory_space=pltpu.HBM)
VMEM_BLOCK = pl.BlockSpec(memory_space=pltpu.VMEM)
SMEM_BLOCK = pl.BlockSpec(memory_space=pltpu.SMEM)


def hop(distance, n):
    return [(i, i + distance) for i in range(n) if 0 <= i + distance < n]


def pairs(n):
    return [(i, i ^ 2) for i in range(n)]


def steps(n):
    return [(i, i - 3 if i % 4 == 3 else i + 1) for i in range(n)]


def neighbours(n):
    return [(i, i ^ 1) for i in range(n)]


def turned(route):
    return [(b, a) for a, b in route]


def mixed(block, route_of_core):
    cores = len(route_of_core)
    route = [(a * cores + c, b * cores + c) for c, r in enumerate(route_of_core) for a, b in r]
    return lax.ppermute(block, ("ctx", "head"), route)


def swap(block):
    return lax.ppermute(block, "head", [(0, 1), (1, 0)])


def nt(a, b):
    return lax.dot_general(a, b, (((1,), (1,)), ((), ())), preferred_element_type=F32)


def tn(a, b):
    return lax.dot_general(a, b, (((0,), (0,)), ((), ())), preferred_element_type=F32)


def nn(a, b):
    return jnp.dot(a, b, preferred_element_type=F32)


def params(mib=24):
    return pltpu.CompilerParams(vmem_limit_bytes=int(mib * 1024 * 1024))


def pick_kernel(k_hbm, v_hbm, out_ref, held, sems):
    tokens = k_hbm.shape[0]
    rows = tokens // STEP
    copies = [pltpu.make_async_copy(x, held.at[i], sems.at[i]) for i, x in enumerate((k_hbm, v_hbm))]
    for copy in copies:
        copy.start()
    at = lax.broadcasted_iota(jnp.int32, (rows, tokens), 0) * STEP
    choose = (at == lax.broadcasted_iota(jnp.int32, (rows, tokens), 1)).astype(BF16)
    for i, copy in enumerate(copies):
        copy.wait()
        out_ref[i * rows : (i + 1) * rows] = nn(choose, held[i]).astype(BF16)


def pick(keys, values):
    tokens, width = keys.shape
    return pl.pallas_call(
        pick_kernel,
        in_specs=[HBM_BLOCK, HBM_BLOCK],
        out_shape=jax.ShapeDtypeStruct((2 * tokens // STEP, width), BF16),
        scratch_shapes=[pltpu.VMEM((2, tokens, width), BF16), pltpu.SemaphoreType.DMA((2,))],
        compiler_params=params(63.5),
        name="pick",
    )(keys, values)


def grad_attn_kernel(part, core_ref, own_ref, other_hbm, w_hbm, after, out_ref, done_ref, got, held, got_sem, sems):
    pieces, tile, _ = held.shape
    core = core_ref[0]
    fetch = pltpu.make_async_copy(other_hbm, got, got_sem)
    fetch.start()
    copies = []
    for i in range(pieces):
        rows = w_hbm.at[pl.ds(((core * 2 + part) * pieces + i) * tile, tile), :]
        copies.append(pltpu.make_async_copy(rows, held.at[i], sems.at[i]))
        copies[i].start()
    done_ref[...] = jnp.zeros_like(done_ref)
    fetch.wait()
    own, other = own_ref[...], got[...]
    cot = jnp.concatenate([jnp.where(core == 0, own, other), jnp.where(core == 0, other, own)], 1)
    for i in range(pieces):
        copies[i].wait()
        out_ref[:, i * tile : (i + 1) * tile] = nt(cot, held[i]).astype(BF16)


def grad_attn(part, core, own, other, weight, after):
    tokens, width = own.shape
    pieces = 2
    return pl.pallas_call(
        functools.partial(grad_attn_kernel, part),
        in_specs=[SMEM_BLOCK, VMEM_BLOCK, HBM_BLOCK, HBM_BLOCK, pl.BlockSpec(memory_space=pl.ANY)],
        out_specs=[VMEM_BLOCK] * 2,
        out_shape=[
            jax.ShapeDtypeStruct((tokens, width // 2), BF16),
            jax.ShapeDtypeStruct((8, DH), F32),
        ],
        scratch_shapes=[
            pltpu.VMEM((tokens, width), BF16),
            pltpu.VMEM((pieces, width // (2 * pieces), weight.shape[1]), BF16),
            pltpu.SemaphoreType.DMA,
            pltpu.SemaphoreType.DMA((pieces,)),
        ],
        compiler_params=params(52),
        cost_estimate=pl.CostEstimate(
            flops=2 * tokens * width * width, bytes_accessed=3 * width * width, transcendentals=0
        ),
        name=f"grad_attn{part}",
    )(core, own, other, weight, after)


def of_head(halves, h):
    count = halves[0].shape[1] // DH
    return halves[h // count][:, (h % count) * DH : (h % count + 1) * DH]


def project_kernel(core_ref, own_ref, other_ref, w_hbm, out_ref, held, sems):
    pieces, tile, width = held.shape
    core = core_ref[0]
    columns = pl.ds(pl.multiple_of(core * width, width), width)
    copies = []
    for i in range(pieces):
        part = w_hbm.at[pl.ds(i * tile, tile), columns]
        copies.append(pltpu.make_async_copy(part, held.at[i], sems.at[i]))
        copies[i].start()
    own, other = own_ref[...], other_ref[...]
    whole = jnp.concatenate([jnp.where(core == 0, own, other), jnp.where(core == 0, other, own)], 1)
    total = None
    for i in range(pieces):
        copies[i].wait()
        term = nn(whole[:, i * tile : (i + 1) * tile], held[i])
        total = term if total is None else total + term
    out_ref[...] = total.astype(BF16)


def project(core, own, other, weight):
    tokens, width = own.shape
    pieces = 4
    return pl.pallas_call(
        project_kernel,
        in_specs=[SMEM_BLOCK, VMEM_BLOCK, VMEM_BLOCK, HBM_BLOCK],
        out_specs=VMEM_BLOCK,
        out_shape=jax.ShapeDtypeStruct((tokens, width), BF16),
        scratch_shapes=[
            pltpu.VMEM((pieces, weight.shape[0] // pieces, width), BF16),
            pltpu.SemaphoreType.DMA((pieces,)),
        ],
        compiler_params=params(52),
        cost_estimate=pl.CostEstimate(
            flops=4 * tokens * width * width, bytes_accessed=6 * width * width, transcendentals=0
        ),
        name="project",
    )(core, own, other, weight)


def documents(positions, bounds_ref):
    count = jnp.zeros(positions.shape, jnp.int32)
    for i in range(bounds_ref.shape[0]):
        count = count + (bounds_ref[i] <= positions).astype(jnp.int32)
    return count


def mask_bias(me, bounds_ref, tokens, order):
    rows = tokens // STEP
    own = lax.broadcasted_iota(jnp.int32, (1, tokens), 1) + me * tokens
    parts = [lax.broadcasted_iota(jnp.int32, (tokens, 1), 0) + me * tokens]
    for distance in order:
        at = lax.broadcasted_iota(jnp.int32, (rows, 1), 0) * STEP
        parts.append(at + (me - distance) * tokens)
    keys = jnp.concatenate(parts, 0)
    key_doc = jnp.where(keys >= 0, documents(keys, bounds_ref), -1)
    ok = (documents(own, bounds_ref) == key_doc) & (keys <= own)
    return jnp.where(ok, 0.0, -jnp.inf).astype(F32)


def sort_arrived(first, two, three, *more):
    return [jnp.where(first, three, two), jnp.where(first, two, three), *more]


def distances(levels):
    return [4, 1, 2] + [2**i for i in range(3, levels)]


SCALE = 1.0 / math.sqrt(DH)
POWER = SCALE * math.log2(math.e)


def near_kernel(
    levels, me_ref, bounds_ref, q_ref, k_ref, v_ref, low_ga_ref, high_ga_ref, far4_ref, far1_ref,
    grown_ref, gp_ref, stat_ref, bias_ref,
):
    tokens = q_ref.shape[0]
    rows = tokens // STEP
    near = tokens + 2 * rows
    bias_ref[...] = mask_bias(me_ref[0], bounds_ref, tokens, distances(levels))
    for h in range(q_ref.shape[1] // DH):
        cols = slice(h * DH, (h + 1) * DH)
        k = jnp.concatenate([k_ref[:, cols], far4_ref[:rows, cols], far1_ref[:rows, cols]], 0)
        v = jnp.concatenate([v_ref[:, cols], far4_ref[rows:, cols], far1_ref[rows:, cols]], 0)
        scores = nt(k, q_ref[:, cols]) + bias_ref[:near]
        top = jnp.max(scores, axis=0, keepdims=True)
        grown = jnp.exp2((scores - top) * POWER)
        grad_prob = nt(v, of_head((low_ga_ref, high_ga_ref), h))
        grown_ref[h] = grown
        gp_ref[h] = grad_prob
        stat_ref[h, 0:1] = top
        stat_ref[h, 1:2] = jnp.sum(grown, axis=0, keepdims=True)
        stat_ref[h, 2:3] = jnp.sum(grown * grad_prob, axis=0, keepdims=True)


def attention_near(me, bounds, q, k, v, ga, far4, far1, levels):
    tokens, width = q.shape
    heads, rows = width // DH, tokens // STEP
    near, count = tokens + 2 * rows, tokens + levels * rows
    early = jax.ShapeDtypeStruct((heads, near, tokens), F32)
    return pl.pallas_call(
        functools.partial(near_kernel, levels),
        in_specs=[SMEM_BLOCK, SMEM_BLOCK] + [VMEM_BLOCK] * 7,
        out_specs=[VMEM_BLOCK] * 4,
        out_shape=[
            early,
            early,
            jax.ShapeDtypeStruct((heads, 8, tokens), F32),
            jax.ShapeDtypeStruct((count, tokens), F32),
        ],
        compiler_params=params(),
        cost_estimate=pl.CostEstimate(
            flops=4 * tokens * near * width, bytes_accessed=16 * tokens * width, transcendentals=0
        ),
        name="attention_near",
    )(me, bounds, q, k, v, *ga, far4, far1)


def far_kernel(levels, *refs):
    me_ref, core_ref, q_ref, low_ga_ref, high_ga_ref, grown_ref, gp_ref, stat_ref, bias_ref = refs[:9]
    refs = refs[1:]
    arrived_refs = refs[8 : 6 + levels]
    w_ref, u_ref, use_ref, far_ref, pass_ref = refs[6 + levels : 11 + levels]
    gfar_refs = refs[11 + levels :]
    tokens = q_ref.shape[0]
    rows = tokens // STEP
    near = tokens + 2 * rows
    first = core_ref[0] == 0
    passes = (core_ref[0] * (me_ref[0] % 2)).astype(F32)
    pass_ref[...] = jnp.full(pass_ref.shape, passes, F32)
    for h in range(q_ref.shape[1] // DH):
        cols = slice(h * DH, (h + 1) * DH)
        q, ga = q_ref[:, cols], of_head((low_ga_ref, high_ga_ref), h)
        far = sort_arrived(first, *[r[:, cols] for r in arrived_refs])
        k = jnp.concatenate([f[:rows] for f in far], 0)
        v = jnp.concatenate([f[rows:] for f in far], 0)
        far_ref[0, :, cols] = k
        far_ref[1, :, cols] = v
        scores = nt(k, q) + bias_ref[near:]
        early_top = stat_ref[h, 0:1]
        top = jnp.maximum(early_top, jnp.max(scores, axis=0, keepdims=True))
        shrink = jnp.exp2((early_top - top) * POWER)
        grown = jnp.exp2((scores - top) * POWER)
        grad_prob = nt(v, ga)
        total = stat_ref[h, 1:2] * shrink + jnp.sum(grown, axis=0, keepdims=True)
        weighted = stat_ref[h, 2:3] * shrink + jnp.sum(grown * grad_prob, axis=0, keepdims=True)
        part = 1.0 / total
        delta = weighted * part
        early_part = shrink * part
        use_ref[h, 0:1] = early_part
        use_ref[h, 1:2] = delta
        prob = jnp.concatenate([grown_ref[h, tokens + rows :] * early_part, grown * part], 0)
        grad_prob = jnp.concatenate([gp_ref[h, tokens + rows :], grad_prob], 0)
        weights = prob.astype(BF16)
        grad_scores = (prob * (grad_prob - delta)).astype(BF16)
        w_ref[h] = weights
        u_ref[h] = grad_scores
        gk = (nn(grad_scores, q) * SCALE).astype(BF16)
        gv = nn(weights, ga).astype(BF16)
        g1, g2, g8, *more = [
            jnp.concatenate([g[i * rows : (i + 1) * rows] for g in (gk, gv)], 0) for i in range(levels - 1)
        ]
        out = [jnp.where(first, g2, g1), jnp.where(first, g1, g8), jnp.where(first, g8, g2)]
        for ref, block in zip(gfar_refs, out + more):
            ref[:, cols] = block


def attention_far(me, core, q, ga, grown, grad_prob, stats, bias, arrived):
    tokens, width = q.shape
    levels = 2 + len(arrived)
    heads, rows = width // DH, tokens // STEP
    prob = jax.ShapeDtypeStruct((heads, (levels - 1) * rows, tokens), BF16)
    return pl.pallas_call(
        functools.partial(far_kernel, levels),
        in_specs=[SMEM_BLOCK] * 2 + [VMEM_BLOCK] * (7 + len(arrived)),
        out_specs=[VMEM_BLOCK] * (4 + levels),
        out_shape=[
            prob,
            prob,
            jax.ShapeDtypeStruct(stats.shape, F32),
            jax.ShapeDtypeStruct((2, (levels - 2) * rows, width), BF16),
            jax.ShapeDtypeStruct((1, width), F32),
        ]
        + [jax.ShapeDtypeStruct((2 * rows, width), BF16)] * (levels - 1),
        compiler_params=params(),
        cost_estimate=pl.CostEstimate(
            flops=8 * tokens * levels * rows * width, bytes_accessed=16 * tokens * width, transcendentals=0
        ),
        name="attention_far",
    )(me, core, q, *ga, grown, grad_prob, stats, bias, *arrived)


def local_kernel(
    q_ref, k_ref, v_ref, low_ga_ref, high_ga_ref, far4_ref, far1_ref, far_ref, grown_ref, gp_ref, use_ref, w_ref, u_ref,
    attn_ref, gq_ref, gk_ref, gv_ref, g4_ref,
):
    tokens = q_ref.shape[0]
    rows = tokens // STEP
    near = tokens + rows
    for h in range(q_ref.shape[1] // DH):
        cols = slice(h * DH, (h + 1) * DH)
        k = jnp.concatenate(
            [k_ref[:, cols], far4_ref[:rows, cols], far1_ref[:rows, cols], far_ref[0, :, cols]], 0
        )
        v = jnp.concatenate(
            [v_ref[:, cols], far4_ref[rows:, cols], far1_ref[rows:, cols], far_ref[1, :, cols]], 0
        )
        prob = grown_ref[h, :near] * use_ref[h, 0:1]
        near_weights = prob.astype(BF16)
        near_scores = (prob * (gp_ref[h, :near] - use_ref[h, 1:2])).astype(BF16)
        weights = jnp.concatenate([near_weights, w_ref[h]], 0)
        grad_scores = jnp.concatenate([near_scores, u_ref[h]], 0)
        attn_ref[:, cols] = tn(weights, v).astype(BF16)
        gq_ref[:, cols] = (tn(grad_scores, k) * SCALE).astype(BF16)
        gk = nn(near_scores, q_ref[:, cols]) * SCALE
        gv = nn(near_weights, of_head((low_ga_ref, high_ga_ref), h))
        gk_ref[:, cols] = gk[:tokens]
        gv_ref[:, cols] = gv[:tokens]
        g4_ref[:rows, cols] = gk[tokens:].astype(BF16)
        g4_ref[rows:, cols] = gv[tokens:].astype(BF16)


def attention_local(q, *operands):
    tokens, width = q.shape
    bf = jax.ShapeDtypeStruct((tokens, width), BF16)
    f32 = jax.ShapeDtypeStruct((tokens, width), F32)
    return pl.pallas_call(
        local_kernel,
        in_specs=[VMEM_BLOCK] * (1 + len(operands)),
        out_specs=[VMEM_BLOCK] * 5,
        out_shape=[bf, bf, f32, f32, jax.ShapeDtypeStruct((2 * tokens // STEP, width), BF16)],
        compiler_params=params(),
        cost_estimate=pl.CostEstimate(
            flops=12 * tokens * tokens * width, bytes_accessed=16 * tokens * width, transcendentals=0
        ),
        name="attention_local",
    )(q, *operands)


def lends_own(index):
    return index % 4 != 3, index % 4 < 2


def returns_own(index, first):
    own1, own2 = lends_own(index)
    rest = jnp.logical_not(first)
    return (first & own2) | (rest & (index % 2 == 0)), first & own1, rest & own2


def returns_lent(index, first):
    own1, own2 = lends_own(index)
    rest = jnp.logical_not(first)
    return first & jnp.logical_not(own2), rest | jnp.logical_not(own1), first | jnp.logical_not(own2)


def choose_kernel(me_ref, core_ref, picked_ref, far4_ref, after, two_ref, three_ref):
    first = core_ref[0] == 0
    picked, far4 = picked_ref[...], far4_ref[...]
    lent = jnp.where(lends_own(me_ref[0])[1], picked, far4)
    two_ref[...] = jnp.where(first, far4, lent)
    three_ref[...] = jnp.where(first, lent, far4)


def include(total, block, use):
    block = block.astype(F32)
    return total + jnp.where(use, block, jnp.zeros_like(block))


def collect_kernel(me_ref, core_ref, own_ref, one_ref, two_ref, three_ref, out_ref):
    total = own_ref[...].astype(F32)
    uses = returns_lent(me_ref[0], core_ref[0] == 0)
    for ref, use in zip((one_ref, two_ref, three_ref), uses):
        total = include(total, ref[...], use)
    out_ref[...] = total.astype(BF16)


def small(kernel, name, count, me, core, *blocks):
    shape = jax.ShapeDtypeStruct(blocks[0].shape, BF16)
    out = pl.pallas_call(
        kernel,
        in_specs=[SMEM_BLOCK] * 2 + [VMEM_BLOCK] * len(blocks),
        out_specs=[VMEM_BLOCK] * count,
        out_shape=[shape] * count,
        compiler_params=params(8),
        cost_estimate=pl.CostEstimate(
            flops=blocks[0].size, bytes_accessed=2 * blocks[0].size, transcendentals=0
        ),
        name=name,
    )(me, core, *blocks)
    return out if count > 1 else out[0]


def settle_kernel(me_ref, core_ref, gk_ref, gv_ref, last_ref, one_ref, two_ref, three_ref, *rest):
    tokens = gk_ref.shape[0]
    rows = tokens // STEP
    back = [last_ref[...]]
    for ref, own in zip((one_ref, two_ref, three_ref), returns_own(me_ref[0], core_ref[0] == 0)):
        block = ref[...]
        back.append(jnp.where(own, block, jnp.zeros_like(block)))
    at = lax.broadcasted_iota(jnp.int32, (tokens, rows), 0)
    spot = (at == lax.broadcasted_iota(jnp.int32, (tokens, rows), 1) * STEP).astype(BF16)
    spot = jnp.concatenate([spot] * len(back), 1)
    out_hbms, (ready, sems) = rest[:2], rest[2:]
    half = gk_ref.shape[1] // 2
    sent = []
    for i, (near_ref, out_hbm) in enumerate(zip((gk_ref, gv_ref), out_hbms)):
        for c in (0, 1):
            cols = slice(c * half, (c + 1) * half)
            extra = nn(spot, jnp.concatenate([b[i * rows : (i + 1) * rows, cols] for b in back], 0))
            ready[i, :, cols] = (near_ref[:, cols] + extra).astype(BF16)
            copy = pltpu.make_async_copy(ready.at[i, :, cols], out_hbm.at[:, cols], sems.at[2 * i + c])
            copy.start()
            sent.append(copy)
    for copy in sent:
        copy.wait()


def settle(me, core, gk, gv, last, one, two, three):
    out = jax.ShapeDtypeStruct(gk.shape, BF16)
    return pl.pallas_call(
        settle_kernel,
        in_specs=[SMEM_BLOCK] * 2 + [VMEM_BLOCK] * 6,
        out_specs=[HBM_BLOCK] * 2,
        out_shape=[out, out],
        scratch_shapes=[pltpu.VMEM((2,) + gk.shape, BF16), pltpu.SemaphoreType.DMA((4,))],
        compiler_params=params(),
        name="settle",
    )(me, core, gk, gv, last, one, two, three)


def add(*blocks):
    total = blocks[0].astype(F32)
    for block in blocks[1:]:
        total = total + block.astype(F32)
    return total.astype(BF16)


def per_device(queries, keys, values, out_weight, cotangent, bounds):
    n = lax.axis_size("ctx")
    levels = n.bit_length() - 1
    me = lax.axis_index("ctx").astype(jnp.int32).reshape(1)
    core = lax.axis_index("head").astype(jnp.int32).reshape(1)

    other_cot = swap(cotangent)
    picked = pick(keys, values)
    far4 = lax.ppermute(picked, "ctx", hop(4, n))
    far1 = lax.ppermute(picked, "ctx", hop(1, n))
    low_ga, done = grad_attn(0, core, cotangent, other_cot, out_weight, me)

    hops, twos = hop(4, n), pairs(n)
    two, three = small(choose_kernel, "choose", 2, me, core, picked, far4, done)
    ga = low_ga, grad_attn(1, core, cotangent, other_cot, out_weight, two)[0]
    two = mixed(two, (hops, twos))
    three = mixed(three, (twos, hops))
    arrived = [two, three]
    first = lax.axis_index("head") == 0 if levels > 4 else None
    farther = jnp.where(first, two, three) if levels > 4 else None
    for i in range(4, levels):
        farther = lax.ppermute(farther, "ctx", hop(2 ** (i - 1), n))
        arrived.append(farther)

    grown, grad_prob, stats, bias = attention_near(
        me, bounds, queries, keys, values, ga, far4, far1, levels
    )
    weights, grad_scores, use, far, passes, two, three, four, *more = attention_far(
        me, core, queries, ga, grown, grad_prob, stats, bias, arrived
    )
    for i in reversed(range(len(more))):
        back = lax.ppermute(more[i], "ctx", hop(-(2 ** (i + 3)), n))
        if i > 0:
            more[i - 1] = add(more[i - 1], back)
        else:
            three = jnp.where(first, three, add(three, back))
            four = jnp.where(first, add(four, back), four)
    hops, ones, twos, nexts = hop(-4, n), turned(steps(n)), turned(twos), neighbours(n)
    one = mixed(two, (twos, nexts))
    two = mixed(three, (ones, hops))
    three = mixed((four.astype(F32) + one.astype(F32) * passes).astype(BF16), (hops, twos))
    attn, gq, gk, gv, g4 = attention_local(
        queries, keys, values, *ga, far4, far1, far, grown, grad_prob, use, weights, grad_scores
    )
    back = (one, two, three)
    g4 = small(collect_kernel, "collect", 1, me, core, g4, *back)
    last = lax.ppermute(g4, "ctx", hop(-4, n))
    other_attn = swap(attn)
    output = project(core, attn, other_attn, out_weight)
    gk, gv = settle(me, core, gk, gv, last, *back)
    return output, gq, gk, gv


def solution(mesh):
    shared = P("ctx", "head")
    return jax.shard_map(
        per_device,
        mesh=mesh,
        in_specs=(shared, shared, shared, P(), shared, P()),
        out_specs=(shared,) * 4,
        check_vma=False,
    )
```

```python
import functools
import math

import jax
import jax.numpy as jnp
from jax import lax
from jax.experimental import pallas as pl
from jax.experimental.pallas import tpu as pltpu
from jax.sharding import PartitionSpec as P

DH = 128
STEP = 4
BF16 = jnp.bfloat16
F32 = jnp.float32
HBM_BLOCK = pl.BlockSpec(memory_space=pltpu.HBM)
VMEM_BLOCK = pl.BlockSpec(memory_space=pltpu.VMEM)
SMEM_BLOCK = pl.BlockSpec(memory_space=pltpu.SMEM)


def hop(distance, n):
    return [(i, i + distance) for i in range(n) if 0 <= i + distance < n]


def pairs(n):
    return [(i, i ^ 2) for i in range(n)]


def steps(n):
    return [(i, i - 3 if i % 4 == 3 else i + 1) for i in range(n)]


def neighbours(n):
    return [(i, i ^ 1) for i in range(n)]


def turned(route):
    return [(b, a) for a, b in route]


def mixed(block, route_of_core):
    cores = len(route_of_core)
    route = [(a * cores + c, b * cores + c) for c, r in enumerate(route_of_core) for a, b in r]
    return lax.ppermute(block, ("ctx", "head"), route)


def swap(block):
    return lax.ppermute(block, "head", [(0, 1), (1, 0)])


def nt(a, b):
    return lax.dot_general(a, b, (((1,), (1,)), ((), ())), preferred_element_type=F32)


def tn(a, b):
    return lax.dot_general(a, b, (((0,), (0,)), ((), ())), preferred_element_type=F32)


def nn(a, b):
    return jnp.dot(a, b, preferred_element_type=F32)


def params(mib=24):
    return pltpu.CompilerParams(vmem_limit_bytes=int(mib * 1024 * 1024))


def pick_kernel(k_hbm, v_hbm, out_ref, held, sems):
    tokens = k_hbm.shape[0]
    rows = tokens // STEP
    copies = [pltpu.make_async_copy(x, held.at[i], sems.at[i]) for i, x in enumerate((k_hbm, v_hbm))]
    for copy in copies:
        copy.start()
    at = lax.broadcasted_iota(jnp.int32, (rows, tokens), 0) * STEP
    choose = (at == lax.broadcasted_iota(jnp.int32, (rows, tokens), 1)).astype(BF16)
    for i, copy in enumerate(copies):
        copy.wait()
        out_ref[i * rows : (i + 1) * rows] = nn(choose, held[i]).astype(BF16)


def pick(keys, values):
    tokens, width = keys.shape
    return pl.pallas_call(
        pick_kernel,
        in_specs=[HBM_BLOCK, HBM_BLOCK],
        out_shape=jax.ShapeDtypeStruct((2 * tokens // STEP, width), BF16),
        scratch_shapes=[pltpu.VMEM((2, tokens, width), BF16), pltpu.SemaphoreType.DMA((2,))],
        compiler_params=params(63.5),
        name="pick",
    )(keys, values)


def grad_attn_kernel(part, core_ref, own_ref, other_hbm, w_hbm, after, out_ref, done_ref, got, held, got_sem, sems):
    pieces, tile, _ = held.shape
    core = core_ref[0]
    fetch = pltpu.make_async_copy(other_hbm, got, got_sem)
    fetch.start()
    copies = []
    for i in range(pieces):
        rows = w_hbm.at[pl.ds(((core * 2 + part) * pieces + i) * tile, tile), :]
        copies.append(pltpu.make_async_copy(rows, held.at[i], sems.at[i]))
        copies[i].start()
    done_ref[...] = jnp.zeros_like(done_ref)
    fetch.wait()
    own, other = own_ref[...], got[...]
    cot = jnp.concatenate([jnp.where(core == 0, own, other), jnp.where(core == 0, other, own)], 1)
    for i in range(pieces):
        copies[i].wait()
        out_ref[:, i * tile : (i + 1) * tile] = nt(cot, held[i]).astype(BF16)


def grad_attn(part, core, own, other, weight, after):
    tokens, width = own.shape
    pieces = 4
    return pl.pallas_call(
        functools.partial(grad_attn_kernel, part),
        in_specs=[SMEM_BLOCK, VMEM_BLOCK, HBM_BLOCK, HBM_BLOCK, pl.BlockSpec(memory_space=pl.ANY)],
        out_specs=[VMEM_BLOCK] * 2,
        out_shape=[
            jax.ShapeDtypeStruct((tokens, width // 2), BF16),
            jax.ShapeDtypeStruct((8, DH), F32),
        ],
        scratch_shapes=[
            pltpu.VMEM((tokens, width), BF16),
            pltpu.VMEM((pieces, width // (2 * pieces), weight.shape[1]), BF16),
            pltpu.SemaphoreType.DMA,
            pltpu.SemaphoreType.DMA((pieces,)),
        ],
        compiler_params=params(52),
        cost_estimate=pl.CostEstimate(
            flops=2 * tokens * width * width, bytes_accessed=3 * width * width, transcendentals=0
        ),
        name=f"grad_attn{part}",
    )(core, own, other, weight, after)


def of_head(halves, h):
    count = halves[0].shape[1] // DH
    return halves[h // count][:, (h % count) * DH : (h % count + 1) * DH]


def project_kernel(core_ref, own_ref, other_ref, w_hbm, out_ref, held, sems):
    pieces, tile, width = held.shape
    core = core_ref[0]
    columns = pl.ds(pl.multiple_of(core * width, width), width)
    copies = []
    for i in range(pieces):
        part = w_hbm.at[pl.ds(i * tile, tile), columns]
        copies.append(pltpu.make_async_copy(part, held.at[i], sems.at[i]))
        copies[i].start()
    own, other = own_ref[...], other_ref[...]
    whole = jnp.concatenate([jnp.where(core == 0, own, other), jnp.where(core == 0, other, own)], 1)
    total = None
    for i in range(pieces):
        copies[i].wait()
        term = nn(whole[:, i * tile : (i + 1) * tile], held[i])
        total = term if total is None else total + term
    out_ref[...] = total.astype(BF16)


def project(core, own, other, weight):
    tokens, width = own.shape
    pieces = 4
    return pl.pallas_call(
        project_kernel,
        in_specs=[SMEM_BLOCK, VMEM_BLOCK, VMEM_BLOCK, HBM_BLOCK],
        out_specs=VMEM_BLOCK,
        out_shape=jax.ShapeDtypeStruct((tokens, width), BF16),
        scratch_shapes=[
            pltpu.VMEM((pieces, weight.shape[0] // pieces, width), BF16),
            pltpu.SemaphoreType.DMA((pieces,)),
        ],
        compiler_params=params(52),
        cost_estimate=pl.CostEstimate(
            flops=4 * tokens * width * width, bytes_accessed=6 * width * width, transcendentals=0
        ),
        name="project",
    )(core, own, other, weight)


def documents(positions, bounds_ref):
    count = jnp.zeros(positions.shape, jnp.int32)
    for i in range(bounds_ref.shape[0]):
        count = count + (bounds_ref[i] <= positions).astype(jnp.int32)
    return count


def mask_bias(me, bounds_ref, tokens, order):
    rows = tokens // STEP
    own = lax.broadcasted_iota(jnp.int32, (1, tokens), 1) + me * tokens
    parts = [lax.broadcasted_iota(jnp.int32, (tokens, 1), 0) + me * tokens]
    for distance in order:
        at = lax.broadcasted_iota(jnp.int32, (rows, 1), 0) * STEP
        parts.append(at + (me - distance) * tokens)
    keys = jnp.concatenate(parts, 0)
    key_doc = jnp.where(keys >= 0, documents(keys, bounds_ref), -1)
    ok = (documents(own, bounds_ref) == key_doc) & (keys <= own)
    return jnp.where(ok, 0.0, -jnp.inf).astype(F32)


def sort_arrived(first, two, three, *more):
    return [jnp.where(first, three, two), jnp.where(first, two, three), *more]


def distances(levels):
    return [4, 1, 2] + [2**i for i in range(3, levels)]


SCALE = 1.0 / math.sqrt(DH)
POWER = SCALE * math.log2(math.e)


def near_kernel(
    levels, me_ref, bounds_ref, q_ref, k_ref, v_ref, low_ga_ref, high_ga_ref, far4_ref, far1_ref,
    grown_ref, gp_ref, stat_ref, bias_ref,
):
    tokens = q_ref.shape[0]
    rows = tokens // STEP
    near = tokens + 2 * rows
    bias_ref[...] = mask_bias(me_ref[0], bounds_ref, tokens, distances(levels))
    for h in range(q_ref.shape[1] // DH):
        cols = slice(h * DH, (h + 1) * DH)
        k = jnp.concatenate([k_ref[:, cols], far4_ref[:rows, cols], far1_ref[:rows, cols]], 0)
        v = jnp.concatenate([v_ref[:, cols], far4_ref[rows:, cols], far1_ref[rows:, cols]], 0)
        scores = nt(k, q_ref[:, cols]) + bias_ref[:near]
        top = jnp.max(scores, axis=0, keepdims=True)
        grown = jnp.exp2((scores - top) * POWER)
        grad_prob = nt(v, of_head((low_ga_ref, high_ga_ref), h))
        grown_ref[h] = grown
        gp_ref[h] = grad_prob
        stat_ref[h, 0:1] = top
        stat_ref[h, 1:2] = jnp.sum(grown, axis=0, keepdims=True)
        stat_ref[h, 2:3] = jnp.sum(grown * grad_prob, axis=0, keepdims=True)


def attention_near(me, bounds, q, k, v, ga, far4, far1, levels):
    tokens, width = q.shape
    heads, rows = width // DH, tokens // STEP
    near, count = tokens + 2 * rows, tokens + levels * rows
    early = jax.ShapeDtypeStruct((heads, near, tokens), F32)
    return pl.pallas_call(
        functools.partial(near_kernel, levels),
        in_specs=[SMEM_BLOCK, SMEM_BLOCK] + [VMEM_BLOCK] * 7,
        out_specs=[VMEM_BLOCK] * 4,
        out_shape=[
            early,
            early,
            jax.ShapeDtypeStruct((heads, 8, tokens), F32),
            jax.ShapeDtypeStruct((count, tokens), F32),
        ],
        compiler_params=params(),
        cost_estimate=pl.CostEstimate(
            flops=4 * tokens * near * width, bytes_accessed=16 * tokens * width, transcendentals=0
        ),
        name="attention_near",
    )(me, bounds, q, k, v, *ga, far4, far1)


def far_kernel(levels, *refs):
    me_ref, core_ref, q_ref, low_ga_ref, high_ga_ref, grown_ref, gp_ref, stat_ref, bias_ref = refs[:9]
    refs = refs[1:]
    arrived_refs = refs[8 : 6 + levels]
    w_ref, u_ref, use_ref, far_ref, pass_ref = refs[6 + levels : 11 + levels]
    gfar_refs = refs[11 + levels :]
    tokens = q_ref.shape[0]
    rows = tokens // STEP
    near = tokens + 2 * rows
    first = core_ref[0] == 0
    passes = (core_ref[0] * (me_ref[0] % 2)).astype(F32)
    pass_ref[...] = jnp.full(pass_ref.shape, passes, F32)
    for h in range(q_ref.shape[1] // DH):
        cols = slice(h * DH, (h + 1) * DH)
        q, ga = q_ref[:, cols], of_head((low_ga_ref, high_ga_ref), h)
        far = sort_arrived(first, *[r[:, cols] for r in arrived_refs])
        k = jnp.concatenate([f[:rows] for f in far], 0)
        v = jnp.concatenate([f[rows:] for f in far], 0)
        far_ref[0, :, cols] = k
        far_ref[1, :, cols] = v
        scores = nt(k, q) + bias_ref[near:]
        early_top = stat_ref[h, 0:1]
        top = jnp.maximum(early_top, jnp.max(scores, axis=0, keepdims=True))
        shrink = jnp.exp2((early_top - top) * POWER)
        grown = jnp.exp2((scores - top) * POWER)
        grad_prob = nt(v, ga)
        total = stat_ref[h, 1:2] * shrink + jnp.sum(grown, axis=0, keepdims=True)
        weighted = stat_ref[h, 2:3] * shrink + jnp.sum(grown * grad_prob, axis=0, keepdims=True)
        part = 1.0 / total
        delta = weighted * part
        early_part = shrink * part
        use_ref[h, 0:1] = early_part
        use_ref[h, 1:2] = delta
        prob = jnp.concatenate([grown_ref[h, tokens + rows :] * early_part, grown * part], 0)
        grad_prob = jnp.concatenate([gp_ref[h, tokens + rows :], grad_prob], 0)
        weights = prob.astype(BF16)
        grad_scores = (prob * (grad_prob - delta)).astype(BF16)
        w_ref[h] = weights
        u_ref[h] = grad_scores
        gk = (nn(grad_scores, q) * SCALE).astype(BF16)
        gv = nn(weights, ga).astype(BF16)
        g1, g2, g8, *more = [
            jnp.concatenate([g[i * rows : (i + 1) * rows] for g in (gk, gv)], 0) for i in range(levels - 1)
        ]
        out = [jnp.where(first, g2, g1), jnp.where(first, g1, g8), jnp.where(first, g8, g2)]
        for ref, block in zip(gfar_refs, out + more):
            ref[:, cols] = block


def attention_far(me, core, q, ga, grown, grad_prob, stats, bias, arrived):
    tokens, width = q.shape
    levels = 2 + len(arrived)
    heads, rows = width // DH, tokens // STEP
    prob = jax.ShapeDtypeStruct((heads, (levels - 1) * rows, tokens), BF16)
    return pl.pallas_call(
        functools.partial(far_kernel, levels),
        in_specs=[SMEM_BLOCK] * 2 + [VMEM_BLOCK] * (7 + len(arrived)),
        out_specs=[VMEM_BLOCK] * (4 + levels),
        out_shape=[
            prob,
            prob,
            jax.ShapeDtypeStruct(stats.shape, F32),
            jax.ShapeDtypeStruct((2, (levels - 2) * rows, width), BF16),
            jax.ShapeDtypeStruct((1, width), F32),
        ]
        + [jax.ShapeDtypeStruct((2 * rows, width), BF16)] * (levels - 1),
        compiler_params=params(),
        cost_estimate=pl.CostEstimate(
            flops=8 * tokens * levels * rows * width, bytes_accessed=16 * tokens * width, transcendentals=0
        ),
        name="attention_far",
    )(me, core, q, *ga, grown, grad_prob, stats, bias, *arrived)


def local_kernel(
    q_ref, k_ref, v_ref, low_ga_ref, high_ga_ref, far4_ref, far1_ref, far_ref, grown_ref, gp_ref, use_ref, w_ref, u_ref,
    attn_ref, gq_ref, gk_ref, gv_ref, g4_ref,
):
    tokens = q_ref.shape[0]
    rows = tokens // STEP
    near = tokens + rows
    for h in range(q_ref.shape[1] // DH):
        cols = slice(h * DH, (h + 1) * DH)
        k = jnp.concatenate(
            [k_ref[:, cols], far4_ref[:rows, cols], far1_ref[:rows, cols], far_ref[0, :, cols]], 0
        )
        v = jnp.concatenate(
            [v_ref[:, cols], far4_ref[rows:, cols], far1_ref[rows:, cols], far_ref[1, :, cols]], 0
        )
        prob = grown_ref[h, :near] * use_ref[h, 0:1]
        near_weights = prob.astype(BF16)
        near_scores = (prob * (gp_ref[h, :near] - use_ref[h, 1:2])).astype(BF16)
        weights = jnp.concatenate([near_weights, w_ref[h]], 0)
        grad_scores = jnp.concatenate([near_scores, u_ref[h]], 0)
        attn_ref[:, cols] = tn(weights, v).astype(BF16)
        gq_ref[:, cols] = (tn(grad_scores, k) * SCALE).astype(BF16)
        gk = nn(near_scores, q_ref[:, cols]) * SCALE
        gv = nn(near_weights, of_head((low_ga_ref, high_ga_ref), h))
        gk_ref[:, cols] = gk[:tokens]
        gv_ref[:, cols] = gv[:tokens]
        g4_ref[:rows, cols] = gk[tokens:].astype(BF16)
        g4_ref[rows:, cols] = gv[tokens:].astype(BF16)


def attention_local(q, *operands):
    tokens, width = q.shape
    bf = jax.ShapeDtypeStruct((tokens, width), BF16)
    f32 = jax.ShapeDtypeStruct((tokens, width), F32)
    return pl.pallas_call(
        local_kernel,
        in_specs=[VMEM_BLOCK] * (1 + len(operands)),
        out_specs=[VMEM_BLOCK] * 5,
        out_shape=[bf, bf, f32, f32, jax.ShapeDtypeStruct((2 * tokens // STEP, width), BF16)],
        compiler_params=params(),
        cost_estimate=pl.CostEstimate(
            flops=12 * tokens * tokens * width, bytes_accessed=16 * tokens * width, transcendentals=0
        ),
        name="attention_local",
    )(q, *operands)


def lends_own(index):
    return index % 4 != 3, index % 4 < 2


def returns_own(index, first):
    own1, own2 = lends_own(index)
    rest = jnp.logical_not(first)
    return (first & own2) | (rest & (index % 2 == 0)), first & own1, rest & own2


def returns_lent(index, first):
    own1, own2 = lends_own(index)
    rest = jnp.logical_not(first)
    return first & jnp.logical_not(own2), rest | jnp.logical_not(own1), first | jnp.logical_not(own2)


def choose_kernel(me_ref, core_ref, picked_ref, far4_ref, after, two_ref, three_ref):
    first = core_ref[0] == 0
    picked, far4 = picked_ref[...], far4_ref[...]
    lent = jnp.where(lends_own(me_ref[0])[1], picked, far4)
    two_ref[...] = jnp.where(first, far4, lent)
    three_ref[...] = jnp.where(first, lent, far4)


def include(total, block, use):
    block = block.astype(F32)
    return total + jnp.where(use, block, jnp.zeros_like(block))


def collect_kernel(me_ref, core_ref, own_ref, one_ref, two_ref, three_ref, out_ref):
    total = own_ref[...].astype(F32)
    uses = returns_lent(me_ref[0], core_ref[0] == 0)
    for ref, use in zip((one_ref, two_ref, three_ref), uses):
        total = include(total, ref[...], use)
    out_ref[...] = total.astype(BF16)


def small(kernel, name, count, me, core, *blocks):
    shape = jax.ShapeDtypeStruct(blocks[0].shape, BF16)
    out = pl.pallas_call(
        kernel,
        in_specs=[SMEM_BLOCK] * 2 + [VMEM_BLOCK] * len(blocks),
        out_specs=[VMEM_BLOCK] * count,
        out_shape=[shape] * count,
        compiler_params=params(8),
        cost_estimate=pl.CostEstimate(
            flops=blocks[0].size, bytes_accessed=2 * blocks[0].size, transcendentals=0
        ),
        name=name,
    )(me, core, *blocks)
    return out if count > 1 else out[0]


def settle_kernel(me_ref, core_ref, gk_ref, gv_ref, last_ref, one_ref, two_ref, three_ref, *rest):
    tokens = gk_ref.shape[0]
    rows = tokens // STEP
    back = [last_ref[...]]
    for ref, own in zip((one_ref, two_ref, three_ref), returns_own(me_ref[0], core_ref[0] == 0)):
        block = ref[...]
        back.append(jnp.where(own, block, jnp.zeros_like(block)))
    at = lax.broadcasted_iota(jnp.int32, (tokens, rows), 0)
    spot = (at == lax.broadcasted_iota(jnp.int32, (tokens, rows), 1) * STEP).astype(BF16)
    spot = jnp.concatenate([spot] * len(back), 1)
    out_hbms, (ready, sems) = rest[:2], rest[2:]
    half = gk_ref.shape[1] // 2
    sent = []
    for i, (near_ref, out_hbm) in enumerate(zip((gk_ref, gv_ref), out_hbms)):
        for c in (0, 1):
            cols = slice(c * half, (c + 1) * half)
            extra = nn(spot, jnp.concatenate([b[i * rows : (i + 1) * rows, cols] for b in back], 0))
            ready[i, :, cols] = (near_ref[:, cols] + extra).astype(BF16)
            copy = pltpu.make_async_copy(ready.at[i, :, cols], out_hbm.at[:, cols], sems.at[2 * i + c])
            copy.start()
            sent.append(copy)
    for copy in sent:
        copy.wait()


def settle(me, core, gk, gv, last, one, two, three):
    out = jax.ShapeDtypeStruct(gk.shape, BF16)
    return pl.pallas_call(
        settle_kernel,
        in_specs=[SMEM_BLOCK] * 2 + [VMEM_BLOCK] * 6,
        out_specs=[HBM_BLOCK] * 2,
        out_shape=[out, out],
        scratch_shapes=[pltpu.VMEM((2,) + gk.shape, BF16), pltpu.SemaphoreType.DMA((4,))],
        compiler_params=params(),
        name="settle",
    )(me, core, gk, gv, last, one, two, three)


def add(*blocks):
    total = blocks[0].astype(F32)
    for block in blocks[1:]:
        total = total + block.astype(F32)
    return total.astype(BF16)


def per_device(queries, keys, values, out_weight, cotangent, bounds):
    n = lax.axis_size("ctx")
    levels = n.bit_length() - 1
    me = lax.axis_index("ctx").astype(jnp.int32).reshape(1)
    core = lax.axis_index("head").astype(jnp.int32).reshape(1)

    other_cot = swap(cotangent)
    picked = pick(keys, values)
    far4 = lax.ppermute(picked, "ctx", hop(4, n))
    far1 = lax.ppermute(picked, "ctx", hop(1, n))
    low_ga, done = grad_attn(0, core, cotangent, other_cot, out_weight, me)

    hops, twos = hop(4, n), pairs(n)
    two, three = small(choose_kernel, "choose", 2, me, core, picked, far4, done)
    ga = low_ga, grad_attn(1, core, cotangent, other_cot, out_weight, two)[0]
    two = mixed(two, (hops, twos))
    three = mixed(three, (twos, hops))
    arrived = [two, three]
    first = lax.axis_index("head") == 0 if levels > 4 else None
    farther = jnp.where(first, two, three) if levels > 4 else None
    for i in range(4, levels):
        farther = lax.ppermute(farther, "ctx", hop(2 ** (i - 1), n))
        arrived.append(farther)

    grown, grad_prob, stats, bias = attention_near(
        me, bounds, queries, keys, values, ga, far4, far1, levels
    )
    weights, grad_scores, use, far, passes, two, three, four, *more = attention_far(
        me, core, queries, ga, grown, grad_prob, stats, bias, arrived
    )
    for i in reversed(range(len(more))):
        back = lax.ppermute(more[i], "ctx", hop(-(2 ** (i + 3)), n))
        if i > 0:
            more[i - 1] = add(more[i - 1], back)
        else:
            three = jnp.where(first, three, add(three, back))
            four = jnp.where(first, add(four, back), four)
    hops, ones, twos, nexts = hop(-4, n), turned(steps(n)), turned(twos), neighbours(n)
    one = mixed(two, (twos, nexts))
    two = mixed(three, (ones, hops))
    three = mixed((four.astype(F32) + one.astype(F32) * passes).astype(BF16), (hops, twos))
    attn, gq, gk, gv, g4 = attention_local(
        queries, keys, values, *ga, far4, far1, far, grown, grad_prob, use, weights, grad_scores
    )
    back = (one, two, three)
    g4 = small(collect_kernel, "collect", 1, me, core, g4, *back)
    last = lax.ppermute(g4, "ctx", hop(-4, n))
    other_attn = swap(attn)
    output = project(core, attn, other_attn, out_weight)
    gk, gv = settle(me, core, gk, gv, last, *back)
    return output, gq, gk, gv


def solution(mesh):
    shared = P("ctx", "head")
    return jax.shard_map(
        per_device,
        mesh=mesh,
        in_specs=(shared, shared, shared, P(), shared, P()),
        out_specs=(shared,) * 4,
        check_vma=False,
    )
```
